32 devices in a mesh: stream: 2 (over x), batch: 16 (over z, y, core).
Axes of the slice: x: 2, y: 2, z: 4, core: 2. Of those that a mesh axis runs over, the one named last changes fastest.
Arguments:
- features: bfloat16 [2, 32, 512, 768], P('stream', 'batch'), may hold values from -6 to 6
- cotangent: bfloat16 [2, 32, 512, 768], P('stream', 'batch'), may hold values from -6 to 6
- segment_ids: int32 [32, 512], P('batch'), may hold values from 0 to 3, never falling along the last dimension, each value on 1 to 256 neighbouring positions
- box_cells: int32 [2, 32, 2, 512], P('stream', 'batch'), may hold values from 0 to 15
- ln_gain: float32 [2, 2, 768], P('stream'), may hold values from 0.5 to 1.5
- ln_shift: float32 [2, 2, 768], P('stream'), may hold values from -1.8 to 1.8
- w_qkv: bfloat16 [2, 768, 2304], P('stream'), may hold values from -0.21875 to 0.21875
- attn_bias: float32 [2, 3, 768], P('stream'), may hold values from -1.8 to 1.8
- distance_table: float32 [2, 64, 12], P('stream'), may hold values from -4 to 4
- w_out: bfloat16 [2, 768, 768], P('stream'), may hold values from -1.25 to 1.25
- w_up: bfloat16 [2, 768, 3072], P('stream'), may hold values from -0.21875 to 0.21875
- up_bias: float32 [2, 3072], P('stream'), may hold values from -1.8 to 1.8
- w_down: bfloat16 [2, 3072, 768], P('stream'), may hold values from -0.109375 to 0.109375
- down_bias: float32 [2, 768], P('stream'), may hold values from -1.8 to 1.8
Outputs:
- output: bfloat16 [2, 32, 512, 768], P('stream', 'batch')
- input_grad: bfloat16 [2, 32, 512, 768], P('stream', 'batch')
- grad_ln_gain: float32 [2, 2, 768], P('stream')
- grad_ln_shift: float32 [2, 2, 768], P('stream')
- grad_w_qkv: float32 [2, 768, 2304], P('stream')
- grad_attn_bias: float32 [2, 3, 768], P('stream')
- grad_distance_table: float32 [2, 64, 12], P('stream')
- grad_w_out: float32 [2, 768, 768], P('stream')
- grad_w_up: float32 [2, 768, 3072], P('stream')
- grad_up_bias: float32 [2, 3072], P('stream')
- grad_w_down: float32 [2, 3072, 768], P('stream')
- grad_down_bias: float32 [2, 768], P('stream')
The draws below stay inside these ranges and needn't reach their ends.
Inputs may be any that keep to these rules, and one draw needn't show every extreme that they name: `segment_ids`: along each row the document numbers never fall; every document has 1 to 256 tokens and one has 256.
All inputs are finite; a program needn't handle non-finite values.
Results may differ from the reference program's by a relative error of at most 0.015.
Values may be sent and summed in bfloat16 or wider, within the bound.
A program may use at most 320 MiB of HBM per device.

```python
import math
import jax
import jax.numpy as jnp
import numpy as np
from jax import lax

D = 768
H = 12
HD = 64
FF = 3072
SEQ = 512
GRID = 8
BUCKETS = 64
ROWS = 32


def place_ends(values, rng, low, largest):
    shape = values.shape
    spot = [jax.random.randint(jax.random.fold_in(rng, axis), (), 0, shape[axis]) for axis in range(len(shape))]
    values = values.at[tuple(spot)].set(low)
    longest = shape.index(max(shape))
    spot[longest] = (spot[longest] + 1) % shape[longest]
    return values.at[tuple(spot)].set(largest)


def level_of(stream_key, shape, shards, low, top_value):
    def one(axis_at, shards_of):
        steps = jax.random.uniform(jax.random.fold_in(jax.random.fold_in(stream_key, 6), axis_at), (shards_of,), jnp.float32, low / len(shards), top_value / len(shards))
        return jnp.repeat(jnp.exp(steps), shape[axis_at] // shards_of).reshape((-1,) + (1,) * (len(shape) - axis_at - 1))

    gain = one(*shards[0])
    for cut in shards[1:]:
        gain = gain * one(*cut)
    return gain


def profile(amount, total, limit, skew):
    weights = [(1 << 20) // math.isqrt(grade ** skew) + 1 for grade in range(2, amount + 1)]
    spare, counts = total - limit - (amount - 1), [1] * (amount - 1)
    while spare > 0:
        candidates = [i for i in range(amount - 1) if counts[i] < limit]
        whole, remaining = sum([weights[i] for i in candidates]), spare
        for i in candidates:
            extra = min(limit - counts[i], max(1, remaining * weights[i] // whole), spare)
            counts[i] = counts[i] + extra
            spare = spare - extra
    return np.array([limit] + counts)


def ragged_sizes(stream_key, amount, total, limit, lean):
    if amount == 2:
        one = jax.random.randint(stream_key, (), max(1, total - limit), min(limit, total - 1) + 1)
        return jnp.stack([one, total - one])
    sizes = jnp.asarray(profile(amount, total, limit, lean), jnp.int32)
    twos = (amount - 1) // 2
    giver, receiver = sizes[1:1 + 2 * twos:2], sizes[2:2 + 2 * twos:2]
    margin = jnp.minimum(giver - 1, limit - receiver)
    shifted = jax.random.randint(jax.random.fold_in(stream_key, 1), (twos,), 0, 1 << 20) % (margin + 1)
    sizes = sizes.at[1:1 + 2 * twos:2].set(giver - shifted).at[2:2 + 2 * twos:2].set(receiver + shifted)
    return sizes[jax.random.permutation(jax.random.fold_in(stream_key, 2), amount)]


def normal_values(stream_key, extent, scale, most, pieces=(), dtype=jnp.bfloat16):
    level = level_of(stream_key, extent, pieces, -0.22, 0.18) if pieces else 1.0
    array = jax.random.normal(stream_key, extent, jnp.float32) * scale * level
    return jnp.minimum(jnp.maximum(array, -most), most).astype(dtype)


def setup_inputs(seed: int = 0) -> dict:
    splits = jax.random.split(jax.random.key(seed), 15)
    return {
        "features": normal_values(splits[0], (2, ROWS, SEQ, D), 1.0, 6.0, ((0, 2), (1, 16))),
        "cotangent": normal_values(splits[1], (2, ROWS, SEQ, D), 1.0, 6.0, ((0, 2), (1, 16))),
        "segment_ids": jax.vmap(lambda own: jnp.searchsorted(jnp.cumsum(ragged_sizes(own, 4, SEQ, SEQ // 2, 0)), jnp.arange(SEQ), side="right"))(jax.random.split(splits[2], ROWS)).reshape((ROWS, SEQ)).astype(jnp.int32),
        "box_cells": place_ends(jax.random.randint(splits[3], (2, ROWS, 2, SEQ), 0, 2 * GRID), jax.random.fold_in(splits[3], 1), 0, (2 * GRID) - 1).astype(jnp.int32),
        "ln_gain": jnp.clip(1.0 + 0.1 * jax.random.normal(splits[4], (2, 2, D), jnp.float32), 0.5, 1.5),
        "ln_shift": normal_values(splits[5], (2, 2, D), 0.3, 1.8, ((0, 2),), jnp.float32),
        "w_qkv": normal_values(splits[6], (2, D, 3 * D), D ** -0.5, 0.21875, ((0, 2),)),
        "attn_bias": normal_values(splits[7], (2, 3, D), 0.3, 1.8, ((0, 2),), jnp.float32),
        "distance_table": normal_values(splits[8], (2, BUCKETS, H), 1.0, 4.0, ((0, 2),), jnp.float32),
        "w_out": normal_values(splits[9], (2, D, D), (D // 32) ** -0.5, 1.25, ((0, 2),)),
        "w_up": normal_values(splits[10], (2, D, FF), D ** -0.5, 0.21875, ((0, 2),)),
        "up_bias": normal_values(splits[11], (2, FF), 0.3, 1.8, ((0, 2),), jnp.float32),
        "w_down": normal_values(splits[12], (2, FF, D), FF ** -0.5, 0.109375, ((0, 2),)),
        "down_bias": normal_values(splits[13], (2, D), 0.3, 1.8, ((0, 2),), jnp.float32),
    }


EPSILON = 1e-05
MASKED = -1000000000.0

@jax.custom_vjp
def low(v):
    return lax.optimization_barrier(v.astype(jnp.bfloat16)).astype(jnp.float32)

@jax.custom_vjp
def low_back(v):
    return v

def low_keep(v):
    return (low(v), None)

def low_pass(kept, grad):
    return (grad,)

def back_keep(v):
    return (v, None)

def back_low(kept, grad):
    return (low(grad),)
low.defvjp(low_keep, low_pass)
low_back.defvjp(back_keep, back_low)

def layer_norm(values, norm_gain, norm_shift):
    center = values - lax.optimization_barrier(jnp.mean(values, axis=-1, keepdims=True))
    spread = lax.optimization_barrier(jnp.mean(center * center, axis=-1, keepdims=True))
    return center * lax.rsqrt(spread + EPSILON) * norm_gain + norm_shift

def matmul_f32(left_mat, right_mat):
    return jnp.dot(left_mat, right_mat, precision=lax.Precision.HIGHEST, preferred_element_type=jnp.float32)

def split_heads(matrix):
    return matrix.reshape(matrix.shape[0], H, HD)

def distance_codes(box_rows):
    step_x = jnp.minimum(jnp.abs(box_rows[0][:, None] - box_rows[0][None, :]), GRID - 1)
    step_y = jnp.minimum(jnp.abs(box_rows[1][:, None] - box_rows[1][None, :]), GRID - 1)
    return (step_x * GRID + step_y).astype(jnp.int32)

def project(inputs, norm_gain, norm_shift, weight, bias_rows):
    normed = low(layer_norm(inputs, norm_gain, norm_shift))
    combined = matmul_f32(normed, weight)
    queries = low_back(low(combined[:, :D] + bias_rows[0]))
    key_part = low_back(low(combined[:, D:2 * D]))
    value_part = low_back(low(combined[:, 2 * D:] + bias_rows[1]))
    return (queries, key_part, value_part)

def attend(queries, key_part, value_part, key_far, value_far, near_bias, allowed):
    keys_all = jnp.concatenate([key_part, key_far], axis=0)
    values_all = jnp.concatenate([value_part, value_far], axis=0)
    raw_scores = jnp.einsum('qhd,khd->hqk', split_heads(queries), split_heads(keys_all), precision=lax.Precision.HIGHEST) * HD ** (-0.5)
    near_scores = jnp.where(allowed[None], raw_scores[:, :, :SEQ] + near_bias, MASKED)
    scores = low_back(jnp.concatenate([near_scores, raw_scores[:, :, SEQ:]], axis=2))
    row_max = lax.optimization_barrier(jnp.max(scores, axis=2, keepdims=True))
    exponent = jnp.exp(scores - row_max)
    probabilities = low(exponent / lax.optimization_barrier(jnp.sum(exponent, axis=2, keepdims=True)))
    combined = jnp.einsum('hqk,khd->qhd', probabilities, split_heads(values_all), precision=lax.Precision.HIGHEST)
    return low_back(low(combined.reshape(SEQ, D)))

def finish(inputs, attended, norm_gain, norm_shift, out_weight, out_bias, up_weight, up_vector, down_weight, down_vector):
    branch = low_back(matmul_f32(attended, out_weight) + out_bias)
    middle = inputs + branch
    normed_two = low(layer_norm(middle, norm_gain, norm_shift))
    pre_act = low_back(matmul_f32(normed_two, up_weight) + up_vector)
    activated = low(jax.nn.gelu(pre_act, approximate=False))
    ffn_out = low_back(matmul_f32(activated, down_weight) + down_vector)
    return middle + ffn_out

def layer_pair(inputs, params, segments, box_pair):
    norm_gains, norm_shifts, qkv_weight, bias_sets, bias_table, out_weight, up_weight, up_vector, down_weight, down_vector = params
    projected = [project(inputs[stream_id], norm_gains[stream_id, 0], norm_shifts[stream_id, 0], qkv_weight[stream_id], bias_sets[stream_id]) for stream_id in range(2)]
    same_doc = segments[:, None] == segments[None, :]
    results = []
    for stream_id in range(2):
        queries, key_part, value_part = projected[stream_id]
        partner = projected[1 - stream_id]
        near_bias = jnp.transpose(bias_table[stream_id][distance_codes(box_pair[stream_id])], (2, 0, 1))
        allowed = same_doc if stream_id == 0 else jnp.ones_like(same_doc)
        attended = attend(queries, key_part, value_part, partner[1], partner[2], near_bias, allowed)
        results.append(finish(inputs[stream_id], attended, norm_gains[stream_id, 1], norm_shifts[stream_id, 1], out_weight[stream_id], bias_sets[stream_id, 2], up_weight[stream_id], up_vector[stream_id], down_weight[stream_id], down_vector[stream_id]))
    return jnp.stack(results)

def reference(features, cotangent, segment_ids, box_cells, ln_gain, ln_shift, w_qkv, attn_bias, distance_table, w_out, w_up, up_bias, w_down, down_bias):
    params = tuple((member.astype(jnp.float32) for member in (ln_gain, ln_shift, w_qkv, attn_bias, distance_table, w_out, w_up, up_bias, w_down, down_bias)))

    def one_row(totals, row_items):
        row_in, row_cot, row_seg, row_box = row_items

        def forward(layer_in, weights):
            return layer_pair(layer_in, weights, row_seg, row_box)
        row_out, pull_back = jax.vjp(forward, row_in.astype(jnp.float32), params)
        grad_in, grad_weights = pull_back(row_cot.astype(jnp.float32))
        totals = jax.tree.map(jnp.add, totals, grad_weights)
        return (totals, (row_out.astype(jnp.bfloat16), grad_in.astype(jnp.bfloat16)))
    starts = tuple((jnp.zeros_like(member) for member in params))
    by_rows = (jnp.swapaxes(features, 0, 1), jnp.swapaxes(cotangent, 0, 1), segment_ids, jnp.swapaxes(box_cells, 0, 1))
    totals, (outputs, input_grads) = lax.scan(one_row, starts, by_rows)
    return (jnp.swapaxes(outputs, 0, 1), jnp.swapaxes(input_grads, 0, 1), totals[0], totals[1], totals[2], totals[3], totals[4], totals[5], totals[6], totals[7], totals[8], totals[9])
```

```python
import functools
import jax
import jax.numpy as jnp
from jax import lax
from jax.experimental import pallas as pl
from jax.experimental.pallas import tpu as pltpu
from jax.sharding import PartitionSpec as P

GRID = 8
EPSILON = 1e-05
MASKED = -1000000000.0

NT=(((1,),(1,)),((),())); NN=(((1,),(0,)),((),())); TN=(((0,),(0,)),((),()))
def mm(a,b,dn=NN): return lax.dot_general(a,b,dn,preferred_element_type=jnp.float32)
BF=jnp.bfloat16

def three(x):
    hi=x.astype(BF); r=x-hi.astype(jnp.float32); mid=r.astype(BF); lo=(r-mid.astype(jnp.float32)).astype(BF)
    return hi,mid,lo

def fwd_kernel(CQ, q_ref,kn_ref,kf_ref,vn_ref,vf_ref,e_ref,b_ref,qseg_ref,kseg_ref,o_ref,qm_ref):
    pair=pl.program_id(1)
    L=q_ref.shape[0]
    lane=lax.broadcasted_iota(jnp.int32,(1,128),1)
    @pl.when(pair==0)
    def _():
        qm_ref[...]=qseg_ref[...]
    outs=[None]*(L//CQ)
    for hh in range(2):
        mh=(lane<64) if hh==0 else (lane>=64)
        h=2*pair+hh
        C=mm(e_ref[...],b_ref[hh]).astype(BF)
        kx=jnp.concatenate([kn_ref[...],C,kseg_ref[...]],axis=1)
        kf=kf_ref[...]
        one=jnp.ones((),BF); zero=jnp.zeros((),BF)
        vnx=jnp.where(mh,vn_ref[...],one); vfx=jnp.where(mh,vf_ref[...],one)
        for c in range(L//CQ):
            sl=slice(c*CQ,(c+1)*CQ)
            qm=jnp.where(mh,q_ref[sl,:],zero)
            qx=jnp.concatenate([qm,e_ref[sl,:],qseg_ref[sl,:]],axis=1)
            sn=mm(qx,kx,NT); sf=mm(qm,kf,NT)
            m=jnp.maximum(jnp.max(sn,axis=1,keepdims=True),jnp.max(sf,axis=1,keepdims=True))
            pn=jnp.exp(sn-m).astype(BF); pf=jnp.exp(sf-m).astype(BF)
            o=mm(pn,vnx)+mm(pf,vfx)
            l=pltpu.roll(o,64,1)
            on=o/l
            outs[c]=on if hh==0 else jnp.where(mh,on,outs[c])
            lse=-(m+jnp.log(jnp.where(mh,l,o)))
            hi,mid,lo=three(lse)
            cur=qm_ref[sl,:]
            cur=jnp.where(lane==3*h,hi,cur); cur=jnp.where(lane==3*h+1,mid,cur); cur=jnp.where(lane==3*h+2,lo,cur)
            qm_ref[sl,:]=cur
    for c in range(L//CQ):
        o_ref[c*CQ:(c+1)*CQ,:]=outs[c].astype(BF)

def fwd(q,kn,kf,vn,vf,e,bt,qseg,kseg,L,CQ=512):
    T=q.shape[0]; R=T//L; NP=q.shape[1]//128
    blk=pl.BlockSpec((L,128),lambda r,p:(r,p))
    row=lambda w: pl.BlockSpec((L,w),lambda r,p:(r,0))
    return pl.pallas_call(functools.partial(fwd_kernel,CQ),grid=(R,NP),
        in_specs=[blk]*5+[row(256),pl.BlockSpec((2,256,256),lambda r,p:(p,0,0)),row(128),row(128)],
        out_specs=[blk,row(128)],
        out_shape=[jax.ShapeDtypeStruct(q.shape,BF),jax.ShapeDtypeStruct((T,128),BF)],
        compiler_params=pltpu.CompilerParams(vmem_limit_bytes=48<<20),name="att_fwd")(q,kn,kf,vn,vf,e,bt,qseg,kseg)

def bwd_kernel(CK,MODE, q_ref,kn_ref,kf_ref,vn_ref,vf_ref,do_ref,o_ref,e_ref,et_ref,b_ref,qmisc_ref,kseg_ref,
               dq_ref,dkn_ref,dkf_ref,dvn_ref,dvf_ref,g_ref):
    pair=pl.program_id(0); r=pl.program_id(1)
    L=q_ref.shape[0]
    lane=lax.broadcasted_iota(jnp.int32,(1,128),1)
    zero=jnp.zeros((),BF)
    n=L//CK
    dkn=[None]*n; dkf=[None]*n; dvn=[None]*n; dvf=[None]*n
    dq=None
    prod=do_ref[...].astype(jnp.float32)*o_ref[...].astype(jnp.float32)
    add=lambda a,b: b if a is None else a+b
    for hh in range(2):
        mh=(lane<64) if hh==0 else (lane>=64)
        h=2*pair+hh
        delta=-jnp.sum(jnp.where(mh,prod,0.0),axis=1,keepdims=True)
        hi,mid,lo=three(delta)
        dmisc=jnp.where(lane==0,hi,jnp.where(lane==1,mid,zero))
        qm=jnp.where(mh,q_ref[...],zero); dom=jnp.where(mh,do_ref[...],zero)
        C=mm(e_ref[...],b_ref[hh]).astype(BF)
        ones_h=jnp.where((lane>=3*h)&(lane<3*h+3),1.0,0.0)
        ones_b=jnp.broadcast_to(ones_h.astype(BF),(CK,128))
        ones01=jnp.broadcast_to(jnp.where(lane<2,1.0,0.0).astype(BF),(CK,128))
        qx=jnp.concatenate([qm,e_ref[...],qmisc_ref[...]],axis=1)
        qf=jnp.concatenate([qm,qmisc_ref[...]],axis=1)
        dox=jnp.concatenate([dom,dmisc],axis=1)
        qe=jnp.concatenate([qm,e_ref[...]],axis=1)
        g=None
        for c in range(n):
            sl=slice(c*CK,(c+1)*CK)
            kseg=(kseg_ref[sl,:].astype(jnp.float32)+ones_h).astype(BF)
            kx=jnp.concatenate([kn_ref[sl,:],C[sl,:],kseg],axis=1)
            p=jnp.exp(mm(kx,qx,NT))
            vx=jnp.concatenate([vn_ref[sl,:],ones01],axis=1)
            ds=(p*mm(vx,dox,NT)).astype(BF); pb=p.astype(BF)
            dvn[c]=add(dvn[c],mm(pb,dom))
            t=mm(ds,qe)
            dkn[c]=add(dkn[c],t[:,:128])
            g=add(g,mm(et_ref[:,sl],t[:,128:].astype(BF)))
            dq=add(dq,mm(ds,jnp.where(mh,kn_ref[sl,:],zero),TN))
        for c in range(n):
            sl=slice(c*CK,(c+1)*CK)
            kx=jnp.concatenate([kf_ref[sl,:],ones_b],axis=1)
            p=jnp.exp(mm(kx,qf,NT))
            vx=jnp.concatenate([vf_ref[sl,:],ones01],axis=1)
            ds=(p*mm(vx,dox,NT)).astype(BF); pb=p.astype(BF)
            dvf[c]=add(dvf[c],mm(pb,dom))
            dkf[c]=add(dkf[c],mm(ds,qm))
            dq=add(dq,mm(ds,jnp.where(mh,kf_ref[sl,:],zero),TN))
        @pl.when(r==0)
        def _(): g_ref[hh]=g
        @pl.when(r!=0)
        def _(): g_ref[hh]+=g
    dq_ref[...]=(dq*0.125).astype(BF)
    for c in range(n):
        sl=slice(c*CK,(c+1)*CK)
        dkn_ref[sl,:]=dkn[c].astype(BF); dkf_ref[sl,:]=dkf[c].astype(BF)
        dvn_ref[sl,:]=dvn[c].astype(BF); dvf_ref[sl,:]=dvf[c].astype(BF)

def bwd(q,kn,kf,vn,vf,do,o,e,et,bt,qmisc,kseg,L,CK=512,MODE=0):
    T=q.shape[0]; R=T//L; NP=q.shape[1]//128
    blk=pl.BlockSpec((L,128),lambda p,r:(r,p))
    row=lambda w: pl.BlockSpec((L,w),lambda p,r:(r,0))
    return pl.pallas_call(functools.partial(bwd_kernel,CK,MODE),grid=(NP,R),
        in_specs=[blk]*7+[row(256),pl.BlockSpec((256,L),lambda p,r:(0,r)),pl.BlockSpec((2,256,256),lambda p,r:(p,0,0)),row(128),row(128)],
        out_specs=[blk]*5+[pl.BlockSpec((2,256,256),lambda p,r:(p,0,0))],
        out_shape=[jax.ShapeDtypeStruct(q.shape,BF)]*5+[jax.ShapeDtypeStruct((2*NP,256,256),jnp.float32)],
        compiler_params=pltpu.CompilerParams(vmem_limit_bytes=48<<20),name="att_bwd")(q,kn,kf,vn,vf,do,o,e,et,bt,qmisc,kseg)


def from_partner(block, axis, stride):
    count = lax.axis_size(axis)
    route = []
    for low in range(count):
        high = low | 1 << stride
        if high != low and high < count:
            route += [(low, high), (high, low)]
    return lax.ppermute(block, axis, route)


def layer_norm(values, norm_gain, norm_shift):
    center = values - jnp.mean(values, axis=-1, keepdims=True)
    spread = jnp.mean(center * center, axis=-1, keepdims=True)
    return center * lax.rsqrt(spread + EPSILON) * norm_gain + norm_shift


def norm_back(values, norm_gain, norm_shift, upstream):
    unused, pull_back = jax.vjp(layer_norm, values, norm_gain, norm_shift)
    return pull_back(upstream)


def gelu_exact(values):
    return jax.nn.gelu(values, approximate=False)


def gelu_back(values, upstream):
    unused, pull_back = jax.vjp(gelu_exact, values)
    return pull_back(upstream)[0]


def prepare(segment_ids, box_cells, table, is_vision):
    cell = (box_cells[:, 0] * 16 + box_cells[:, 1]).reshape(-1)
    cells = jnp.arange(256)
    e = (cell[:, None] == cells[None]).astype(BF)
    et = (cells[:, None] == cell[None]).astype(BF)
    lane = jnp.arange(128)
    same = segment_ids.reshape(-1)[:, None] == lane[None] - 64
    inside = (lane >= 64) & (lane < 68)
    qseg = same.astype(BF)
    kseg = jnp.where(inside[None] & ~same & jnp.logical_not(is_vision), MASKED, 0.0).astype(BF)
    return e, et, qseg, kseg


def code_onehot():
    c = jnp.arange(65536)
    step_x = jnp.minimum(jnp.abs(c // 4096 - (c // 16) % 16), GRID - 1)
    step_y = jnp.minimum(jnp.abs((c // 256) % 16 - c % 16), GRID - 1)
    return ((step_x * GRID + step_y)[None] == jnp.arange(GRID * GRID)[:, None]).astype(BF)


def on_device(features, cotangent, segment_ids, box_cells, ln_gain, ln_shift, w_qkv, attn_bias,
              distance_table, w_out, w_up, up_bias, w_down, down_bias):
    rows, length, width = features.shape[1:]
    tokens = rows * length
    heads = distance_table.shape[2]
    is_vision = lax.axis_index("stream") != 0
    norm_gains, norm_shifts = ln_gain[0], ln_shift[0]
    bias_rows = attn_bias[0]
    qkv_weight, out_weight, up_weight, down_weight = w_qkv[0], w_out[0], w_up[0], w_down[0]
    plain_in = features[0].reshape(tokens, width).astype(jnp.float32)
    normed = layer_norm(plain_in, norm_gains[0], norm_shifts[0]).astype(BF)
    combined = jnp.dot(normed, qkv_weight, preferred_element_type=jnp.float32)
    queries = (combined[:, :width] + bias_rows[0]).astype(BF) * BF(0.125)
    key_part = combined[:, width:2 * width].astype(BF)
    value_part = (combined[:, 2 * width:] + bias_rows[1]).astype(BF)
    partner_k = from_partner(key_part, "stream", 0)
    partner_v = from_partner(value_part, "stream", 0)
    e, et, qseg, kseg = prepare(segment_ids, box_cells[0], distance_table[0], is_vision)
    onehot = code_onehot()
    bt = jnp.dot(distance_table[0].T.astype(BF), onehot, preferred_element_type=jnp.float32).astype(BF).reshape(heads, 256, 256)
    attended, qmisc = fwd(queries, key_part, partner_k, value_part, partner_v, e, bt, qseg, kseg, length)
    middle = plain_in + jnp.dot(attended, out_weight, preferred_element_type=jnp.float32) + bias_rows[2]
    normed_two = layer_norm(middle, norm_gains[1], norm_shifts[1]).astype(BF)
    pre_act = jnp.dot(normed_two, up_weight, preferred_element_type=jnp.float32) + up_bias[0]
    activated = gelu_exact(pre_act).astype(BF)
    result = middle + jnp.dot(activated, down_weight, preferred_element_type=jnp.float32) + down_bias[0]
    output = result.astype(BF).reshape(1, rows, length, width)
    cot_bf = cotangent[0].reshape(tokens, width)
    cot_f32 = cot_bf.astype(jnp.float32)
    grad_down = jnp.einsum("tf,td->fd", activated, cot_bf, preferred_element_type=jnp.float32).astype(BF)
    grad_down_bias = jnp.sum(cot_f32, axis=0)
    grad_act = jnp.einsum("td,fd->tf", cot_bf, down_weight, preferred_element_type=jnp.float32)
    grad_pre = gelu_back(pre_act, grad_act).astype(BF)
    grad_up = jnp.einsum("td,tf->df", normed_two, grad_pre, preferred_element_type=jnp.float32).astype(BF)
    grad_up_bias = jnp.sum(grad_pre.astype(jnp.float32), axis=0)
    grad_normed_two = jnp.einsum("tf,df->td", grad_pre, up_weight, preferred_element_type=jnp.float32)
    grad_mid_part, gain_two, shift_two = norm_back(middle, norm_gains[1], norm_shifts[1], grad_normed_two)
    grad_middle = cot_f32 + grad_mid_part
    grad_branch = grad_middle.astype(BF)
    grad_out = jnp.einsum("td,te->de", attended, grad_branch, preferred_element_type=jnp.float32).astype(BF)
    grad_out_bias = jnp.sum(grad_branch.astype(jnp.float32), axis=0)
    grad_attended = jnp.einsum("te,de->td", grad_branch, out_weight, preferred_element_type=jnp.float32).astype(BF)
    sum_up, sum_down, sum_out = lax.psum((grad_up, grad_down, grad_out), "batch")
    dq, dkn, dkf, dvn, dvf, g = bwd(queries, key_part, partner_k, value_part, partner_v, grad_attended, attended,
                                    e, et, bt, qmisc, kseg, length)
    back_k = from_partner(dkf, "stream", 0)
    back_v = from_partner(dvf, "stream", 0)
    grad_k = (dkn.astype(jnp.float32) + back_k.astype(jnp.float32)).astype(BF)
    grad_v = (dvn.astype(jnp.float32) + back_v.astype(jnp.float32)).astype(BF)
    grad_dist = jnp.einsum("hp,np->nh", g.reshape(heads, 65536).astype(BF), onehot, preferred_element_type=jnp.float32)
    grad_mixed = jnp.concatenate([dq, grad_k, grad_v], axis=1)
    grad_qkv = jnp.einsum("td,te->de", normed, grad_mixed, preferred_element_type=jnp.float32).astype(BF)
    grad_bias_rows = jnp.stack([jnp.sum(dq.astype(jnp.float32), axis=0), jnp.sum(grad_v.astype(jnp.float32), axis=0), grad_out_bias])
    grad_normed = jnp.einsum("te,de->td", grad_mixed, qkv_weight, preferred_element_type=jnp.float32)
    grad_in_part, gain_one, shift_one = norm_back(plain_in, norm_gains[0], norm_shifts[0], grad_normed)
    input_grad = (grad_middle + grad_in_part).astype(BF).reshape(1, rows, length, width)
    small = [jnp.stack([gain_one, gain_two]), jnp.stack([shift_one, shift_two]), grad_bias_rows, grad_dist, grad_up_bias, grad_down_bias]
    flat = jnp.concatenate([s.reshape(-1) for s in small])
    sum_qkv = lax.psum(grad_qkv, "batch")
    flat = lax.psum(flat, "batch")
    parts, at = [], 0
    for s in small:
        parts.append(flat[at:at + s.size].reshape(s.shape)[None])
        at += s.size
    gain, shift, bias, dist, upb, downb = parts
    f32 = lambda a: a.astype(jnp.float32)[None]
    return (output, input_grad, gain, shift, f32(sum_qkv), bias, dist, f32(sum_out), f32(sum_up), upb, f32(sum_down), downb)


def solution(mesh):
    in_specs = (
        P("stream", "batch", None, None),
        P("stream", "batch", None, None),
        P("batch", None),
        P("stream", "batch", None, None),
        P("stream", None, None),
        P("stream", None, None),
        P("stream", None, None),
        P("stream", None, None),
        P("stream", None, None),
        P("stream", None, None),
        P("stream", None, None),
        P("stream", None),
        P("stream", None, None),
        P("stream", None),
    )
    out_specs = (
        P("stream", "batch", None, None),
        P("stream", "batch", None, None),
        P("stream", None, None),
        P("stream", None, None),
        P("stream", None, None),
        P("stream", None, None),
        P("stream", None, None),
        P("stream", None, None),
        P("stream", None, None),
        P("stream", None),
        P("stream", None, None),
        P("stream", None),
    )
    return jax.shard_map(
        on_device, mesh=mesh, in_specs=in_specs, out_specs=out_specs, check_vma=False
    )
```

```python
import functools
import jax
import jax.numpy as jnp
from jax import lax
from jax.experimental import pallas as pl
from jax.experimental.pallas import tpu as pltpu
from jax.sharding import PartitionSpec as P

GRID = 8
EPSILON = 1e-05
MASKED = -1000000000.0

NT=(((1,),(1,)),((),())); NN=(((1,),(0,)),((),())); TN=(((0,),(0,)),((),()))
def mm(a,b,dn=NN): return lax.dot_general(a,b,dn,preferred_element_type=jnp.float32)
BF=jnp.bfloat16

def three(x):
    hi=x.astype(BF); r=x-hi.astype(jnp.float32); mid=r.astype(BF); lo=(r-mid.astype(jnp.float32)).astype(BF)
    return hi,mid,lo

def fwd_kernel(CQ, q_ref,kn_ref,kf_ref,vn_ref,vf_ref,e_ref,b_ref,qseg_ref,kseg_ref,o_ref,qm_ref):
    pair=pl.program_id(1)
    L=q_ref.shape[0]
    lane=lax.broadcasted_iota(jnp.int32,(1,128),1)
    @pl.when(pair==0)
    def _():
        qm_ref[...]=qseg_ref[...]
    outs=[None]*(L//CQ)
    for hh in range(2):
        mh=(lane<64) if hh==0 else (lane>=64)
        h=2*pair+hh
        C=mm(e_ref[...],b_ref[hh]).astype(BF)
        kx=jnp.concatenate([kn_ref[...],C,kseg_ref[...]],axis=1)
        kf=kf_ref[...]
        one=jnp.ones((),BF); zero=jnp.zeros((),BF)
        vnx=jnp.where(mh,vn_ref[...],one); vfx=jnp.where(mh,vf_ref[...],one)
        for c in range(L//CQ):
            sl=slice(c*CQ,(c+1)*CQ)
            qm=jnp.where(mh,q_ref[sl,:],zero)
            qx=jnp.concatenate([qm,e_ref[sl,:],qseg_ref[sl,:]],axis=1)
            sn=mm(qx,kx,NT); sf=mm(qm,kf,NT)
            m=jnp.maximum(jnp.max(sn,axis=1,keepdims=True),jnp.max(sf,axis=1,keepdims=True))
            pn=jnp.exp(sn-m).astype(BF); pf=jnp.exp(sf-m).astype(BF)
            o=mm(pn,vnx)+mm(pf,vfx)
            l=pltpu.roll(o,64,1)
            on=o/l
            outs[c]=on if hh==0 else jnp.where(mh,on,outs[c])
            lse=-(m+jnp.log(jnp.where(mh,l,o)))
            hi,mid,lo=three(lse)
            cur=qm_ref[sl,:]
            cur=jnp.where(lane==3*h,hi,cur); cur=jnp.where(lane==3*h+1,mid,cur); cur=jnp.where(lane==3*h+2,lo,cur)
            qm_ref[sl,:]=cur
    for c in range(L//CQ):
        o_ref[c*CQ:(c+1)*CQ,:]=outs[c].astype(BF)

def fwd(q,kn,kf,vn,vf,e,bt,qseg,kseg,L,CQ=512):
    T=q.shape[0]; R=T//L; NP=q.shape[1]//128
    blk=pl.BlockSpec((L,128),lambda r,p:(r,p))
    row=lambda w: pl.BlockSpec((L,w),lambda r,p:(r,0))
    return pl.pallas_call(functools.partial(fwd_kernel,CQ),grid=(R,NP),
        in_specs=[blk]*5+[row(256),pl.BlockSpec((2,256,256),lambda r,p:(p,0,0)),row(128),row(128)],
        out_specs=[blk,row(128)],
        out_shape=[jax.ShapeDtypeStruct(q.shape,BF),jax.ShapeDtypeStruct((T,128),BF)],
        compiler_params=pltpu.CompilerParams(vmem_limit_bytes=48<<20),name="att_fwd")(q,kn,kf,vn,vf,e,bt,qseg,kseg)

def bwd_kernel(CK,MODE, q_ref,kn_ref,kf_ref,vn_ref,vf_ref,do_ref,o_ref,e_ref,et_ref,b_ref,qmisc_ref,kseg_ref,
               dq_ref,dkn_ref,dkf_ref,dvn_ref,dvf_ref,g_ref):
    pair=pl.program_id(0); r=pl.program_id(1)
    L=q_ref.shape[0]
    lane=lax.broadcasted_iota(jnp.int32,(1,128),1)
    zero=jnp.zeros((),BF)
    n=L//CK
    dkn=[None]*n; dkf=[None]*n; dvn=[None]*n; dvf=[None]*n
    dq=None
    prod=do_ref[...].astype(jnp.float32)*o_ref[...].astype(jnp.float32)
    add=lambda a,b: b if a is None else a+b
    for hh in range(2):
        mh=(lane<64) if hh==0 else (lane>=64)
        h=2*pair+hh
        delta=-jnp.sum(jnp.where(mh,prod,0.0),axis=1,keepdims=True)
        hi,mid,lo=three(delta)
        dmisc=jnp.where(lane==0,hi,jnp.where(lane==1,mid,zero))
        qm=jnp.where(mh,q_ref[...],zero); dom=jnp.where(mh,do_ref[...],zero)
        C=mm(e_ref[...],b_ref[hh]).astype(BF)
        ones_h=jnp.where((lane>=3*h)&(lane<3*h+3),1.0,0.0)
        ones_b=jnp.broadcast_to(ones_h.astype(BF),(CK,128))
        ones01=jnp.broadcast_to(jnp.where(lane<2,1.0,0.0).astype(BF),(CK,128))
        qx=jnp.concatenate([qm,e_ref[...],qmisc_ref[...]],axis=1)
        qf=jnp.concatenate([qm,qmisc_ref[...]],axis=1)
        dox=jnp.concatenate([dom,dmisc],axis=1)
        qe=jnp.concatenate([qm,e_ref[...]],axis=1)
        g=None
        for c in range(n):
            sl=slice(c*CK,(c+1)*CK)
            kseg=(kseg_ref[sl,:].astype(jnp.float32)+ones_h).astype(BF)
            kx=jnp.concatenate([kn_ref[sl,:],C[sl,:],kseg],axis=1)
            p=jnp.exp(mm(kx,qx,NT))
            vx=jnp.concatenate([vn_ref[sl,:],ones01],axis=1)
            ds=(p*mm(vx,dox,NT)).astype(BF); pb=p.astype(BF)
            dvn[c]=add(dvn[c],mm(pb,dom))
            t=mm(ds,qe)
            dkn[c]=add(dkn[c],t[:,:128])
            g=add(g,mm(et_ref[:,sl],t[:,128:].astype(BF)))
            dq=add(dq,mm(ds,jnp.where(mh,kn_ref[sl,:],zero),TN))
        for c in range(n):
            sl=slice(c*CK,(c+1)*CK)
            kx=jnp.concatenate([kf_ref[sl,:],ones_b],axis=1)
            p=jnp.exp(mm(kx,qf,NT))
            vx=jnp.concatenate([vf_ref[sl,:],ones01],axis=1)
            ds=(p*mm(vx,dox,NT)).astype(BF); pb=p.astype(BF)
            dvf[c]=add(dvf[c],mm(pb,dom))
            dkf[c]=add(dkf[c],mm(ds,qm))
            dq=add(dq,mm(ds,jnp.where(mh,kf_ref[sl,:],zero),TN))
        @pl.when(r==0)
        def _(): g_ref[hh]=g
        @pl.when(r!=0)
        def _(): g_ref[hh]+=g
    dq_ref[...]=(dq*0.125).astype(BF)
    for c in range(n):
        sl=slice(c*CK,(c+1)*CK)
        dkn_ref[sl,:]=dkn[c].astype(BF); dkf_ref[sl,:]=dkf[c].astype(BF)
        dvn_ref[sl,:]=dvn[c].astype(BF); dvf_ref[sl,:]=dvf[c].astype(BF)

def bwd(q,kn,kf,vn,vf,do,o,e,et,bt,qmisc,kseg,L,CK=512,MODE=0):
    T=q.shape[0]; R=T//L; NP=q.shape[1]//128
    blk=pl.BlockSpec((L,128),lambda p,r:(r,p))
    row=lambda w: pl.BlockSpec((L,w),lambda p,r:(r,0))
    return pl.pallas_call(functools.partial(bwd_kernel,CK,MODE),grid=(NP,R),
        in_specs=[blk]*7+[row(256),pl.BlockSpec((256,L),lambda p,r:(0,r)),pl.BlockSpec((2,256,256),lambda p,r:(p,0,0)),row(128),row(128)],
        out_specs=[blk]*5+[pl.BlockSpec((2,256,256),lambda p,r:(p,0,0))],
        out_shape=[jax.ShapeDtypeStruct(q.shape,BF)]*5+[jax.ShapeDtypeStruct((2*NP,256,256),jnp.float32)],
        compiler_params=pltpu.CompilerParams(vmem_limit_bytes=48<<20),name="att_bwd")(q,kn,kf,vn,vf,do,o,e,et,bt,qmisc,kseg)


F32=jnp.float32
SIDE=768
WIDE=384
LAG=3

def bit_orders(n, count):
    bits=n.bit_length()-1
    plain=list(range(bits))
    other=[0]+plain[2:]+[1] if bits>2 else plain
    return [other if c%5==3 else plain for c in range(count)]

def plan_of(n, order, rows):
    sizes=[rows]
    for _ in order:
        m=sizes[-1]
        sizes.append(m//2 if m%32==0 else m)
    return sizes

def place(me, b):
    bit=(me//(1<<b))%2
    return bit, me+(1-2*bit)*(1<<b)

class Engine:
    def __init__(self, n, orders, x, y, recv, offs, send_sem, recv_sem, me):
        self.n,self.orders,self.x,self.y,self.recv,self.offs=n,orders,x,y,recv,offs
        self.ss,self.rs,self.me=send_sem,recv_sem,me
        self.bits=n.bit_length()-1
        self.pending={}
    def seg(self,c,upto):
        sizes=plan_of(self.n,self.orders[c],SIDE); off=0
        for s in range(upto):
            if sizes[s+1]!=sizes[s]:
                off=off+place(self.me,self.orders[c][s])[0]*sizes[s+1]
        return off,sizes[upto]
    def ds(self,off,size):
        return pl.ds(off if isinstance(off,int) else pl.multiple_of(off,16),size)
    def start(self,c,stage):
        B=self.bits; order=self.orders[c]; sizes=plan_of(self.n,order,SIDE)
        if stage<B:
            b=order[stage]; bit,partner=place(self.me,b)
            off,m=self.seg(c,stage)
            if sizes[stage+1]!=m:
                src=self.x.at[c,self.ds(off+(1-bit)*(m//2),m//2)]
            else:
                src=self.x.at[c,self.ds(off,m)]
            dst=self.recv.at[c,pl.ds(self.offs[c][stage],sizes[stage+1])]
        else:
            s=2*B-1-stage
            if sizes[s+1]==sizes[s]: return
            b=order[s]; bit,partner=place(self.me,b)
            off,m=self.seg(c,s+1)
            src=self.y.at[c,self.ds(off,m)]; dst=src
        d=pltpu.make_async_remote_copy(src,dst,self.ss.at[c,stage],self.rs.at[c,stage],
            device_id={"batch":partner},device_id_type=pl.DeviceIdType.MESH)
        d.start(); self.pending[(c,stage)]=d
    def finish(self,c,stage):
        B=self.bits; order=self.orders[c]; sizes=plan_of(self.n,order,SIDE)
        d=self.pending.pop((c,stage),None)
        if d is None: return
        d.wait()
        if stage<B:
            off,m=self.seg(c,stage+1); ro=self.offs[c][stage]; x,recv=self.x,self.recv
            to=self.y if stage==B-1 else x
            step=48
            def body(i,_):
                at=self.ds(off+i*step,step)
                to[c,at]=(x[c,at].astype(F32)+recv[c,pl.ds(pl.multiple_of(ro+i*step,16),step)].astype(F32)).astype(BF)
                return 0
            lax.fori_loop(0,m//step,body,0)

def recv_offsets(n, orders):
    res=[]
    for o in orders:
        sizes=plan_of(n,o,SIDE); at=[0]
        for s in range(len(o)): at.append(at[-1]+sizes[s+1])
        res.append(at)
    return res

def barrier(n, me):
    sem=pltpu.get_barrier_semaphore()
    bits=n.bit_length()-1
    for b in range(bits):
        pl.semaphore_signal(sem,inc=1,device_id={"batch":place(me,b)[1]},device_id_type=pl.DeviceIdType.MESH)
    pl.semaphore_wait(sem,bits)

def ar_kernel(n, layout, with_small, *refs):
    na=max(a for a,_,_ in layout)+1
    ins=refs[:na]; refs=refs[na:]
    if with_small: small_in,refs=refs[0],refs[1:]
    outs=refs[:na]; refs=refs[na:]
    if with_small: small_out,refs=refs[0],refs[1:]
    x,y,recv,in_sem,out_sem,ss,rs=refs[:7]
    C=len(layout)
    me=lax.axis_index("batch")
    orders=bit_orders(n,C); offs=recv_offsets(n,orders)
    def view(ref,a,r,c): return ref.at[pl.ds(r*SIDE,SIDE),pl.ds(c*WIDE,WIDE)]
    loads=[]
    for c,(a,r,k) in enumerate(layout):
        d=pltpu.make_async_copy(view(ins[a],a,r,k),x.at[c],in_sem.at[c]); d.start(); loads.append(d)
    barrier(n,me)
    eng=Engine(n,orders,x,y,recv,offs,ss,rs,me)
    B=eng.bits
    if with_small:
        small_x,small_recv,small_sem,small_ss,small_rs=refs[7:12]
        d=pltpu.make_async_copy(small_in,small_x.at[0],small_sem); d.start(); d.wait()
    def small_copy(s):
        return pltpu.make_async_remote_copy(small_x.at[s],small_recv.at[s],small_ss.at[s],small_rs.at[s],
            device_id={"batch":place(me,s)[1]},device_id_type=pl.DeviceIdType.MESH)
    small_d=None
    stores={}
    for t in range(C+LAG*2*B):
        if with_small and t%LAG==0 and t//LAG<=B:
            i=t//LAG
            if i>0:
                small_d.wait()
                small_x[i]=small_x[i-1]+small_recv[i-1]
            if i<B:
                small_d=small_copy(i); small_d.start()
            else:
                small_d=pltpu.make_async_copy(small_x.at[i],small_out,small_sem); small_d.start()
        for s in range(2*B,-1,-1):
            c=t-LAG*s
            if not 0<=c<C: continue
            if s==0: loads[c].wait()
            else: eng.finish(c,s-1)
            if s<2*B: eng.start(c,s)
            else:
                a,r,k=layout[c]
                d=pltpu.make_async_copy(y.at[c],view(outs[a],a,r,k),out_sem.at[c]); d.start(); stores[c]=d
    for c in range(C): stores[c].wait()
    if with_small: small_d.wait()

def allreduce(arrays, n, collective_id, small=None):
    layout=[]
    for a,arr in enumerate(arrays):
        for r in range(arr.shape[0]//SIDE):
            for k in range(arr.shape[1]//WIDE): layout.append((a,r,k))
    C=len(layout); bits=n.bit_length()-1
    rows=max(o[-1] for o in recv_offsets(n,bit_orders(n,C)))
    scratch=[pltpu.VMEM((C,SIDE,WIDE),BF),pltpu.VMEM((C,SIDE,WIDE),BF),pltpu.VMEM((C,rows,WIDE),BF),
            pltpu.SemaphoreType.DMA((C,)),pltpu.SemaphoreType.DMA((C,)),pltpu.SemaphoreType.DMA((C,2*bits)),pltpu.SemaphoreType.DMA((C,2*bits))]
    extra=[]
    if small is not None:
        extra=[small]
        scratch+=[pltpu.VMEM((bits+1,)+small.shape,F32),pltpu.VMEM((bits,)+small.shape,F32),pltpu.SemaphoreType.DMA,
            pltpu.SemaphoreType.DMA((bits,)),pltpu.SemaphoreType.DMA((bits,))]
    return pl.pallas_call(functools.partial(ar_kernel,n,layout,small is not None),
        in_specs=[pl.BlockSpec(memory_space=pl.ANY)]*(len(arrays)+len(extra)),
        out_specs=[pl.BlockSpec(memory_space=pl.ANY)]*(len(arrays)+len(extra)),
        out_shape=[jax.ShapeDtypeStruct(a.shape,a.dtype) for a in list(arrays)+extra],
        scratch_shapes=scratch,
        compiler_params=pltpu.CompilerParams(collective_id=collective_id,has_side_effects=True,vmem_limit_bytes=60<<20),
        name="weight_sum")(*arrays,*extra)


def from_partner(block, axis, stride):
    count = lax.axis_size(axis)
    route = []
    for low in range(count):
        high = low | 1 << stride
        if high != low and high < count:
            route += [(low, high), (high, low)]
    return lax.ppermute(block, axis, route)


def layer_norm(values, norm_gain, norm_shift):
    center = values - jnp.mean(values, axis=-1, keepdims=True)
    spread = jnp.mean(center * center, axis=-1, keepdims=True)
    return center * lax.rsqrt(spread + EPSILON) * norm_gain + norm_shift


def norm_back(values, norm_gain, norm_shift, upstream):
    unused, pull_back = jax.vjp(layer_norm, values, norm_gain, norm_shift)
    return pull_back(upstream)


def gelu_exact(values):
    return jax.nn.gelu(values, approximate=False)


def gelu_back(values, upstream):
    unused, pull_back = jax.vjp(gelu_exact, values)
    return pull_back(upstream)[0]


def prepare(segment_ids, box_cells, table, is_vision):
    cell = (box_cells[:, 0] * 16 + box_cells[:, 1]).reshape(-1)
    cells = jnp.arange(256)
    e = (cell[:, None] == cells[None]).astype(BF)
    et = (cells[:, None] == cell[None]).astype(BF)
    lane = jnp.arange(128)
    same = segment_ids.reshape(-1)[:, None] == lane[None] - 64
    inside = (lane >= 64) & (lane < 68)
    qseg = same.astype(BF)
    kseg = jnp.where(inside[None] & ~same & jnp.logical_not(is_vision), MASKED, 0.0).astype(BF)
    return e, et, qseg, kseg


def code_onehot():
    c = jnp.arange(65536)
    step_x = jnp.minimum(jnp.abs(c // 4096 - (c // 16) % 16), GRID - 1)
    step_y = jnp.minimum(jnp.abs((c // 256) % 16 - c % 16), GRID - 1)
    return ((step_x * GRID + step_y)[None] == jnp.arange(GRID * GRID)[:, None]).astype(BF)


def on_device(features, cotangent, segment_ids, box_cells, ln_gain, ln_shift, w_qkv, attn_bias,
              distance_table, w_out, w_up, up_bias, w_down, down_bias):
    rows, length, width = features.shape[1:]
    tokens = rows * length
    heads = distance_table.shape[2]
    is_vision = lax.axis_index("stream") != 0
    norm_gains, norm_shifts = ln_gain[0], ln_shift[0]
    bias_rows = attn_bias[0]
    qkv_weight, out_weight, up_weight, down_weight = w_qkv[0], w_out[0], w_up[0], w_down[0]
    plain_in = features[0].reshape(tokens, width).astype(jnp.float32)
    normed = layer_norm(plain_in, norm_gains[0], norm_shifts[0]).astype(BF)
    combined = jnp.dot(normed, qkv_weight, preferred_element_type=jnp.float32)
    queries = (combined[:, :width] + bias_rows[0]).astype(BF) * BF(0.125)
    key_part = combined[:, width:2 * width].astype(BF)
    value_part = (combined[:, 2 * width:] + bias_rows[1]).astype(BF)
    partner_k = from_partner(key_part, "stream", 0)
    partner_v = from_partner(value_part, "stream", 0)
    e, et, qseg, kseg = prepare(segment_ids, box_cells[0], distance_table[0], is_vision)
    onehot = code_onehot()
    bt = jnp.dot(distance_table[0].T.astype(BF), onehot, preferred_element_type=jnp.float32).astype(BF).reshape(heads, 256, 256)
    attended, qmisc = fwd(queries, key_part, partner_k, value_part, partner_v, e, bt, qseg, kseg, length)
    middle = plain_in + jnp.dot(attended, out_weight, preferred_element_type=jnp.float32) + bias_rows[2]
    normed_two = layer_norm(middle, norm_gains[1], norm_shifts[1]).astype(BF)
    pre_act = jnp.dot(normed_two, up_weight, preferred_element_type=jnp.float32) + up_bias[0]
    activated = gelu_exact(pre_act).astype(BF)
    result = middle + jnp.dot(activated, down_weight, preferred_element_type=jnp.float32) + down_bias[0]
    output = result.astype(BF).reshape(1, rows, length, width)
    cot_bf = cotangent[0].reshape(tokens, width)
    cot_f32 = cot_bf.astype(jnp.float32)
    grad_down = jnp.einsum("tf,td->fd", activated, cot_bf, preferred_element_type=jnp.float32).astype(BF)
    grad_down_bias = jnp.sum(cot_f32, axis=0)
    grad_act = jnp.einsum("td,fd->tf", cot_bf, down_weight, preferred_element_type=jnp.float32)
    grad_pre = gelu_back(pre_act, grad_act).astype(BF)
    grad_up = jnp.einsum("td,tf->df", normed_two, grad_pre, preferred_element_type=jnp.float32).astype(BF)
    grad_up_bias = jnp.sum(grad_pre.astype(jnp.float32), axis=0)
    grad_normed_two = jnp.einsum("tf,df->td", grad_pre, up_weight, preferred_element_type=jnp.float32)
    grad_mid_part, gain_two, shift_two = norm_back(middle, norm_gains[1], norm_shifts[1], grad_normed_two)
    grad_middle = cot_f32 + grad_mid_part
    grad_branch = grad_middle.astype(BF)
    grad_out = jnp.einsum("td,te->de", attended, grad_branch, preferred_element_type=jnp.float32).astype(BF)
    grad_out_bias = jnp.sum(grad_branch.astype(jnp.float32), axis=0)
    grad_attended = jnp.einsum("te,de->td", grad_branch, out_weight, preferred_element_type=jnp.float32).astype(BF)
    dq, dkn, dkf, dvn, dvf, g = bwd(queries, key_part, partner_k, value_part, partner_v, grad_attended, attended,
                                    e, et, bt, qmisc, kseg, length)
    back_k = from_partner(dkf, "stream", 0)
    back_v = from_partner(dvf, "stream", 0)
    grad_k = (dkn.astype(jnp.float32) + back_k.astype(jnp.float32)).astype(BF)
    grad_v = (dvn.astype(jnp.float32) + back_v.astype(jnp.float32)).astype(BF)
    grad_dist = jnp.einsum("hp,np->nh", g.reshape(heads, 65536).astype(BF), onehot, preferred_element_type=jnp.float32)
    grad_mixed = jnp.concatenate([dq, grad_k, grad_v], axis=1)
    grad_qkv = jnp.einsum("td,te->de", normed, grad_mixed, preferred_element_type=jnp.float32).astype(BF)
    grad_bias_rows = jnp.stack([jnp.sum(dq.astype(jnp.float32), axis=0), jnp.sum(grad_v.astype(jnp.float32), axis=0), grad_out_bias])
    grad_normed = jnp.einsum("te,de->td", grad_mixed, qkv_weight, preferred_element_type=jnp.float32)
    grad_in_part, gain_one, shift_one = norm_back(plain_in, norm_gains[0], norm_shifts[0], grad_normed)
    input_grad = (grad_middle + grad_in_part).astype(BF).reshape(1, rows, length, width)
    small = [jnp.stack([gain_one, gain_two]), jnp.stack([shift_one, shift_two]), grad_bias_rows, grad_dist, grad_up_bias, grad_down_bias]
    flat = jnp.concatenate([s.reshape(-1) for s in small])
    rows_of = -(-flat.size // 1024) * 8
    flat = jnp.pad(flat, (0, rows_of * 128 - flat.size)).reshape(rows_of, 128)
    sum_up, sum_down, sum_out, sum_qkv, flat = allreduce(
        [grad_up, grad_down, grad_out, grad_qkv], lax.axis_size("batch"), 3, flat)
    flat = flat.reshape(-1)
    parts, at = [], 0
    for s in small:
        parts.append(flat[at:at + s.size].reshape(s.shape)[None])
        at += s.size
    gain, shift, bias, dist, upb, downb = parts
    f32 = lambda a: a.astype(jnp.float32)[None]
    return (output, input_grad, gain, shift, f32(sum_qkv), bias, dist, f32(sum_out), f32(sum_up), upb, f32(sum_down), downb)


def solution(mesh):
    in_specs = (
        P("stream", "batch", None, None),
        P("stream", "batch", None, None),
        P("batch", None),
        P("stream", "batch", None, None),
        P("stream", None, None),
        P("stream", None, None),
        P("stream", None, None),
        P("stream", None, None),
        P("stream", None, None),
        P("stream", None, None),
        P("stream", None, None),
        P("stream", None),
        P("stream", None, None),
        P("stream", None),
    )
    out_specs = (
        P("stream", "batch", None, None),
        P("stream", "batch", None, None),
        P("stream", None, None),
        P("stream", None, None),
        P("stream", None, None),
        P("stream", None, None),
        P("stream", None, None),
        P("stream", None, None),
        P("stream", None, None),
        P("stream", None),
        P("stream", None, None),
        P("stream", None),
    )
    return jax.shard_map(
        on_device, mesh=mesh, in_specs=in_specs, out_specs=out_specs, check_vma=False
    )
```

```python
import functools
import jax
import jax.numpy as jnp
from jax import lax
from jax.experimental import pallas as pl
from jax.experimental.pallas import tpu as pltpu
from jax.sharding import PartitionSpec as P

GRID = 8
EPSILON = 1e-05
MASKED = -1000000000.0

NT=(((1,),(1,)),((),())); NN=(((1,),(0,)),((),())); TN=(((0,),(0,)),((),()))
def mm(a,b,dn=NN): return lax.dot_general(a,b,dn,preferred_element_type=jnp.float32)
BF=jnp.bfloat16

def three(x):
    hi=x.astype(BF); r=x-hi.astype(jnp.float32); mid=r.astype(BF); lo=(r-mid.astype(jnp.float32)).astype(BF)
    return hi,mid,lo

def fwd_kernel(CQ, q_ref,kn_ref,kf_ref,vn_ref,vf_ref,e_ref,b_ref,qseg_ref,kseg_ref,o_ref,qm_ref):
    pair=pl.program_id(1)
    L=q_ref.shape[0]
    lane=lax.broadcasted_iota(jnp.int32,(1,128),1)
    @pl.when(pair==0)
    def _():
        qm_ref[...]=qseg_ref[...]
    outs=[None]*(L//CQ)
    for hh in range(2):
        mh=(lane<64) if hh==0 else (lane>=64)
        h=2*pair+hh
        C=mm(e_ref[...],b_ref[hh]).astype(BF)
        kx=jnp.concatenate([kn_ref[...],C,kseg_ref[...]],axis=1)
        kf=kf_ref[...]
        one=jnp.ones((),BF); zero=jnp.zeros((),BF)
        vnx=jnp.where(mh,vn_ref[...],one); vfx=jnp.where(mh,vf_ref[...],one)
        for c in range(L//CQ):
            sl=slice(c*CQ,(c+1)*CQ)
            qm=jnp.where(mh,q_ref[sl,:],zero)
            qx=jnp.concatenate([qm,e_ref[sl,:],qseg_ref[sl,:]],axis=1)
            sn=mm(qx,kx,NT); sf=mm(qm,kf,NT)
            m=jnp.maximum(jnp.max(sn,axis=1,keepdims=True),jnp.max(sf,axis=1,keepdims=True))
            pn=jnp.exp(sn-m).astype(BF); pf=jnp.exp(sf-m).astype(BF)
            o=mm(pn,vnx)+mm(pf,vfx)
            l=pltpu.roll(o,64,1)
            on=o/l
            outs[c]=on if hh==0 else jnp.where(mh,on,outs[c])
            lse=-(m+jnp.log(jnp.where(mh,l,o)))
            hi,mid,lo=three(lse)
            cur=qm_ref[sl,:]
            cur=jnp.where(lane==3*h,hi,cur); cur=jnp.where(lane==3*h+1,mid,cur); cur=jnp.where(lane==3*h+2,lo,cur)
            qm_ref[sl,:]=cur
    for c in range(L//CQ):
        o_ref[c*CQ:(c+1)*CQ,:]=outs[c].astype(BF)

def fwd(q,kn,kf,vn,vf,e,bt,qseg,kseg,L,CQ=512):
    T=q.shape[0]; R=T//L; NP=q.shape[1]//128
    blk=pl.BlockSpec((L,128),lambda r,p:(r,p))
    row=lambda w: pl.BlockSpec((L,w),lambda r,p:(r,0))
    return pl.pallas_call(functools.partial(fwd_kernel,CQ),grid=(R,NP),
        in_specs=[blk]*5+[row(256),pl.BlockSpec((2,256,256),lambda r,p:(p,0,0)),row(128),row(128)],
        out_specs=[blk,row(128)],
        out_shape=[jax.ShapeDtypeStruct(q.shape,BF),jax.ShapeDtypeStruct((T,128),BF)],
        compiler_params=pltpu.CompilerParams(vmem_limit_bytes=48<<20),name="att_fwd")(q,kn,kf,vn,vf,e,bt,qseg,kseg)


F32=jnp.float32
SIDE=768
WIDE=384
LAG=3

def bit_orders(n, count):
    bits=n.bit_length()-1
    plain=list(range(bits))
    other=[0]+plain[2:]+[1] if bits>2 else plain
    return [other if c%5==3 else plain for c in range(count)]

def plan_of(n, order, rows):
    sizes=[rows]
    for _ in order:
        m=sizes[-1]
        sizes.append(m//2 if m%32==0 else m)
    return sizes

def place(me, b):
    bit=(me//(1<<b))%2
    return bit, me+(1-2*bit)*(1<<b)

class Engine:
    def __init__(self, n, orders, x, y, recv, send_sem, recv_sem, me):
        self.n, self.orders, self.x, self.y, self.recv = n, orders, x, y, recv
        self.offs = recv_offsets(n, orders)
        self.ss, self.rs, self.me = send_sem, recv_sem, me
        self.bits = n.bit_length() - 1

    def seg(self, c, upto):
        sizes = plan_of(self.n, self.orders[c], SIDE)
        off = 0
        for s in range(upto):
            if sizes[s + 1] != sizes[s]:
                off = off + place(self.me, self.orders[c][s])[0] * sizes[s + 1]
        return off, sizes[upto]

    def ds(self, off, size):
        return pl.ds(off if isinstance(off, int) else pl.multiple_of(off, 16), size)

    def copy(self, c, stage):
        B, order = self.bits, self.orders[c]
        sizes = plan_of(self.n, order, SIDE)
        if stage < B:
            bit, partner = place(self.me, order[stage])
            off, m = self.seg(c, stage)
            if sizes[stage + 1] != m:
                src = self.x.at[c, self.ds(off + (1 - bit) * (m // 2), m // 2)]
            else:
                src = self.x.at[c, self.ds(off, m)]
            dst = self.recv.at[c, pl.ds(self.offs[c][stage], sizes[stage + 1])]
        else:
            s = 2 * B - 1 - stage
            if sizes[s + 1] == sizes[s]:
                return None
            partner = place(self.me, order[s])[1]
            off, m = self.seg(c, s + 1)
            src = self.y.at[c, self.ds(off, m)]
            dst = src
        return pltpu.make_async_remote_copy(
            src, dst, self.ss.at[c, stage], self.rs.at[c, stage],
            device_id={"batch": partner}, device_id_type=pl.DeviceIdType.MESH)

    def start(self, c, stage):
        d = self.copy(c, stage)
        if d is not None:
            d.start()

    def finish(self, c, stage):
        d = self.copy(c, stage)
        if d is not None:
            d.wait()
        if stage < self.bits:
            off, m = self.seg(c, stage + 1)
            ro = self.offs[c][stage]
            x, recv = self.x, self.recv
            to = self.y if stage == self.bits - 1 else x

            def body(i, _):
                at = self.ds(off + i * 48, 48)
                other = recv[c, pl.ds(pl.multiple_of(ro + i * 48, 16), 48)]
                to[c, at] = (x[c, at].astype(F32) + other.astype(F32)).astype(BF)
                return 0

            lax.fori_loop(0, m // 48, body, 0)

    def slot(self, t, load, store, count):
        for s in range(2 * self.bits, -1, -1):
            c = t - LAG * s
            if not 0 <= c < count:
                continue
            if s == 0:
                load(c)
            else:
                self.finish(c, s - 1)
            if s < 2 * self.bits:
                self.start(c, s)
            else:
                store(c)

    def slots(self, count):
        return count + LAG * 2 * self.bits


def recv_offsets(n, orders):
    res=[]
    for o in orders:
        sizes=plan_of(n,o,SIDE); at=[0]
        for s in range(len(o)): at.append(at[-1]+sizes[s+1])
        res.append(at)
    return res

def barrier(n, me):
    sem=pltpu.get_barrier_semaphore()
    bits=n.bit_length()-1
    for b in range(bits):
        pl.semaphore_signal(sem,inc=1,device_id={"batch":place(me,b)[1]},device_id_type=pl.DeviceIdType.MESH)
    pl.semaphore_wait(sem,bits)

def ar_kernel(n, layout, with_small, *refs):
    na=max(a for a,_,_ in layout)+1
    ins=refs[:na]; refs=refs[na:]
    if with_small: small_in,refs=refs[0],refs[1:]
    outs=refs[:na]; refs=refs[na:]
    if with_small: small_out,refs=refs[0],refs[1:]
    x,y,recv,in_sem,out_sem,ss,rs=refs[:7]
    C=len(layout)
    me=lax.axis_index("batch")
    orders=bit_orders(n,C)
    def view(ref,a,r,c): return ref.at[pl.ds(r*SIDE,SIDE),pl.ds(c*WIDE,WIDE)]
    loads=[]
    for c,(a,r,k) in enumerate(layout):
        d=pltpu.make_async_copy(view(ins[a],a,r,k),x.at[c],in_sem.at[c]); d.start(); loads.append(d)
    barrier(n,me)
    eng=Engine(n,orders,x,y,recv,ss,rs,me)
    B=eng.bits
    if with_small:
        small_x,small_recv,small_sem,small_ss,small_rs=refs[7:12]
        d=pltpu.make_async_copy(small_in,small_x.at[0],small_sem); d.start(); d.wait()
    def small_copy(s):
        return pltpu.make_async_remote_copy(small_x.at[s],small_recv.at[s],small_ss.at[s],small_rs.at[s],
            device_id={"batch":place(me,s)[1]},device_id_type=pl.DeviceIdType.MESH)
    small_d=None
    stores={}
    def put(c):
        a,r,k=layout[c]
        stores[c]=pltpu.make_async_copy(y.at[c],view(outs[a],a,r,k),out_sem.at[c]); stores[c].start()
    for t in range(C+LAG*2*B):
        if with_small and t%LAG==0 and t//LAG<=B:
            i=t//LAG
            if i>0:
                small_d.wait()
                small_x[i]=small_x[i-1]+small_recv[i-1]
            if i<B:
                small_d=small_copy(i); small_d.start()
            else:
                small_d=pltpu.make_async_copy(small_x.at[i],small_out,small_sem); small_d.start()
        eng.slot(t,lambda c: loads[c].wait(),put,C)
    for c in range(C): stores[c].wait()
    if with_small: small_d.wait()

def allreduce(arrays, n, collective_id, small=None):
    layout=[]
    for a,arr in enumerate(arrays):
        for r in range(arr.shape[0]//SIDE):
            for k in range(arr.shape[1]//WIDE): layout.append((a,r,k))
    C=len(layout); bits=n.bit_length()-1
    rows=max(o[-1] for o in recv_offsets(n,bit_orders(n,C)))
    scratch=[pltpu.VMEM((C,SIDE,WIDE),BF),pltpu.VMEM((C,SIDE,WIDE),BF),pltpu.VMEM((C,rows,WIDE),BF),
            pltpu.SemaphoreType.DMA((C,)),pltpu.SemaphoreType.DMA((C,)),pltpu.SemaphoreType.DMA((C,2*bits)),pltpu.SemaphoreType.DMA((C,2*bits))]
    extra=[]
    if small is not None:
        extra=[small]
        scratch+=[pltpu.VMEM((bits+1,)+small.shape,F32),pltpu.VMEM((bits,)+small.shape,F32),pltpu.SemaphoreType.DMA,
            pltpu.SemaphoreType.DMA((bits,)),pltpu.SemaphoreType.DMA((bits,))]
    return pl.pallas_call(functools.partial(ar_kernel,n,layout,small is not None),
        in_specs=[pl.BlockSpec(memory_space=pl.ANY)]*(len(arrays)+len(extra)),
        out_specs=[pl.BlockSpec(memory_space=pl.ANY)]*(len(arrays)+len(extra)),
        out_shape=[jax.ShapeDtypeStruct(a.shape,a.dtype) for a in list(arrays)+extra],
        scratch_shapes=scratch,
        compiler_params=pltpu.CompilerParams(collective_id=collective_id,has_side_effects=True,vmem_limit_bytes=60<<20),
        name="weight_sum")(*arrays,*extra)


def gelu_both(u):
    a=jnp.abs(u)
    t=1.0/(1.0+a*(0.3275911*0.7071067811865476))
    ex=jnp.exp(u*u*-0.5)
    poly=((((1.061405429*t-1.453152027)*t+1.421413741)*t-0.284496736)*t+0.254829592)*t
    half=0.5*poly*ex
    cdf=jnp.where(u<0,half,1.0-half)
    return u*cdf, cdf+u*ex*0.3989422804014327

def norm_parts(v):
    center=v-jnp.mean(v,axis=1,keepdims=True)
    inv=lax.rsqrt(jnp.mean(center*center,axis=1,keepdims=True)+EPSILON)
    return center*inv,inv

def colsum(v): return jnp.sum(v,axis=0,keepdims=True)

def mid_kernel(RC, x_ref,cot_ref,att_ref,wo_ref,vec_ref,wu_ref,wd_ref,ub_ref,
               out_ref,gm_ref,do_ref,dm_ref,gwo_ref,gwu_ref,gwd_ref,gub_ref,small_ref,
               mid_s,nt_s,ntt_s,acc_s,gn_s):
    j=pl.program_id(0); T=x_ref.shape[0]; NTL=pl.num_programs(0)
    chunks=[slice(i*RC,(i+1)*RC) for i in range(T//RC)]
    @pl.when(j==0)
    def _():
        for sl in chunks:
            v=x_ref[sl,:].astype(F32)+mm(att_ref[sl,:],wo_ref[...])+vec_ref[0:1,:]
            mid_s[sl,:]=v
            n,_=norm_parts(v)
            nt=(n*vec_ref[1:2,:]+vec_ref[2:3,:]).astype(BF)
            nt_s[sl,:]=nt
            ntt_s[:,sl]=nt.T
            acc_s[sl,:]=v+vec_ref[3:4,:]
            gn_s[sl,:]=jnp.zeros_like(v)
    gub=0.0; gwd=0.0; gwu=0.0
    for sl in chunks:
        pre=mm(nt_s[sl,:],wu_ref[...])+ub_ref[...]
        act,slope=gelu_both(pre)
        act=act.astype(BF)
        gp=(mm(cot_ref[sl,:],wd_ref[...],NT)*slope).astype(BF)
        acc_s[sl,:]+=mm(act,wd_ref[...])
        gn_s[sl,:]+=mm(gp,wu_ref[...],NT)
        gub=gub+colsum(gp.astype(F32))
        gwd=gwd+mm(act,cot_ref[sl,:],TN)
        gwu=gwu+mm(ntt_s[:,sl],gp)
    gub_ref[...]=gub
    gwd_ref[...]=gwd.astype(BF); gwu_ref[...]=gwu.astype(BF)
    @pl.when(j==NTL-1)
    def _():
        g2=0.0; s2=0.0; ob=0.0; db=0.0; gwo=0.0
        row=lax.broadcasted_iota(jnp.int32,(x_ref.shape[1],128),0)//64
        col=lax.broadcasted_iota(jnp.int32,(x_ref.shape[1],128),1)
        pick=(row==col//3).astype(BF)
        lane=lax.broadcasted_iota(jnp.int32,(1,128),1)
        for sl in chunks:
            out_ref[sl,:]=acc_s[sl,:].astype(BF)
            n,inv=norm_parts(mid_s[sl,:])
            q=gn_s[sl,:]
            g2=g2+colsum(q*n); s2=s2+colsum(q)
            qg=q*vec_ref[1:2,:]
            cot=cot_ref[sl,:].astype(F32)
            db=db+colsum(cot)
            gm=cot+(qg-jnp.mean(qg,axis=1,keepdims=True)-n*jnp.mean(qg*n,axis=1,keepdims=True))*inv
            gm_ref[sl,:]=gm
            gb=gm.astype(BF)
            ob=ob+colsum(gb.astype(F32))
            do=mm(gb,wo_ref[...],NT).astype(BF)
            do_ref[sl,:]=do
            gwo=gwo+mm(att_ref[sl,:],gb,TN)
            prod=do.astype(F32)*att_ref[sl,:].astype(F32)
            hi=prod.astype(BF); lo=(prod-hi.astype(F32)).astype(BF)
            delta=-(mm(hi,pick)+mm(lo,pick))
            hi,md,lo=three(delta)
            dm_ref[sl,:]=jnp.where(lane>=36,jnp.zeros((),BF),jnp.where(lane%3==0,hi,jnp.where(lane%3==1,md,lo)))
        gwo_ref[...]=gwo.astype(BF)
        small_ref[0:1,:]=g2; small_ref[1:2,:]=s2; small_ref[2:3,:]=ob; small_ref[3:4,:]=db
        small_ref[4:8,:]=jnp.zeros((4,x_ref.shape[1]),F32)

def mid(x,cot,att,wo,vec,wu,wd,ub,FT=512,RC=256):
    T,D=x.shape; FF=wu.shape[1]
    full=lambda a: pl.BlockSpec(a.shape,lambda j:(0,0))
    S=jax.ShapeDtypeStruct
    fs=lambda *s: pl.BlockSpec(s,lambda j:(0,0))
    return pl.pallas_call(functools.partial(mid_kernel,RC),grid=(FF//FT,),
        in_specs=[full(x),full(cot),full(att),full(wo),full(vec),pl.BlockSpec((D,FT),lambda j:(0,j)),pl.BlockSpec((FT,D),lambda j:(j,0)),pl.BlockSpec((1,FT),lambda j:(0,j))],
        out_specs=[fs(T,D),fs(T,D),fs(T,D),fs(T,128),fs(D,D),pl.BlockSpec((D,FT),lambda j:(0,j)),pl.BlockSpec((FT,D),lambda j:(j,0)),pl.BlockSpec((1,FT),lambda j:(0,j)),fs(8,D)],
        out_shape=[S((T,D),BF),S((T,D),F32),S((T,D),BF),S((T,128),BF),S((D,D),BF),S((D,FF),BF),S((FF,D),BF),S((1,FF),F32),S((8,D),F32)],
        scratch_shapes=[pltpu.VMEM((T,D),F32),pltpu.VMEM((T,D),BF),pltpu.VMEM((D,T),BF),pltpu.VMEM((T,D),F32),pltpu.VMEM((T,D),F32)],
        compiler_params=pltpu.CompilerParams(vmem_limit_bytes=60<<20),name="feed_forward")(x,cot,att,wo,vec,wu,wd,ub)


MESH=pl.DeviceIdType.MESH
TICKS=2

def bwd_kernel(n, NP, R, layout, first_tick,
               q_ref,kn_ref,kf_ref,vn_ref,vf_ref,do_ref,dm_ref,qm_ref,e_ref,et_ref,b_ref,kseg_ref,qf_ref,qmf_ref,
               do_any,dm_any,gu_any,gd_any,go_any,
               dq_ref,dk_ref,dv_ref,g_ref,su_any,sd_any,so_any,
               dof,dmf,dk_acc,dv_acc,x,y,recv,in_sem,out_sem,ss,rs,xs_sem,xr_sem):
    step=pl.program_id(0)
    per=NP*R
    second=step>=per
    inner=step%per; pair=inner//R; r=inner%R
    L=q_ref.shape[0]
    steps=2*per
    me=lax.axis_index("batch"); other={"stream":1-lax.axis_index("stream")}
    lane=lax.broadcasted_iota(jnp.int32,(1,128),1)
    zero=jnp.zeros((),BF)
    C=len(layout)
    grads=(gu_any,gd_any,go_any); sums=(su_any,sd_any,so_any)
    def view(ref,i,k): return ref.at[pl.ds(i*SIDE,SIDE),pl.ds(k*WIDE,WIDE)]
    def load(c):
        a,i,k=layout[c]
        return pltpu.make_async_copy(view(grads[a],i,k),x.at[c],in_sem.at[c])
    def store(c):
        a,i,k=layout[c]
        return pltpu.make_async_copy(y.at[c],view(sums[a],i,k),out_sem.at[c])
    def across():
        res=[pltpu.make_async_remote_copy(dm_any,dmf,xs_sem.at[NP],xr_sem.at[NP],device_id=other,device_id_type=MESH)]
        for p in range(NP):
            res.append(pltpu.make_async_remote_copy(do_any.at[:,pl.ds(p*128,128)],dof.at[p],xs_sem.at[p],xr_sem.at[p],device_id=other,device_id_type=MESH))
        return res
    eng=Engine(n,bit_orders(n,C),x,y,recv,ss,rs,me)

    @pl.when(step==0)
    def _():
        sem=pltpu.get_barrier_semaphore()
        for b in range(eng.bits):
            pl.semaphore_signal(sem,inc=1,device_id={"batch":place(me,b)[1]},device_id_type=MESH)
        pl.semaphore_signal(sem,inc=1,device_id=other,device_id_type=MESH)
        for c in range(C): load(c).start()
        pl.semaphore_wait(sem,eng.bits+1)
        for d in across(): d.start()
    total=eng.slots(C)
    ticks=TICKS*steps
    edges=[total*i//(ticks-first_tick) for i in range(ticks-first_tick+1)]
    def tick(half):
        for k in range(steps):
            i=k*TICKS+half-first_tick
            if i<0 or edges[i]==edges[i+1]: continue
            @pl.when(step==k)
            def _():
                for t in range(edges[i],edges[i+1]):
                    eng.slot(t,lambda c: load(c).wait(),lambda c: store(c).start(),C)
    def half_of(hh):
        return (lane<64) if hh==0 else (lane>=64)
    def ones_of(h):
        return jnp.where((lane>=3*h)&(lane<3*h+3),1.0,0.0)
    add=lambda a,b: b if a is None else a+b

    tick(0)
    @pl.when(jnp.logical_not(second))
    def _():
        dkn=None; dvn=None; dq=None
        for hh in range(2):
            mh=half_of(hh); h=2*pair+hh
            ones_h=ones_of(h); ones_b=jnp.broadcast_to(ones_h.astype(BF),(L,128))
            qm=jnp.where(mh,q_ref[...],zero); dom=jnp.where(mh,do_ref[...],zero)
            C_h=mm(e_ref[...],b_ref[hh]).astype(BF)
            qx=jnp.concatenate([qm,e_ref[...],qm_ref[...]],axis=1)
            dox=jnp.concatenate([dom,dm_ref[...]],axis=1)
            kseg=(kseg_ref[...].astype(F32)+ones_h).astype(BF)
            p=jnp.exp(mm(jnp.concatenate([kn_ref[...],C_h,kseg],axis=1),qx,NT))
            ds=(p*mm(jnp.concatenate([vn_ref[...],ones_b],axis=1),dox,NT)).astype(BF)
            dvn=add(dvn,mm(p.astype(BF),dom))
            t=mm(ds,jnp.concatenate([qm,e_ref[...]],axis=1))
            dkn=add(dkn,t[:,:128])
            g=mm(et_ref[...],t[:,128:].astype(BF))
            dq=add(dq,mm(ds,jnp.where(mh,kn_ref[...],zero),TN))
            p=jnp.exp(mm(jnp.concatenate([kf_ref[...],ones_b],axis=1),jnp.concatenate([qm,qm_ref[...]],axis=1),NT))
            ds=(p*mm(jnp.concatenate([vf_ref[...],ones_b],axis=1),dox,NT)).astype(BF)
            dq=add(dq,mm(ds,jnp.where(mh,kf_ref[...],zero),TN))
            @pl.when(r==0)
            def _(): g_ref[hh]=g
            @pl.when(r!=0)
            def _(): g_ref[hh]+=g
        dq_ref[...]=(dq*0.125).astype(BF)
        dk_acc[inner]=dkn; dv_acc[inner]=dvn
    tick(1)
    @pl.when(step==per)
    def _():
        for d in across(): d.wait_recv()
    @pl.when(second)
    def _():
        dk=dk_acc[inner]; dv=dv_acc[inner]
        at=pl.ds(pl.multiple_of(r*L,L),L)
        for hh in range(2):
            mh=half_of(hh); h=2*pair+hh
            ones_b=jnp.broadcast_to(ones_of(h).astype(BF),(L,128))
            qm=jnp.where(mh,qf_ref[...],zero); dom=jnp.where(mh,dof[pair,at],zero)
            p=jnp.exp(mm(jnp.concatenate([kn_ref[...],ones_b],axis=1),jnp.concatenate([qm,qmf_ref[...]],axis=1),NT))
            ds=(p*mm(jnp.concatenate([vn_ref[...],ones_b],axis=1),jnp.concatenate([dom,dmf[at]],axis=1),NT)).astype(BF)
            dv=dv+mm(p.astype(BF),dom)
            dk=dk+mm(ds,qm)
        dk_ref[...]=dk.astype(BF); dv_ref[...]=dv.astype(BF)
    @pl.when(step==steps-1)
    def _():
        for c in range(C): store(c).wait()
        for d in across(): d.wait_send()

def bwd(q,kn,kf,vn,vf,do,dm,qmisc,e,et,bt,kseg,qf,qmf,grads,L,n,collective_id,first_tick=0):
    T=q.shape[0]; R=T//L; NP=q.shape[1]//128; per=R*NP
    def one(step): i=jnp.minimum(step,per-1); return i%R,i//R
    def cyc(step): i=step%per; return i%R,i//R
    def two(step): i=jnp.maximum(step-per,0); return i%R,i//R
    blk=lambda f: pl.BlockSpec((L,128),f)
    row=lambda w,f: pl.BlockSpec((L,w),lambda s:(f(s)[0],0))
    any_=pl.BlockSpec(memory_space=pl.ANY)
    layout=[]
    for a,arr in enumerate(grads):
        for i in range(arr.shape[0]//SIDE):
            for k in range(arr.shape[1]//WIDE): layout.append((a,i,k))
    C=len(layout); bits=n.bit_length()-1
    rows=max(o[-1] for o in recv_offsets(n,bit_orders(n,C)))
    S=jax.ShapeDtypeStruct; sem=pltpu.SemaphoreType.DMA
    gspec=pl.BlockSpec((2,256,256),lambda s:(one(s)[1],0,0))
    return pl.pallas_call(functools.partial(bwd_kernel,n,NP,R,layout,first_tick),grid=(2*per,),
        in_specs=[blk(one),blk(cyc),blk(one),blk(cyc),blk(one),blk(one),row(128,one),row(128,one),row(256,one),
                  pl.BlockSpec((256,L),lambda s:(0,one(s)[0])),gspec,row(128,one),blk(two),row(128,two)]+[any_]*5,
        out_specs=[blk(one),blk(two),blk(two),gspec]+[any_]*3,
        out_shape=[S(q.shape,BF)]*3+[S((2*NP,256,256),F32)]+[S(a.shape,BF) for a in grads],
        scratch_shapes=[pltpu.VMEM((NP,T,128),BF),pltpu.VMEM((T,128),BF),pltpu.VMEM((per,L,128),F32),pltpu.VMEM((per,L,128),F32),
            pltpu.VMEM((C,SIDE,WIDE),BF),pltpu.VMEM((C,SIDE,WIDE),BF),pltpu.VMEM((C,rows,WIDE),BF),
            sem((C,)),sem((C,)),sem((C,2*bits)),sem((C,2*bits)),sem((NP+1,)),sem((NP+1,))],
        compiler_params=pltpu.CompilerParams(collective_id=collective_id,has_side_effects=True,vmem_limit_bytes=62<<20),
        name="att_bwd")(q,kn,kf,vn,vf,do,dm,qmisc,e,et,bt,kseg,qf,qmf,do,dm,*grads)


def from_partner(block, axis, stride):
    count = lax.axis_size(axis)
    route = []
    for low in range(count):
        high = low | 1 << stride
        if high != low and high < count:
            route += [(low, high), (high, low)]
    return lax.ppermute(block, axis, route)


def layer_norm(values, norm_gain, norm_shift):
    center = values - jnp.mean(values, axis=-1, keepdims=True)
    spread = jnp.mean(center * center, axis=-1, keepdims=True)
    return center * lax.rsqrt(spread + EPSILON) * norm_gain + norm_shift


def norm_back(values, norm_gain, norm_shift, upstream):
    unused, pull_back = jax.vjp(layer_norm, values, norm_gain, norm_shift)
    return pull_back(upstream)


def gelu_exact(values):
    return jax.nn.gelu(values, approximate=False)


def gelu_back(values, upstream):
    unused, pull_back = jax.vjp(gelu_exact, values)
    return pull_back(upstream)[0]


def prepare(segment_ids, box_cells, table, is_vision):
    cell = (box_cells[:, 0] * 16 + box_cells[:, 1]).reshape(-1)
    cells = jnp.arange(256)
    e = (cell[:, None] == cells[None]).astype(BF)
    et = (cells[:, None] == cell[None]).astype(BF)
    lane = jnp.arange(128)
    same = segment_ids.reshape(-1)[:, None] == lane[None] - 64
    inside = (lane >= 64) & (lane < 68)
    qseg = same.astype(BF)
    kseg = jnp.where(inside[None] & ~same & jnp.logical_not(is_vision), MASKED, 0.0).astype(BF)
    return e, et, qseg, kseg


def code_onehot():
    c = jnp.arange(65536)
    step_x = jnp.minimum(jnp.abs(c // 4096 - (c // 16) % 16), GRID - 1)
    step_y = jnp.minimum(jnp.abs((c // 256) % 16 - c % 16), GRID - 1)
    return ((step_x * GRID + step_y)[None] == jnp.arange(GRID * GRID)[:, None]).astype(BF)


def on_device(features, cotangent, segment_ids, box_cells, ln_gain, ln_shift, w_qkv, attn_bias,
              distance_table, w_out, w_up, up_bias, w_down, down_bias):
    rows, length, width = features.shape[1:]
    tokens = rows * length
    heads = distance_table.shape[2]
    is_vision = lax.axis_index("stream") != 0
    norm_gains, norm_shifts = ln_gain[0], ln_shift[0]
    bias_rows = attn_bias[0]
    qkv_weight, out_weight, up_weight, down_weight = w_qkv[0], w_out[0], w_up[0], w_down[0]
    plain_in = features[0].reshape(tokens, width).astype(jnp.float32)
    normed = layer_norm(plain_in, norm_gains[0], norm_shifts[0]).astype(BF)
    combined = jnp.dot(normed, qkv_weight, preferred_element_type=jnp.float32)
    queries = (combined[:, :width] + bias_rows[0]).astype(BF) * BF(0.125)
    key_part = combined[:, width:2 * width].astype(BF)
    value_part = (combined[:, 2 * width:] + bias_rows[1]).astype(BF)
    partner_k = from_partner(key_part, "stream", 0)
    partner_v = from_partner(value_part, "stream", 0)
    e, et, qseg, kseg = prepare(segment_ids, box_cells[0], distance_table[0], is_vision)
    onehot = code_onehot()
    bt = jnp.dot(distance_table[0].T.astype(BF), onehot, preferred_element_type=jnp.float32).astype(BF).reshape(heads, 256, 256)
    attended, qmisc = fwd(queries, key_part, partner_k, value_part, partner_v, e, bt, qseg, kseg, length)
    vec = jnp.concatenate([bias_rows[2:3], norm_gains[1:2], norm_shifts[1:2], down_bias, jnp.zeros((4, width), F32)])
    q_send, m_send = lax.optimization_barrier((queries, qmisc))
    partner_q = from_partner(q_send, "stream", 0)
    partner_m = from_partner(m_send, "stream", 0)
    (output, grad_middle, grad_attended, dmisc, grad_out, grad_up, grad_down, grad_up_bias, small_mid) = mid(
        features[0].reshape(tokens, width), cotangent[0].reshape(tokens, width), attended, out_weight, vec,
        up_weight, down_weight, up_bias)
    output = output.reshape(1, rows, length, width)
    dq, grad_k, grad_v, g, sum_up, sum_down, sum_out = bwd(
        queries, key_part, partner_k, value_part, partner_v, grad_attended, dmisc, qmisc, e, et, bt, kseg,
        partner_q, partner_m, [grad_up, grad_down, grad_out], length, lax.axis_size("batch"), 4)
    grad_dist = jnp.einsum("hp,np->nh", g.reshape(heads, 65536).astype(BF), onehot, preferred_element_type=jnp.float32)
    grad_mixed = jnp.concatenate([dq, grad_k, grad_v], axis=1)
    grad_qkv = jnp.einsum("td,te->de", normed, grad_mixed, preferred_element_type=jnp.float32).astype(BF)
    grad_bias_rows = jnp.stack([jnp.sum(dq.astype(jnp.float32), axis=0), jnp.sum(grad_v.astype(jnp.float32), axis=0), small_mid[2]])
    grad_normed = jnp.einsum("te,de->td", grad_mixed, qkv_weight, preferred_element_type=jnp.float32)
    grad_in_part, gain_one, shift_one = norm_back(plain_in, norm_gains[0], norm_shifts[0], grad_normed)
    input_grad = (grad_middle + grad_in_part).astype(BF).reshape(1, rows, length, width)
    small = [jnp.stack([gain_one, small_mid[0]]), jnp.stack([shift_one, small_mid[1]]), grad_bias_rows, grad_dist, grad_up_bias[0], small_mid[3]]
    flat = jnp.concatenate([s.reshape(-1) for s in small])
    rows_of = -(-flat.size // 1024) * 8
    flat = jnp.pad(flat, (0, rows_of * 128 - flat.size)).reshape(rows_of, 128)
    sum_qkv, flat = allreduce(
        [grad_qkv], lax.axis_size("batch"), 3, flat)
    flat = flat.reshape(-1)
    parts, at = [], 0
    for s in small:
        parts.append(flat[at:at + s.size].reshape(s.shape)[None])
        at += s.size
    gain, shift, bias, dist, upb, downb = parts
    f32 = lambda a: a.astype(jnp.float32)[None]
    return (output, input_grad, gain, shift, f32(sum_qkv), bias, dist, f32(sum_out), f32(sum_up), upb, f32(sum_down), downb)


def solution(mesh):
    in_specs = (
        P("stream", "batch", None, None),
        P("stream", "batch", None, None),
        P("batch", None),
        P("stream", "batch", None, None),
        P("stream", None, None),
        P("stream", None, None),
        P("stream", None, None),
        P("stream", None, None),
        P("stream", None, None),
        P("stream", None, None),
        P("stream", None, None),
        P("stream", None),
        P("stream", None, None),
        P("stream", None),
    )
    out_specs = (
        P("stream", "batch", None, None),
        P("stream", "batch", None, None),
        P("stream", None, None),
        P("stream", None, None),
        P("stream", None, None),
        P("stream", None, None),
        P("stream", None, None),
        P("stream", None, None),
        P("stream", None, None),
        P("stream", None),
        P("stream", None, None),
        P("stream", None),
    )
    return jax.shard_map(
        on_device, mesh=mesh, in_specs=in_specs, out_specs=out_specs, check_vma=False
    )
```

```python
import functools
import jax
import jax.numpy as jnp
from jax import lax
from jax.experimental import pallas as pl
from jax.experimental.pallas import tpu as pltpu
from jax.sharding import PartitionSpec as P

GRID = 8
EPSILON = 1e-05
MASKED = -1000000000.0

NT=(((1,),(1,)),((),())); NN=(((1,),(0,)),((),())); TN=(((0,),(0,)),((),()))
def mm(a,b,dn=NN): return lax.dot_general(a,b,dn,preferred_element_type=jnp.float32)
BF=jnp.bfloat16

def three(x):
    hi=x.astype(BF); r=x-hi.astype(jnp.float32); mid=r.astype(BF); lo=(r-mid.astype(jnp.float32)).astype(BF)
    return hi,mid,lo

def fwd_kernel(CQ, q_ref,kn_ref,kf_ref,vn_ref,vf_ref,e_ref,b_ref,qseg_ref,kseg_ref,o_ref,qm_ref):
    pair=pl.program_id(1)
    L=q_ref.shape[0]
    lane=lax.broadcasted_iota(jnp.int32,(1,128),1)
    @pl.when(pair==0)
    def _():
        qm_ref[...]=qseg_ref[...]
    outs=[None]*(L//CQ)
    for hh in range(2):
        mh=(lane<64) if hh==0 else (lane>=64)
        h=2*pair+hh
        C=mm(e_ref[...],b_ref[hh]).astype(BF)
        kx=jnp.concatenate([kn_ref[...],C,kseg_ref[...]],axis=1)
        kf=kf_ref[...]
        one=jnp.ones((),BF); zero=jnp.zeros((),BF)
        vnx=jnp.where(mh,vn_ref[...],one); vfx=jnp.where(mh,vf_ref[...],one)
        for c in range(L//CQ):
            sl=slice(c*CQ,(c+1)*CQ)
            qm=jnp.where(mh,q_ref[sl,:],zero)
            qx=jnp.concatenate([qm,e_ref[sl,:],qseg_ref[sl,:]],axis=1)
            sn=mm(qx,kx,NT); sf=mm(qm,kf,NT)
            m=jnp.maximum(jnp.max(sn,axis=1,keepdims=True),jnp.max(sf,axis=1,keepdims=True))
            pn=jnp.exp(sn-m).astype(BF); pf=jnp.exp(sf-m).astype(BF)
            o=mm(pn,vnx)+mm(pf,vfx)
            l=pltpu.roll(o,64,1)
            on=o/l
            outs[c]=on if hh==0 else jnp.where(mh,on,outs[c])
            lse=-(m+jnp.log(jnp.where(mh,l,o)))
            hi,mid,lo=three(lse)
            cur=qm_ref[sl,:]
            cur=jnp.where(lane==3*h,hi,cur); cur=jnp.where(lane==3*h+1,mid,cur); cur=jnp.where(lane==3*h+2,lo,cur)
            qm_ref[sl,:]=cur
    for c in range(L//CQ):
        o_ref[c*CQ:(c+1)*CQ,:]=outs[c].astype(BF)

def fwd(q,kn,kf,vn,vf,e,bt,qseg,kseg,L,CQ=512):
    T=q.shape[0]; R=T//L; NP=q.shape[1]//128
    blk=pl.BlockSpec((L,128),lambda r,p:(r,p))
    row=lambda w: pl.BlockSpec((L,w),lambda r,p:(r,0))
    return pl.pallas_call(functools.partial(fwd_kernel,CQ),grid=(R,NP),
        in_specs=[blk]*5+[row(256),pl.BlockSpec((2,256,256),lambda r,p:(p,0,0)),row(128),row(128)],
        out_specs=[blk,row(128)],
        out_shape=[jax.ShapeDtypeStruct(q.shape,BF),jax.ShapeDtypeStruct((T,128),BF)],
        compiler_params=pltpu.CompilerParams(vmem_limit_bytes=48<<20),name="att_fwd")(q,kn,kf,vn,vf,e,bt,qseg,kseg)


F32=jnp.float32


def gelu_both(u):
    a=jnp.abs(u)
    t=1.0/(1.0+a*(0.3275911*0.7071067811865476))
    ex=jnp.exp(u*u*-0.5)
    poly=((((1.061405429*t-1.453152027)*t+1.421413741)*t-0.284496736)*t+0.254829592)*t
    half=0.5*poly*ex
    cdf=jnp.where(u<0,half,1.0-half)
    return u*cdf, cdf+u*ex*0.3989422804014327

def norm_parts(v):
    center=v-jnp.mean(v,axis=1,keepdims=True)
    inv=lax.rsqrt(jnp.mean(center*center,axis=1,keepdims=True)+EPSILON)
    return center*inv,inv

def colsum(v): return jnp.sum(v,axis=0,keepdims=True)

def mid_kernel(RC, x_ref,cot_ref,att_ref,wo_ref,vec_ref,wu_ref,wd_ref,ub_ref,
               out_ref,gm_ref,do_ref,dm_ref,gwo_ref,gwu_ref,gwd_ref,gub_ref,small_ref,
               mid_s,nt_s,ntt_s,acc_s,gn_s):
    j=pl.program_id(0); T=x_ref.shape[0]; NTL=pl.num_programs(0)
    chunks=[slice(i*RC,(i+1)*RC) for i in range(T//RC)]
    @pl.when(j==0)
    def _():
        for sl in chunks:
            v=x_ref[sl,:].astype(F32)+mm(att_ref[sl,:],wo_ref[...])+vec_ref[0:1,:]
            mid_s[sl,:]=v
            n,_=norm_parts(v)
            nt=(n*vec_ref[1:2,:]+vec_ref[2:3,:]).astype(BF)
            nt_s[sl,:]=nt
            ntt_s[:,sl]=nt.T
            acc_s[sl,:]=v+vec_ref[3:4,:]
            gn_s[sl,:]=jnp.zeros_like(v)
    gub=0.0; gwd=0.0; gwu=0.0
    for sl in chunks:
        pre=mm(nt_s[sl,:],wu_ref[...])+ub_ref[...]
        act,slope=gelu_both(pre)
        act=act.astype(BF)
        gp=(mm(cot_ref[sl,:],wd_ref[...],NT)*slope).astype(BF)
        acc_s[sl,:]+=mm(act,wd_ref[...])
        gn_s[sl,:]+=mm(gp,wu_ref[...],NT)
        gub=gub+colsum(gp.astype(F32))
        gwd=gwd+mm(act,cot_ref[sl,:],TN)
        gwu=gwu+mm(ntt_s[:,sl],gp)
    gub_ref[...]=gub
    gwd_ref[...]=gwd.astype(BF); gwu_ref[...]=gwu.astype(BF)
    @pl.when(j==NTL-1)
    def _():
        g2=0.0; s2=0.0; ob=0.0; db=0.0; gwo=0.0
        row=lax.broadcasted_iota(jnp.int32,(x_ref.shape[1],128),0)//64
        col=lax.broadcasted_iota(jnp.int32,(x_ref.shape[1],128),1)
        pick=(row==col//3).astype(BF)
        lane=lax.broadcasted_iota(jnp.int32,(1,128),1)
        for sl in chunks:
            out_ref[sl,:]=acc_s[sl,:].astype(BF)
            n,inv=norm_parts(mid_s[sl,:])
            q=gn_s[sl,:]
            g2=g2+colsum(q*n); s2=s2+colsum(q)
            qg=q*vec_ref[1:2,:]
            cot=cot_ref[sl,:].astype(F32)
            db=db+colsum(cot)
            gm=cot+(qg-jnp.mean(qg,axis=1,keepdims=True)-n*jnp.mean(qg*n,axis=1,keepdims=True))*inv
            gm_ref[sl,:]=gm
            gb=gm.astype(BF)
            ob=ob+colsum(gb.astype(F32))
            do=mm(gb,wo_ref[...],NT).astype(BF)
            do_ref[sl,:]=do
            gwo=gwo+mm(att_ref[sl,:],gb,TN)
            prod=do.astype(F32)*att_ref[sl,:].astype(F32)
            hi=prod.astype(BF); lo=(prod-hi.astype(F32)).astype(BF)
            delta=-(mm(hi,pick)+mm(lo,pick))
            hi,md,lo=three(delta)
            dm_ref[sl,:]=jnp.where(lane>=36,jnp.zeros((),BF),jnp.where(lane%3==0,hi,jnp.where(lane%3==1,md,lo)))
        gwo_ref[...]=gwo.astype(BF)
        small_ref[0:1,:]=g2; small_ref[1:2,:]=s2; small_ref[2:3,:]=ob; small_ref[3:4,:]=db
        small_ref[4:8,:]=jnp.zeros((4,x_ref.shape[1]),F32)

def mid(x,cot,att,wo,vec,wu,wd,ub,FT=512,RC=256):
    T,D=x.shape; FF=wu.shape[1]
    full=lambda a: pl.BlockSpec(a.shape,lambda j:(0,0))
    S=jax.ShapeDtypeStruct
    fs=lambda *s: pl.BlockSpec(s,lambda j:(0,0))
    return pl.pallas_call(functools.partial(mid_kernel,RC),grid=(FF//FT,),
        in_specs=[full(x),full(cot),full(att),full(wo),full(vec),pl.BlockSpec((D,FT),lambda j:(0,j)),pl.BlockSpec((FT,D),lambda j:(j,0)),pl.BlockSpec((1,FT),lambda j:(0,j))],
        out_specs=[fs(T,D),fs(T,D),fs(T,D),fs(T,128),fs(D,D),pl.BlockSpec((D,FT),lambda j:(0,j)),pl.BlockSpec((FT,D),lambda j:(j,0)),pl.BlockSpec((1,FT),lambda j:(0,j)),fs(8,D)],
        out_shape=[S((T,D),BF),S((T,D),F32),S((T,D),BF),S((T,128),BF),S((D,D),BF),S((D,FF),BF),S((FF,D),BF),S((1,FF),F32),S((8,D),F32)],
        scratch_shapes=[pltpu.VMEM((T,D),F32),pltpu.VMEM((T,D),BF),pltpu.VMEM((D,T),BF),pltpu.VMEM((T,D),F32),pltpu.VMEM((T,D),F32)],
        compiler_params=pltpu.CompilerParams(vmem_limit_bytes=60<<20),name="feed_forward")(x,cot,att,wo,vec,wu,wd,ub)


MESH=pl.DeviceIdType.MESH
SIDE=768
WIDE=384
LAG=3
STEP=48

def bit_orders(n, count):
    plain=list(range(n.bit_length()-1))
    other=[0]+plain[2:]+[1] if len(plain)>2 else plain
    return [other if c%6==3 else plain for c in range(count)]

def plan_of(order, rows):
    sizes=[rows]
    for _ in order:
        m=sizes[-1]
        sizes.append(m//2 if m%32==0 else m)
    return sizes

def place(me, b):
    bit=(me//(1<<b))%2
    return bit, me+(1-2*bit)*(1<<b)

def rows_at(off, size):
    return pl.ds(off if isinstance(off,int) else pl.multiple_of(off,16),size)

class Engine:
    def __init__(self, n, entry, held, x, recv, sums, layout, send_sem, recv_sem, out_sem, me):
        self.orders=bit_orders(n,len(entry)); self.entry=entry; self.held=held
        self.x,self.recv,self.sums,self.layout=x,recv,sums,layout
        self.ss,self.rs,self.os,self.me=send_sem,recv_sem,out_sem,me
        self.bits=n.bit_length()-1
        self.sizes=plan_of(range(self.bits),SIDE)
        self.offs=[sum(self.sizes[1:s+1]) for s in range(self.bits+1)]

    def seg(self,c,upto):
        off=0
        for s in range(upto):
            if self.sizes[s+1]!=self.sizes[s]:
                off=off+place(self.me,self.orders[c][s])[0]*self.sizes[s+1]
        return off,self.sizes[upto]

    def out(self,c,off,m):
        a,i,k=self.layout[c]
        return self.sums[a].at[rows_at(i*SIDE+off,m),pl.ds(k*WIDE,WIDE)]

    def copy(self,c,stage):
        B,order,sizes,h=self.bits,self.orders[c],self.sizes,self.held[c]
        if stage<B:
            bit,partner=place(self.me,order[stage])
            off,m=self.seg(c,stage)
            if sizes[stage+1]!=m:
                src=self.x.at[h,rows_at(off+(1-bit)*(m//2),m//2)]
            else:
                src=self.x.at[h,rows_at(off,m)]
            dst=self.recv.at[c,pl.ds(self.offs[stage],sizes[stage+1])]
        else:
            s=2*B-1-stage
            if sizes[s+1]==sizes[s]:
                return None
            partner=place(self.me,order[s])[1]
            off,m=self.seg(c,s+1)
            dst=self.out(c,off,m)
            src=self.x.at[h,rows_at(off,m)] if stage==B else dst
        return pltpu.make_async_remote_copy(src,dst,self.ss.at[c,stage],self.rs.at[c,stage],
            device_id={"batch":partner},device_id_type=MESH)

    def keep(self,c):
        off,m=self.seg(c,self.bits)
        return pltpu.make_async_copy(self.x.at[self.held[c],rows_at(off,m)],self.out(c,off,m),self.os.at[c])

    def start(self,c,stage):
        if stage==self.bits:
            self.keep(c).start()
        d=self.copy(c,stage)
        if d is not None: d.start()

    def finish(self,c,stage):
        d=self.copy(c,stage)
        if d is not None: d.wait()
        if stage==self.bits:
            self.keep(c).wait()
        if stage<self.bits:
            off,m=self.seg(c,stage+1)
            ro=self.offs[stage]; x,recv,h=self.x,self.recv,self.held[c]
            def body(i,_):
                at=rows_at(off+i*STEP,STEP)
                more=recv[c,pl.ds(pl.multiple_of(ro+i*STEP,16),STEP)]
                x[h,at]=(x[h,at].astype(F32)+more.astype(F32)).astype(BF)
                return 0
            lax.fori_loop(0,m//STEP,body,0)

    def slot(self,t,load):
        for s in range(2*self.bits,-1,-1):
            for c in range(len(self.entry)):
                if t-self.entry[c]!=LAG*s: continue
                if s==0: load(c)
                else: self.finish(c,s-1)
                if s<2*self.bits: self.start(c,s)

    def last(self):
        return max(self.entry)+LAG*2*self.bits

def small_copy(me,x,recv,ss,rs,s):
    return pltpu.make_async_remote_copy(x.at[s],recv.at[s],ss.at[s],rs.at[s],device_id={"batch":place(me,s)[1]},device_id_type=MESH)

def back_kernel(n, NP, R, layout, loaded, att_slots,
               q_ref,kn_ref,kf_ref,vn_ref,vf_ref,do_ref,dm_ref,qm_ref,e_ref,et_ref,b_ref,kseg_ref,qf_ref,qmf_ref,
               feat_ref,wqkv_ref,gm_ref,vec_ref,early_ref,
               do_any,dm_any,gu_any,gd_any,go_any,
               ig_ref,smalla_ref,smallb_ref,su_any,sd_any,so_any,sq_any,
               dof,dmf,gmix,nt_s,g_s,x,recv,ax,arecv,bx,brecv,in_sem,out_sem,ss,rs,xs_sem,xr_sem,a_ss,a_rs,b_ss,b_rs):
    step=pl.program_id(0)
    per=NP*R
    second=(step>=per)&(step<2*per)
    inner=step%per; pair=inner//R; r=inner%R
    L=q_ref.shape[0]; T=feat_ref.shape[0]; D=feat_ref.shape[1]
    me=lax.axis_index("batch"); other={"stream":1-lax.axis_index("stream")}
    lane=lax.broadcasted_iota(jnp.int32,(1,128),1)
    zero=jnp.zeros((),BF)
    C=len(layout); extra=C-loaded
    grads=(gu_any,gd_any,go_any)
    held=[c if c<loaded else c-loaded for c in range(C)]
    entry=[c if c<loaded else att_slots+(c-loaded) for c in range(C)]
    eng=Engine(n,entry,held,x,recv,(su_any,sd_any,so_any,sq_any),layout,ss,rs,out_sem,me)
    B=eng.bits
    assert all(c+LAG*(B+1)<att_slots for c in range(extra))
    def load(c):
        a,i,k=layout[c]
        return pltpu.make_async_copy(grads[a].at[pl.ds(i*SIDE,SIDE),pl.ds(k*WIDE,WIDE)],x.at[c],in_sem.at[c])
    def ready(c):
        if c<loaded: load(c).wait()
    def across():
        res=[pltpu.make_async_remote_copy(dm_any,dmf,xs_sem.at[NP],xr_sem.at[NP],device_id=other,device_id_type=MESH)]
        for p in range(NP):
            res.append(pltpu.make_async_remote_copy(do_any.at[:,pl.ds(p*128,128)],dof.at[p],xs_sem.at[p],xr_sem.at[p],device_id=other,device_id_type=MESH))
        return res

    @pl.when(step==0)
    def _():
        sem=pltpu.get_barrier_semaphore()
        for b in range(B):
            pl.semaphore_signal(sem,inc=1,device_id={"batch":place(me,b)[1]},device_id_type=MESH)
        pl.semaphore_signal(sem,inc=1,device_id=other,device_id_type=MESH)
        for c in range(loaded): load(c).start()
        pl.semaphore_wait(sem,B+1)
        for d in across(): d.start()
    ticks=4*per
    edges=[att_slots*i//ticks for i in range(ticks+1)]
    first_small=2*per
    def tick(half):
        for k in range(2*per):
            i=k*2+half
            if edges[i]==edges[i+1] and not (half==0 and k>=per and k-per<=B): continue
            @pl.when(step==k)
            def _():
                for t in range(edges[i],edges[i+1]): eng.slot(t,ready)
                if half==0 and k>=per and k-per<=B:
                    s=k-per
                    if s==0: ax[0,256:]=early_ref[...]
                    else:
                        small_copy(me,ax,arecv,a_ss,a_rs,s-1).wait()
                        ax[s]=ax[s-1]+arecv[s-1]
                    if s<B: small_copy(me,ax,arecv,a_ss,a_rs,s).start()
                    else: smalla_ref[...]=ax[B]
    def half_of(hh):
        return (lane<64) if hh==0 else (lane>=64)
    def ones_of(h):
        return jnp.where((lane>=3*h)&(lane<3*h+3),1.0,0.0)
    add=lambda a,b: b if a is None else a+b
    def cols(part): return pl.ds(pl.multiple_of(part*D+pair*128,128),128)
    at=pl.ds(pl.multiple_of(r*L,L),L)

    tick(0)
    @pl.when(step<per)
    def _():
        dkn=None; dvn=None; dq=None
        for hh in range(2):
            mh=half_of(hh); h=2*pair+hh
            ones_h=ones_of(h); ones_b=jnp.broadcast_to(ones_h.astype(BF),(L,128))
            qm=jnp.where(mh,q_ref[...],zero); dom=jnp.where(mh,do_ref[...],zero)
            C_h=mm(e_ref[...],b_ref[hh]).astype(BF)
            qx=jnp.concatenate([qm,e_ref[...],qm_ref[...]],axis=1)
            dox=jnp.concatenate([dom,dm_ref[...]],axis=1)
            kseg=(kseg_ref[...].astype(F32)+ones_h).astype(BF)
            p=jnp.exp(mm(jnp.concatenate([kn_ref[...],C_h,kseg],axis=1),qx,NT))
            ds=(p*mm(jnp.concatenate([vn_ref[...],ones_b],axis=1),dox,NT)).astype(BF)
            dvn=add(dvn,mm(p.astype(BF),dom))
            t=mm(ds,jnp.concatenate([qm,e_ref[...]],axis=1))
            dkn=add(dkn,t[:,:128])
            g=mm(et_ref[...],t[:,128:].astype(BF))
            dq=add(dq,mm(ds,jnp.where(mh,kn_ref[...],zero),TN))
            p=jnp.exp(mm(jnp.concatenate([kf_ref[...],ones_b],axis=1),jnp.concatenate([qm,qm_ref[...]],axis=1),NT))
            ds=(p*mm(jnp.concatenate([vf_ref[...],ones_b],axis=1),dox,NT)).astype(BF)
            dq=add(dq,mm(ds,jnp.where(mh,kf_ref[...],zero),TN))
            @pl.when(r==0)
            def _(): g_s[hh]=g
            @pl.when(r!=0)
            def _(): g_s[hh]+=g
        gmix[at,cols(0)]=(dq*0.125).astype(BF)
        gmix[at,cols(1)]=dkn.astype(BF); gmix[at,cols(2)]=dvn.astype(BF)
    @pl.when((step<per)&(r==R-1))
    def _():
        i0=lax.broadcasted_iota(jnp.int32,(256,256),0); i1=lax.broadcasted_iota(jnp.int32,(256,256),1)
        gap=jnp.minimum(jnp.abs(i0%16-i1%16),7)
        pick=(lax.broadcasted_iota(jnp.int32,(16,256),0)==lax.broadcasted_iota(jnp.int32,(16,256),1)//16).astype(BF)
        rowi=lax.broadcasted_iota(jnp.int32,(256,128),0)//16; coli=lax.broadcasted_iota(jnp.int32,(256,128),1)
        tot=None
        for hh in range(2):
            h=2*pair+hh
            parts=[]
            for k in range(8):
                parts.append(mm(pick,jnp.where(gap==k,g_s[hh],0.0).astype(BF)))
            z=jnp.concatenate(parts,axis=0)
            hi=z.astype(BF); lo=(z-hi.astype(F32)).astype(BF)
            put=(coli==rowi+(h%8)*16).astype(BF)
            tot=add(tot,mm(hi,put)+mm(lo,put))
        base=pl.ds(pl.multiple_of((2*pair//8)*128,128),128)
        @pl.when((2*pair)%8==0)
        def _(): ax[0,base]=tot
        @pl.when((2*pair)%8!=0)
        def _(): ax[0,base]+=tot
    tick(1)
    @pl.when(step==per)
    def _():
        for d in across(): d.wait_recv()
    @pl.when(second)
    def _():
        dk=gmix[at,cols(1)].astype(F32); dv=gmix[at,cols(2)].astype(F32)
        for hh in range(2):
            mh=half_of(hh); h=2*pair+hh
            ones_b=jnp.broadcast_to(ones_of(h).astype(BF),(L,128))
            qm=jnp.where(mh,qf_ref[...],zero); dom=jnp.where(mh,dof[pair,at],zero)
            p=jnp.exp(mm(jnp.concatenate([kn_ref[...],ones_b],axis=1),jnp.concatenate([qm,qmf_ref[...]],axis=1),NT))
            ds=(p*mm(jnp.concatenate([vn_ref[...],ones_b],axis=1),jnp.concatenate([dom,dmf[at]],axis=1),NT)).astype(BF)
            dv=dv+mm(p.astype(BF),dom)
            dk=dk+mm(ds,qm)
        gmix[at,cols(1)]=dk.astype(BF); gmix[at,cols(2)]=dv.astype(BF)
    RC=256
    @pl.when(step==2*per)
    def _():
        now=att_slots
        for i in range(T//RC):
            sl=slice(i*RC,(i+1)*RC)
            nrm,_=norm_parts(feat_ref[sl,:].astype(F32))
            nt_s[:,sl]=(nrm*vec_ref[0:1,:]+vec_ref[1:2,:]).astype(BF).T
        for j in range(extra):
            a,i,k=layout[loaded+j]
            x[held[loaded+j]]=mm(nt_s[i*SIDE:(i+1)*SIDE,:],gmix[:,k*WIDE:(k+1)*WIDE]).astype(BF)
            eng.slot(now,ready); now+=1
        gain=0.0; shift=0.0; qb=0.0; vb=0.0
        for i in range(T//RC):
            sl=slice(i*RC,(i+1)*RC)
            g=mm(gmix[sl,:],wqkv_ref[...],NT)
            nrm,inv=norm_parts(feat_ref[sl,:].astype(F32))
            gain=gain+colsum(g*nrm); shift=shift+colsum(g)
            qb=qb+colsum(gmix[sl,:D].astype(F32)); vb=vb+colsum(gmix[sl,2*D:].astype(F32))
            qg=g*vec_ref[0:1,:]
            ig_ref[sl,:]=(gm_ref[sl,:]+(qg-jnp.mean(qg,axis=1,keepdims=True)-nrm*jnp.mean(qg*nrm,axis=1,keepdims=True))*inv).astype(BF)
            eng.slot(now,ready); now+=1
        w=D//128
        for i,v in enumerate((gain,shift,qb,vb)):
            for k in range(w): bx[0,i*w+k:i*w+k+1,:]=v[:,k*128:(k+1)*128]
        small_copy(me,bx,brecv,b_ss,b_rs,0).start()
        done=1
        for t in range(now,eng.last()+1):
            eng.slot(t,ready)
            if (t-now)%LAG==LAG-1 and done<=B:
                small_copy(me,bx,brecv,b_ss,b_rs,done-1).wait()
                bx[done]=bx[done-1]+brecv[done-1]
                if done<B: small_copy(me,bx,brecv,b_ss,b_rs,done).start()
                done+=1
        assert done==B+1
        smallb_ref[...]=bx[B]
        for d in across(): d.wait_send()

def back(q,kn,kf,vn,vf,do,dm,qmisc,e,et,bt,kseg,qf,qmf,feat,wqkv,gm,vec,early,grads,L,n,collective_id,att_slots=None):
    T,D=q.shape; R=T//L; NP=D//128; per=R*NP
    def one(step): i=jnp.minimum(step,per-1); return i%R,i//R
    def cyc(step): i=jnp.minimum(step,2*per-1)%per; return i%R,i//R
    def two(step): i=jnp.clip(step-per,0,per-1); return i%R,i//R
    blk=lambda f: pl.BlockSpec((L,128),f)
    row=lambda w,f: pl.BlockSpec((L,w),lambda s:(f(s)[0],0))
    full=lambda a: pl.BlockSpec(a.shape,lambda s:(0,)*len(a.shape),pipeline_mode=pl.Buffered(1))
    any_=pl.BlockSpec(memory_space=pl.ANY)
    S=jax.ShapeDtypeStruct; sem=pltpu.SemaphoreType.DMA
    qkv=S(wqkv.shape,BF)
    layout=[(a,i,k) for a,arr in enumerate(list(grads)+[qkv]) for i in range(arr.shape[0]//SIDE) for k in range(arr.shape[1]//WIDE)]
    loaded=sum(1 for l in layout if l[0]<len(grads))
    C=len(layout); bits=n.bit_length()-1
    rows=sum(plan_of(range(bits),SIDE)[1:])
    if att_slots is None: att_slots=loaded+LAG*2*bits
    asmall=(256+early.shape[0],128); bsmall=(4*D//128,128)
    outs=[S((T,D),BF),S(asmall,F32),S(bsmall,F32)]
    return pl.pallas_call(functools.partial(back_kernel,n,NP,R,layout,loaded,att_slots),grid=(2*per+1,),
        in_specs=[blk(one),blk(cyc),blk(one),blk(cyc),blk(one),blk(one),row(128,one),row(128,one),row(256,one),
                  pl.BlockSpec((256,L),lambda s:(0,one(s)[0])),pl.BlockSpec((2,256,256),lambda s:(one(s)[1],0,0)),row(128,one),blk(two),row(128,two),
                  full(feat),full(wqkv),full(gm),full(vec),full(early)]+[any_]*5,
        out_specs=[full(o) for o in outs]+[any_]*4,
        out_shape=outs+[S(a.shape,BF) for a in grads]+[qkv],
        scratch_shapes=[pltpu.VMEM((NP,T,128),BF),pltpu.VMEM((T,128),BF),pltpu.VMEM((T,3*D),BF),pltpu.VMEM((D,T),BF),pltpu.VMEM((2,256,256),F32),
            pltpu.VMEM((loaded,SIDE,WIDE),BF),pltpu.VMEM((C,rows,WIDE),BF),
            pltpu.VMEM((bits+1,)+asmall,F32),pltpu.VMEM((bits,)+asmall,F32),pltpu.VMEM((bits+1,)+bsmall,F32),pltpu.VMEM((bits,)+bsmall,F32),
            sem((C,)),sem((C,)),sem((C,2*bits)),sem((C,2*bits)),sem((NP+1,)),sem((NP+1,)),sem((bits,)),sem((bits,)),sem((bits,)),sem((bits,))],
        compiler_params=pltpu.CompilerParams(collective_id=collective_id,has_side_effects=True,vmem_limit_bytes=64<<20),
        name="att_bwd")(q,kn,kf,vn,vf,do,dm,qmisc,e,et,bt,kseg,qf,qmf,feat,wqkv,gm,vec,early,do,dm,*grads)


def from_partner(block, axis, stride):
    count = lax.axis_size(axis)
    route = []
    for low in range(count):
        high = low | 1 << stride
        if high != low and high < count:
            route += [(low, high), (high, low)]
    return lax.ppermute(block, axis, route)


def layer_norm(values, norm_gain, norm_shift):
    center = values - jnp.mean(values, axis=-1, keepdims=True)
    spread = jnp.mean(center * center, axis=-1, keepdims=True)
    return center * lax.rsqrt(spread + EPSILON) * norm_gain + norm_shift


def norm_back(values, norm_gain, norm_shift, upstream):
    unused, pull_back = jax.vjp(layer_norm, values, norm_gain, norm_shift)
    return pull_back(upstream)


def gelu_exact(values):
    return jax.nn.gelu(values, approximate=False)


def gelu_back(values, upstream):
    unused, pull_back = jax.vjp(gelu_exact, values)
    return pull_back(upstream)[0]


def prepare(segment_ids, box_cells, table, is_vision):
    cell = (box_cells[:, 0] * 16 + box_cells[:, 1]).reshape(-1)
    cells = jnp.arange(256)
    e = (cell[:, None] == cells[None]).astype(BF)
    et = (cells[:, None] == cell[None]).astype(BF)
    lane = jnp.arange(128)
    same = segment_ids.reshape(-1)[:, None] == lane[None] - 64
    inside = (lane >= 64) & (lane < 68)
    qseg = same.astype(BF)
    kseg = jnp.where(inside[None] & ~same & jnp.logical_not(is_vision), MASKED, 0.0).astype(BF)
    return e, et, qseg, kseg


def code_onehot():
    c = jnp.arange(65536)
    step_x = jnp.minimum(jnp.abs(c // 4096 - (c // 16) % 16), GRID - 1)
    step_y = jnp.minimum(jnp.abs((c // 256) % 16 - c % 16), GRID - 1)
    return ((step_x * GRID + step_y)[None] == jnp.arange(GRID * GRID)[:, None]).astype(BF)


def on_device(features, cotangent, segment_ids, box_cells, ln_gain, ln_shift, w_qkv, attn_bias,
              distance_table, w_out, w_up, up_bias, w_down, down_bias):
    rows, length, width = features.shape[1:]
    tokens = rows * length
    heads = distance_table.shape[2]
    is_vision = lax.axis_index("stream") != 0
    norm_gains, norm_shifts = ln_gain[0], ln_shift[0]
    bias_rows = attn_bias[0]
    qkv_weight, out_weight, up_weight, down_weight = w_qkv[0], w_out[0], w_up[0], w_down[0]
    plain_in = features[0].reshape(tokens, width).astype(jnp.float32)
    normed = layer_norm(plain_in, norm_gains[0], norm_shifts[0]).astype(BF)
    combined = jnp.dot(normed, qkv_weight, preferred_element_type=jnp.float32)
    queries = (combined[:, :width] + bias_rows[0]).astype(BF) * BF(0.125)
    key_part = combined[:, width:2 * width].astype(BF)
    value_part = (combined[:, 2 * width:] + bias_rows[1]).astype(BF)
    partner_k = from_partner(key_part, "stream", 0)
    partner_v = from_partner(value_part, "stream", 0)
    e, et, qseg, kseg = prepare(segment_ids, box_cells[0], distance_table[0], is_vision)
    onehot = code_onehot()
    bt = jnp.dot(distance_table[0].T.astype(BF), onehot, preferred_element_type=jnp.float32).astype(BF).reshape(heads, 256, 256)
    attended, qmisc = fwd(queries, key_part, partner_k, value_part, partner_v, e, bt, qseg, kseg, length)
    vec = jnp.concatenate([bias_rows[2:3], norm_gains[1:2], norm_shifts[1:2], down_bias, jnp.zeros((4, width), F32)])
    q_send, m_send = lax.optimization_barrier((queries, qmisc))
    partner_q = from_partner(q_send, "stream", 0)
    partner_m = from_partner(m_send, "stream", 0)
    (output, grad_middle, grad_attended, dmisc, grad_out, grad_up, grad_down, grad_up_bias, small_mid) = mid(
        features[0].reshape(tokens, width), cotangent[0].reshape(tokens, width), attended, out_weight, vec,
        up_weight, down_weight, up_bias)
    output = output.reshape(1, rows, length, width)
    small_up = grad_up_bias.reshape(-1, 128)
    early = jnp.concatenate([small_mid.reshape(-1, 128), small_up])
    vec_one = jnp.concatenate([norm_gains[0:1], norm_shifts[0:1], jnp.zeros((6, width), F32)])
    input_grad, small_a, small_b, sum_up, sum_down, sum_out, sum_qkv = back(
        queries, key_part, partner_k, value_part, partner_v, grad_attended, dmisc, qmisc, e, et, bt, kseg,
        partner_q, partner_m, features[0].reshape(tokens, width), qkv_weight, grad_middle, vec_one, early,
        [grad_up, grad_down, grad_out], length, lax.axis_size("batch"), 4)
    input_grad = input_grad.reshape(1, rows, length, width)
    by_gap = small_a[:256].reshape(2, 8, 16, 8, 16)
    steps = jnp.minimum(jnp.abs(jnp.arange(16)[:, None] - jnp.arange(16)[None]), GRID - 1)
    near = (steps[None] == jnp.arange(GRID)[:, None, None]).astype(F32)
    dist = jnp.einsum("gyahb,xab->xygh", by_gap, near, precision=lax.Precision.HIGHEST).reshape(GRID * GRID, 16)[:, :heads][None]
    mid_sums = small_a[256:256 + 8 * width // 128].reshape(8, width)
    upb = small_a[256 + 8 * width // 128:].reshape(1, -1)
    last = small_b.reshape(4, width)
    gain = jnp.stack([last[0], mid_sums[0]])[None]
    shift = jnp.stack([last[1], mid_sums[1]])[None]
    bias = jnp.stack([last[2], last[3], mid_sums[2]])[None]
    downb = mid_sums[3][None]
    f32 = lambda a: a.astype(jnp.float32)[None]
    return (output, input_grad, gain, shift, f32(sum_qkv), bias, dist, f32(sum_out), f32(sum_up), upb, f32(sum_down), downb)


def solution(mesh):
    in_specs = (
        P("stream", "batch", None, None),
        P("stream", "batch", None, None),
        P("batch", None),
        P("stream", "batch", None, None),
        P("stream", None, None),
        P("stream", None, None),
        P("stream", None, None),
        P("stream", None, None),
        P("stream", None, None),
        P("stream", None, None),
        P("stream", None, None),
        P("stream", None),
        P("stream", None, None),
        P("stream", None),
    )
    out_specs = (
        P("stream", "batch", None, None),
        P("stream", "batch", None, None),
        P("stream", None, None),
        P("stream", None, None),
        P("stream", None, None),
        P("stream", None, None),
        P("stream", None, None),
        P("stream", None, None),
        P("stream", None, None),
        P("stream", None),
        P("stream", None, None),
        P("stream", None),
    )
    return jax.shard_map(
        on_device, mesh=mesh, in_specs=in_specs, out_specs=out_specs, check_vma=False
    )
```

```python
import functools
import jax
import jax.numpy as jnp
from jax import lax
from jax.experimental import pallas as pl
from jax.experimental.pallas import tpu as pltpu
from jax.sharding import PartitionSpec as P

GRID = 8
EPSILON = 1e-05
MASKED = -1000000000.0

NT=(((1,),(1,)),((),())); NN=(((1,),(0,)),((),())); TN=(((0,),(0,)),((),()))
def mm(a,b,dn=NN): return lax.dot_general(a,b,dn,preferred_element_type=jnp.float32)
BF=jnp.bfloat16

def three(x):
    hi=x.astype(BF); r=x-hi.astype(jnp.float32); mid=r.astype(BF); lo=(r-mid.astype(jnp.float32)).astype(BF)
    return hi,mid,lo

def fwd_kernel(CQ, q_ref,kn_ref,kf_ref,vn_ref,vf_ref,e_ref,b_ref,qseg_ref,kseg_ref,o_ref,qm_ref):
    pair=pl.program_id(1)
    L=q_ref.shape[0]
    lane=lax.broadcasted_iota(jnp.int32,(1,128),1)
    @pl.when(pair==0)
    def _():
        qm_ref[...]=qseg_ref[...]
    outs=[None]*(L//CQ)
    for hh in range(2):
        mh=(lane<64) if hh==0 else (lane>=64)
        h=2*pair+hh
        C=mm(e_ref[...],b_ref[hh]).astype(BF)
        kx=jnp.concatenate([kn_ref[...],C,kseg_ref[...]],axis=1)
        kf=kf_ref[...]
        one=jnp.ones((),BF); zero=jnp.zeros((),BF)
        vnx=jnp.where(mh,vn_ref[...],one); vfx=jnp.where(mh,vf_ref[...],one)
        for c in range(L//CQ):
            sl=slice(c*CQ,(c+1)*CQ)
            qm=jnp.where(mh,q_ref[sl,:],zero)
            qx=jnp.concatenate([qm,e_ref[sl,:],qseg_ref[sl,:]],axis=1)
            sn=mm(qx,kx,NT); sf=mm(qm,kf,NT)
            m=jnp.maximum(jnp.max(sn,axis=1,keepdims=True),jnp.max(sf,axis=1,keepdims=True))
            pn=jnp.exp(sn-m).astype(BF); pf=jnp.exp(sf-m).astype(BF)
            o=mm(pn,vnx)+mm(pf,vfx)
            l=pltpu.roll(o,64,1)
            on=o/l
            outs[c]=on if hh==0 else jnp.where(mh,on,outs[c])
            lse=-(m+jnp.log(jnp.where(mh,l,o)))
            hi,mid,lo=three(lse)
            cur=qm_ref[sl,:]
            cur=jnp.where(lane==3*h,hi,cur); cur=jnp.where(lane==3*h+1,mid,cur); cur=jnp.where(lane==3*h+2,lo,cur)
            qm_ref[sl,:]=cur
    for c in range(L//CQ):
        o_ref[c*CQ:(c+1)*CQ,:]=outs[c].astype(BF)

def fwd(q,kn,kf,vn,vf,e,bt,qseg,kseg,L,CQ=512):
    T=q.shape[0]; R=T//L; NP=q.shape[1]//128
    blk=pl.BlockSpec((L,128),lambda r,p:(r,p))
    row=lambda w: pl.BlockSpec((L,w),lambda r,p:(r,0))
    return pl.pallas_call(functools.partial(fwd_kernel,CQ),grid=(R,NP),
        in_specs=[blk]*5+[row(256),pl.BlockSpec((2,256,256),lambda r,p:(p,0,0)),row(128),row(128)],
        out_specs=[blk,row(128)],
        out_shape=[jax.ShapeDtypeStruct(q.shape,BF),jax.ShapeDtypeStruct((T,128),BF)],
        compiler_params=pltpu.CompilerParams(vmem_limit_bytes=48<<20),name="att_fwd")(q,kn,kf,vn,vf,e,bt,qseg,kseg)


F32=jnp.float32


MESH=pl.DeviceIdType.MESH
SIDE=768
WIDE=384
LAG=3
STEP=48

def bit_order(n, c):
    plain=list(range(n.bit_length()-1))
    other=[0]+plain[2:]+[1] if len(plain)>2 else plain
    return other if c%6==3 else plain

def plan_of(bits, rows):
    sizes=[rows]
    for _ in range(bits):
        m=sizes[-1]
        sizes.append(m//2 if m%32==0 else m)
    return sizes

def place(me, b):
    bit=(me//(1<<b))%2
    return bit, me+(1-2*bit)*(1<<b)

def rows_at(off, size):
    return pl.ds(off if isinstance(off,int) else pl.multiple_of(off,16),size)

class Engine:
    def __init__(self, n, me, lag, chunks, x, recv, segs, sums, ss, rs, os):
        self.me,self.lag,self.chunks=me,lag,chunks
        self.x,self.recv,self.segs,self.sums=x,recv,segs,sums
        self.ss,self.rs,self.os=ss,rs,os
        self.bits=n.bit_length()-1
        self.sizes=plan_of(self.bits,SIDE)
        self.offs=[sum(self.sizes[1:s+1]) for s in range(self.bits+1)]
        self.n=n

    def seg(self,c,upto):
        order=bit_order(self.n,self.chunks[c]["kind"]); off=0
        for s in range(upto):
            if self.sizes[s+1]!=self.sizes[s]:
                off=off+place(self.me,order[s])[0]*self.sizes[s+1]
        return off,self.sizes[upto]

    def out(self,c,off,m):
        a,i,k=self.chunks[c]["to"]
        return self.sums[a].at[rows_at(i*SIDE+off,m),pl.ds(k*WIDE,WIDE)]

    def final(self,c):
        off,m=self.seg(c,self.bits)
        ch=self.chunks[c]
        if ch["first"]: return self.segs.at[ch["seg"]]
        return self.x.at[ch["slot"],rows_at(off,m)]

    def copy(self,c,stage):
        B,sizes,ch=self.bits,self.sizes,self.chunks[c]
        order=bit_order(self.n,ch["kind"])
        if stage<B:
            bit,partner=place(self.me,order[stage])
            off,m=self.seg(c,stage)
            if sizes[stage+1]!=m:
                src=self.x.at[ch["slot"],rows_at(off+(1-bit)*(m//2),m//2)]
            else:
                src=self.x.at[ch["slot"],rows_at(off,m)]
            dst=self.recv.at[ch["land"],pl.ds(self.offs[stage],sizes[stage+1])]
        else:
            s=2*B-1-stage
            if sizes[s+1]==sizes[s]:
                return None
            partner=place(self.me,order[s])[1]
            off,m=self.seg(c,s+1)
            dst=self.out(c,off,m)
            src=self.final(c) if stage==B else dst
        return pltpu.make_async_remote_copy(src,dst,self.ss.at[c,stage],self.rs.at[c,stage],
            device_id={"batch":partner},device_id_type=MESH)

    def keep(self,c):
        off,m=self.seg(c,self.bits)
        return pltpu.make_async_copy(self.final(c),self.out(c,off,m),self.os.at[c])

    def start(self,c,stage):
        if stage==self.bits:
            self.keep(c).start()
        d=self.copy(c,stage)
        if d is not None: d.start()

    def finish(self,c,stage):
        d=self.copy(c,stage)
        if d is not None: d.wait()
        if stage==self.bits:
            self.keep(c).wait()
        if stage<self.bits:
            off,m=self.seg(c,stage+1)
            ro=self.offs[stage]; x,recv=self.x,self.recv
            h,land=self.chunks[c]["slot"],self.chunks[c]["land"]
            def body(i,_):
                at=rows_at(off+i*STEP,STEP)
                more=recv[land,pl.ds(pl.multiple_of(ro+i*STEP,16),STEP)]
                x[h,at]=(x[h,at].astype(F32)+more.astype(F32)).astype(BF)
                return 0
            lax.fori_loop(0,m//STEP,body,0)
            if stage==self.bits-1 and self.chunks[c]["last"]==self.bits:
                self.segs[self.chunks[c]["seg"]]=x[h,rows_at(off,m)]

    def slot(self,t,load):
        for c in sorted(range(len(self.chunks)),key=lambda c:self.chunks[c]["entry"]):
            ch=self.chunks[c]
            if t<ch["entry"] or (t-ch["entry"])%self.lag: continue
            s=ch["first"]+(t-ch["entry"])//self.lag
            if s>ch["last"]: continue
            if s==ch["first"]: load(c)
            else: self.finish(c,s-1)
            if s<ch["last"]: self.start(c,s)

    def end(self):
        return 1+max(ch["entry"]+self.lag*(ch["last"]-ch["first"]) for ch in self.chunks)

def small_copy(me,x,recv,ss,rs,s):
    return pltpu.make_async_remote_copy(x.at[s],recv.at[s],ss.at[s],rs.at[s],device_id={"batch":place(me,s)[1]},device_id_type=MESH)

def back_kernel(n, NP, R, chunks, loads, cuts,
               q_ref,kn_ref,kf_ref,vn_ref,vf_ref,do_ref,dm_ref,qm_ref,e_ref,et_ref,b_ref,kseg_ref,qf_ref,qmf_ref,
               feat_ref,wqkv_ref,gm_ref,vec_ref,early_ref,
               do_any,dm_any,segs,gu_any,gd_any,go_any,
               ig_ref,smalla_ref,smallb_ref,su_any,sd_any,so_any,sq_any,
               dof,dmf,gmix,nt_s,g_s,tab,x,recv,ax,arecv,bx,brecv,in_sem,out_sem,ss,rs,xs_sem,xr_sem,a_ss,a_rs,b_ss,b_rs):
    step=pl.program_id(0)
    per=NP*R
    second=(step>=per)&(step<2*per)
    inner=step%per; pair=inner//R; r=inner%R
    L=q_ref.shape[0]; T=feat_ref.shape[0]; D=feat_ref.shape[1]
    me=lax.axis_index("batch"); other={"stream":1-lax.axis_index("stream")}
    lane=lax.broadcasted_iota(jnp.int32,(1,128),1)
    zero=jnp.zeros((),BF)
    RC=256
    grads=(gu_any,gd_any,go_any)
    eng=Engine(n,me,LAG,chunks,x,recv,segs,(su_any,sd_any,so_any,sq_any),ss,rs,out_sem)
    B=eng.bits
    q_set,mid_set,end_set=[[c for c in range(len(chunks)) if chunks[c].get("set")==i] for i in range(3)]
    def load(c):
        a,k=loads[c]
        return pltpu.make_async_copy(grads[a].at[:,pl.ds(k*WIDE,WIDE)],x.at[chunks[c]["slot"]],in_sem.at[c])
    def ready(c):
        if c in loads: load(c).wait()
    def across():
        res=[pltpu.make_async_remote_copy(dm_any,dmf,xs_sem.at[NP],xr_sem.at[NP],device_id=other,device_id_type=MESH)]
        for p in range(NP):
            res.append(pltpu.make_async_remote_copy(do_any.at[:,pl.ds(p*128,128)],dof.at[p],xs_sem.at[p],xr_sem.at[p],device_id=other,device_id_type=MESH))
        return res

    @pl.when(step==0)
    def _():
        sem=pltpu.get_barrier_semaphore()
        for b in range(B):
            pl.semaphore_signal(sem,inc=1,device_id={"batch":place(me,b)[1]},device_id_type=MESH)
        pl.semaphore_signal(sem,inc=1,device_id=other,device_id_type=MESH)
        for c in loads: load(c).start()
        pl.semaphore_wait(sem,B+1)
        for d in across(): d.start()
    def spread(lo,hi,parts): return [lo+(hi-lo)*i//parts for i in range(parts)]
    edges=spread(0,cuts[0],2*per)+spread(cuts[0],cuts[1],per)+spread(cuts[1],cuts[2],per)+[cuts[2]]
    def form(c):
        a,i,k=chunks[c]["to"]
        x[chunks[c]["slot"]]=mm(nt_s[i*SIDE:(i+1)*SIDE,:],gmix[:,k*WIDE:(k+1)*WIDE]).astype(BF)
    def tick(half):
        for k in range(2*per):
            i=k*2+half
            small_now=half==0 and k>=per and k-per<=B
            group=q_set if i==2*per else mid_set if i==3*per else []
            if edges[i]==edges[i+1] and not small_now and not group: continue
            @pl.when(step==k)
            def _():
                if i==2*per:
                    for j in range(T//RC):
                        sl=slice(j*RC,(j+1)*RC)
                        nrm,_=norm_parts(feat_ref[sl,:].astype(F32))
                        nt_s[:,sl]=(nrm*vec_ref[0:1,:]+vec_ref[1:2,:]).astype(BF).T
                for c in group: form(c)
                for t in range(edges[i],edges[i+1]): eng.slot(t,ready)
                if small_now:
                    s=k-per
                    if s==0:
                        put=(lax.broadcasted_iota(jnp.int32,(256,128),1)==lax.broadcasted_iota(jnp.int32,(256,128),0)//16).astype(BF)
                        ax[0,:2*NP*16]=sum(mm(v,put) for v in three(tab[...]))
                        ax[0,2*NP*16:]=early_ref[...]
                    else:
                        small_copy(me,ax,arecv,a_ss,a_rs,s-1).wait()
                        ax[s]=ax[s-1]+arecv[s-1]
                    if s<B: small_copy(me,ax,arecv,a_ss,a_rs,s).start()
                    else: smalla_ref[...]=ax[B]
    def half_of(hh):
        return (lane<64) if hh==0 else (lane>=64)
    def ones_of(h):
        return jnp.where((lane>=3*h)&(lane<3*h+3),1.0,0.0)
    add=lambda a,b: b if a is None else a+b
    def cols(part): return pl.ds(pl.multiple_of(part*D+pair*128,128),128)
    at=pl.ds(pl.multiple_of(r*L,L),L)

    tick(0)
    @pl.when(step<per)
    def _():
        dkn=None; dvn=None; dq=None
        for hh in range(2):
            mh=half_of(hh); h=2*pair+hh
            ones_h=ones_of(h); ones_b=jnp.broadcast_to(ones_h.astype(BF),(L,128))
            qm=jnp.where(mh,q_ref[...],zero); dom=jnp.where(mh,do_ref[...],zero)
            C_h=mm(e_ref[...],b_ref[hh]).astype(BF)
            qx=jnp.concatenate([qm,e_ref[...],qm_ref[...]],axis=1)
            dox=jnp.concatenate([dom,dm_ref[...]],axis=1)
            kseg=(kseg_ref[...].astype(F32)+ones_h).astype(BF)
            p=jnp.exp(mm(jnp.concatenate([kn_ref[...],C_h,kseg],axis=1),qx,NT))
            ds=(p*mm(jnp.concatenate([vn_ref[...],ones_b],axis=1),dox,NT)).astype(BF)
            dvn=add(dvn,mm(p.astype(BF),dom))
            t=mm(ds,jnp.concatenate([qm,e_ref[...]],axis=1))
            dkn=add(dkn,t[:,:128])
            g=mm(et_ref[...],t[:,128:].astype(BF))
            dq=add(dq,mm(ds,jnp.where(mh,kn_ref[...],zero),TN))
            p=jnp.exp(mm(jnp.concatenate([kf_ref[...],ones_b],axis=1),jnp.concatenate([qm,qm_ref[...]],axis=1),NT))
            ds=(p*mm(jnp.concatenate([vf_ref[...],ones_b],axis=1),dox,NT)).astype(BF)
            dq=add(dq,mm(ds,jnp.where(mh,kf_ref[...],zero),TN))
            @pl.when(r==0)
            def _(): g_s[hh]=g
            @pl.when(r!=0)
            def _(): g_s[hh]+=g
        gmix[at,cols(0)]=(dq*0.125).astype(BF)
        gmix[at,cols(1)]=dkn.astype(BF); gmix[at,cols(2)]=dvn.astype(BF)
    @pl.when((step<per)&(r==R-1))
    def _():
        turn=lax.broadcasted_iota(jnp.int32,(1,256),1)
        gap=jnp.minimum(jnp.abs(lax.broadcasted_iota(jnp.int32,(16,256),0)-turn%16),7)
        for hh in range(2):
            ahead=None; behind=None
            for i in range(16):
                blk=g_s[hh,16*i:16*i+16,:]
                if i: blk=pltpu.roll(blk,256-16*i,1)
                ahead=add(ahead,jnp.where(turn<256-16*i,blk,0.0))
                behind=add(behind,jnp.where(turn<256-16*i,0.0,blk))
            sums=[colsum(jnp.where(gap==k,v,0.0)) for v in (ahead,behind) for k in range(8)]
            tab[pl.ds(pl.multiple_of((2*pair+hh)*16,16),16),:]=jnp.concatenate(sums,axis=0)
    tick(1)
    @pl.when(step==per)
    def _():
        for d in across(): d.wait_recv()
    @pl.when(second)
    def _():
        dk=gmix[at,cols(1)].astype(F32); dv=gmix[at,cols(2)].astype(F32)
        for hh in range(2):
            mh=half_of(hh); h=2*pair+hh
            ones_b=jnp.broadcast_to(ones_of(h).astype(BF),(L,128))
            qm=jnp.where(mh,qf_ref[...],zero); dom=jnp.where(mh,dof[pair,at],zero)
            p=jnp.exp(mm(jnp.concatenate([kn_ref[...],ones_b],axis=1),jnp.concatenate([qm,qmf_ref[...]],axis=1),NT))
            ds=(p*mm(jnp.concatenate([vn_ref[...],ones_b],axis=1),jnp.concatenate([dom,dmf[at]],axis=1),NT)).astype(BF)
            dv=dv+mm(p.astype(BF),dom)
            dk=dk+mm(ds,qm)
        gmix[at,cols(1)]=dk.astype(BF); gmix[at,cols(2)]=dv.astype(BF)
    @pl.when(step==2*per)
    def _():
        now=cuts[2]
        for c in end_set:
            form(c); eng.slot(now,ready); now+=1
        gain=0.0; shift=0.0; qb=0.0; vb=0.0
        for i in range(T//RC):
            sl=slice(i*RC,(i+1)*RC)
            g=mm(gmix[sl,:],wqkv_ref[...],NT)
            nrm,inv=norm_parts(feat_ref[sl,:].astype(F32))
            gain=gain+colsum(g*nrm); shift=shift+colsum(g)
            qb=qb+colsum(gmix[sl,:D].astype(F32)); vb=vb+colsum(gmix[sl,2*D:].astype(F32))
            qg=g*vec_ref[0:1,:]
            ig_ref[sl,:]=(gm_ref[sl,:]+(qg-jnp.mean(qg,axis=1,keepdims=True)-nrm*jnp.mean(qg*nrm,axis=1,keepdims=True))*inv).astype(BF)
            eng.slot(now,ready); now+=1
        w=D//128
        for i,v in enumerate((gain,shift,qb,vb)):
            for k in range(w): bx[0,i*w+k:i*w+k+1,:]=v[:,k*128:(k+1)*128]
        small_copy(me,bx,brecv,b_ss,b_rs,0).start()
        done=1
        for t in range(now,max(eng.end(),now+LAG*B)):
            eng.slot(t,ready)
            if (t-now)%LAG==LAG-1 and done<=B:
                small_copy(me,bx,brecv,b_ss,b_rs,done-1).wait()
                bx[done]=bx[done-1]+brecv[done-1]
                if done<B: small_copy(me,bx,brecv,b_ss,b_rs,done).start()
                done+=1
        assert done==B+1
        smallb_ref[...]=bx[B]
        for d in across(): d.wait_send()

def back(q,kn,kf,vn,vf,do,dm,qmisc,e,et,bt,kseg,qf,qmf,feat,wqkv,gm,vec,early,segs,grads,full_ff,L,n,collective_id):
    T,D=q.shape; R=T//L; NP=D//128; per=R*NP
    def one(step): i=jnp.minimum(step,per-1); return i%R,i//R
    def cyc(step): i=jnp.minimum(step,2*per-1)%per; return i%R,i//R
    def two(step): i=jnp.clip(step-per,0,per-1); return i%R,i//R
    blk=lambda f: pl.BlockSpec((L,128),f)
    row=lambda w,f: pl.BlockSpec((L,w),lambda s:(f(s)[0],0))
    full=lambda a: pl.BlockSpec(a.shape,lambda s:(0,)*len(a.shape),pipeline_mode=pl.Buffered(1))
    any_=pl.BlockSpec(memory_space=pl.ANY)
    S=jax.ShapeDtypeStruct; sem=pltpu.SemaphoreType.DMA
    bits=n.bit_length()-1; per_side=D//WIDE; tiles=full_ff//SIDE
    first=max(20,LAG*(bits+1)+per_side)
    cuts=(first,first+9,first+20)
    chunks=[]; loads={}
    def chunk(to,entry,**more):
        ch=dict(to=to,entry=entry,kind=len(chunks),first=0,last=2*bits); ch.update(more); chunks.append(ch)
    for i,(a,r,k) in enumerate([(0,0,(tiles-1)*per_side+k) for k in range(per_side)]+[(1,tiles-1,k) for k in range(per_side)]+[(2,0,k) for k in range(per_side)]):
        loads[len(chunks)]=(a,i%per_side)
        chunk((a,r,k),3*i,slot=i,land=i)
    place_of=[p for t in range(tiles-1) for p in [(0,0,t*per_side+k) for k in range(per_side)]+[(1,t,k) for k in range(per_side)]]
    spare=[t for t in range(first) if t%3 or t>=3*len(loads)]
    for i,p in enumerate(place_of):
        chunk(p,spare[i],first=bits,seg=i,kind=i)
    at=len(loads)
    half=per_side//2
    for g,group in enumerate(([k for k in range(per_side)],[per_side+k for k in range(half)]+[2*per_side+k for k in range(half)],
                  [per_side+k for k in range(half,per_side)]+[2*per_side+k for k in range(half,per_side)])):
        for i,k in enumerate(group):
            chunk((3,0,k),cuts[g]+i,slot=at,land=at,set=g); at+=1
    C=len(chunks)
    rows=sum(plan_of(bits,SIDE)[1:])
    asmall=(2*NP*16+early.shape[0],128); bsmall=(4*D//128,128)
    outs=[S((T,D),BF),S(asmall,F32),S(bsmall,F32)]
    sums=[S((D,full_ff),BF),S((full_ff,D),BF),S((D,D),BF),S(wqkv.shape,BF)]
    return pl.pallas_call(functools.partial(back_kernel,n,NP,R,chunks,loads,cuts),grid=(2*per+1,),
        in_specs=[blk(one),blk(cyc),blk(one),blk(cyc),blk(one),blk(one),row(128,one),row(128,one),row(256,one),
                  pl.BlockSpec((256,L),lambda s:(0,one(s)[0])),pl.BlockSpec((2,256,256),lambda s:(one(s)[1],0,0)),row(128,one),blk(two),row(128,two),
                  full(feat),full(wqkv),full(gm),full(vec),full(early)]+[any_]*2+[full(segs)]+[any_]*3,
        out_specs=[full(o) for o in outs]+[any_]*4,
        out_shape=outs+sums,
        scratch_shapes=[pltpu.VMEM((NP,T,128),BF),pltpu.VMEM((T,128),BF),pltpu.VMEM((T,3*D),BF),pltpu.VMEM((D,T),BF),pltpu.VMEM((2,256,256),F32),pltpu.VMEM((2*NP*16,256),F32),
            pltpu.VMEM((at,SIDE,WIDE),BF),pltpu.VMEM((at,rows,WIDE),BF),
            pltpu.VMEM((bits+1,)+asmall,F32),pltpu.VMEM((bits,)+asmall,F32),pltpu.VMEM((bits+1,)+bsmall,F32),pltpu.VMEM((bits,)+bsmall,F32),
            sem((C,)),sem((C,)),sem((C,2*bits)),sem((C,2*bits)),sem((NP+1,)),sem((NP+1,)),sem((bits,)),sem((bits,)),sem((bits,)),sem((bits,))],
        compiler_params=pltpu.CompilerParams(collective_id=collective_id,has_side_effects=True,vmem_limit_bytes=64<<20),
        name="att_bwd")(q,kn,kf,vn,vf,do,dm,qmisc,e,et,bt,kseg,qf,qmf,feat,wqkv,gm,vec,early,do,dm,segs,*grads)


def gelu_both(u):
    a=jnp.abs(u)
    t=1.0/(1.0+a*(0.3275911*0.7071067811865476))
    ex=jnp.exp(u*u*-0.5)
    poly=((((1.061405429*t-1.453152027)*t+1.421413741)*t-0.284496736)*t+0.254829592)*t
    half=0.5*poly*ex
    cdf=jnp.where(u<0,half,1.0-half)
    return u*cdf, cdf+u*ex*0.3989422804014327

def norm_parts(v):
    center=v-jnp.mean(v,axis=1,keepdims=True)
    inv=lax.rsqrt(jnp.mean(center*center,axis=1,keepdims=True)+EPSILON)
    return center*inv,inv

def colsum(v): return jnp.sum(v,axis=0,keepdims=True)


MID_LAG=2
def mid_kernel(n, chunks, TILES, x_ref,cot_ref,att_ref,wo_ref,vec_ref,wu_ref,wd_ref,ub_ref,
               out_ref,gm_ref,do_ref,dm_ref,gwo_ref,gul_ref,gdl_ref,gub_ref,small_ref,seg_ref,
               mid_s,nt_s,ntt_s,acc_s,gn_s,act_s,gp_s,x,recv,ss,rs):
    j=pl.program_id(0); T=x_ref.shape[0]; D=x_ref.shape[1]; RC=256
    parts=[slice(i*RC,(i+1)*RC) for i in range(T//RC)]
    me=lax.axis_index("batch")
    eng=Engine(n,me,MID_LAG,chunks,x,recv,seg_ref,None,ss,rs,None)
    per_tile=2*D//WIDE; pace=2*len(parts)
    def tick(i):
        for jj in range(1,TILES):
            @pl.when(j==jj)
            def _():
                for t in range(2*i,2*i+2): eng.slot(pace*(jj-1)+t,lambda c:None)
    @pl.when(j==0)
    def _():
        sem=pltpu.get_barrier_semaphore()
        for b in range(eng.bits):
            pl.semaphore_signal(sem,inc=1,device_id={"batch":place(me,b)[1]},device_id_type=MESH)
        for sl in parts:
            v=x_ref[sl,:].astype(F32)+mm(att_ref[sl,:],wo_ref[...])+vec_ref[0:1,:]
            mid_s[sl,:]=v
            nrm,_=norm_parts(v)
            nt=(nrm*vec_ref[1:2,:]+vec_ref[2:3,:]).astype(BF)
            nt_s[sl,:]=nt
            ntt_s[:,sl]=nt.T
            acc_s[sl,:]=v+vec_ref[3:4,:]
            gn_s[sl,:]=jnp.zeros_like(v)
        pl.semaphore_wait(sem,eng.bits)
    gub=0.0
    for i,sl in enumerate(parts):
        tick(i)
        pre=mm(nt_s[sl,:],wu_ref[...])+ub_ref[...]
        act,slope=gelu_both(pre)
        act=act.astype(BF)
        gp=(mm(cot_ref[sl,:],wd_ref[...],NT)*slope).astype(BF)
        act_s[sl,:]=act; gp_s[sl,:]=gp
        acc_s[sl,:]+=mm(act,wd_ref[...])
        gn_s[sl,:]+=mm(gp,wu_ref[...],NT)
        gub=gub+colsum(gp.astype(F32))
    gub_ref[...]=gub
    for k in range(D//WIDE):
        cs=slice(k*WIDE,(k+1)*WIDE)
        up=mm(ntt_s[...],gp_s[:,cs]).astype(BF)
        down=mm(act_s[...],cot_ref[:,cs],TN).astype(BF)
        @pl.when(j<TILES-1)
        def _():
            x[per_tile*j+k]=up
            x[per_tile*j+D//WIDE+k]=down
        @pl.when(j==TILES-1)
        def _():
            gul_ref[:,cs]=up; gdl_ref[:,cs]=down
    @pl.when(j==TILES-1)
    def _():
        g2=0.0; s2=0.0; ob=0.0; db=0.0; gwo=0.0
        row=lax.broadcasted_iota(jnp.int32,(D,128),0)//64
        col=lax.broadcasted_iota(jnp.int32,(D,128),1)
        pick=(row==col//3).astype(BF)
        lane=lax.broadcasted_iota(jnp.int32,(1,128),1)
        now=pace*(TILES-1)
        for sl in parts:
            out_ref[sl,:]=acc_s[sl,:].astype(BF)
            nrm,inv=norm_parts(mid_s[sl,:])
            q=gn_s[sl,:]
            g2=g2+colsum(q*nrm); s2=s2+colsum(q)
            qg=q*vec_ref[1:2,:]
            cot=cot_ref[sl,:].astype(F32)
            db=db+colsum(cot)
            gm=cot+(qg-jnp.mean(qg,axis=1,keepdims=True)-nrm*jnp.mean(qg*nrm,axis=1,keepdims=True))*inv
            gm_ref[sl,:]=gm
            gb=gm.astype(BF)
            gp_s[sl,:]=gb
            ob=ob+colsum(gb.astype(F32))
            do=mm(gb,wo_ref[...],NT).astype(BF)
            do_ref[sl,:]=do
            prod=do.astype(F32)*att_ref[sl,:].astype(F32)
            hi=prod.astype(BF); lo=(prod-hi.astype(F32)).astype(BF)
            delta=-(mm(hi,pick)+mm(lo,pick))
            hi,md,lo=three(delta)
            dm_ref[sl,:]=jnp.where(lane>=6*(D//128),jnp.zeros((),BF),jnp.where(lane%3==0,hi,jnp.where(lane%3==1,md,lo)))
            eng.slot(now,lambda c:None); now+=1
        gwo_ref[...]=mm(att_ref[...],gp_s[...],TN).astype(BF)
        small_ref[0:1,:]=g2; small_ref[1:2,:]=s2; small_ref[2:3,:]=ob; small_ref[3:4,:]=db
        small_ref[4:8,:]=jnp.zeros((4,D),F32)
        for t in range(now,eng.end()): eng.slot(t,lambda c:None)

def mid(x,cot,att,wo,vec,wu,wd,ub,n,collective_id):
    T,D=x.shape; FF=wu.shape[1]; FT=SIDE; TILES=FF//FT
    bits=n.bit_length()-1; pace=2*(T//256); per_tile=2*D//WIDE
    sizes=plan_of(bits,SIDE)
    chunks=[dict(entry=pace*(c//per_tile)+c%per_tile,kind=c,first=0,last=bits,slot=c,land=c,seg=c) for c in range(per_tile*(TILES-1))]
    C=len(chunks)
    one=lambda a: pl.BlockSpec(a.shape,lambda j:(0,)*len(a.shape),pipeline_mode=pl.Buffered(1))
    S=jax.ShapeDtypeStruct; sem=pltpu.SemaphoreType.DMA
    outs=[S((T,D),BF),S((T,D),F32),S((T,D),BF),S((T,128),BF),S((D,D),BF),S((D,D),BF),S((D,D),BF)]
    tail=[S((8,D),F32),S((C,sizes[-1],WIDE),BF)]
    return pl.pallas_call(functools.partial(mid_kernel,n,chunks,TILES),grid=(TILES,),
        in_specs=[one(x),one(cot),one(att),one(wo),one(vec),pl.BlockSpec((D,FT),lambda j:(0,j)),pl.BlockSpec((FT,D),lambda j:(j,0)),pl.BlockSpec((1,FT),lambda j:(0,j))],
        out_specs=[one(o) for o in outs]+[pl.BlockSpec((1,FT),lambda j:(0,j))]+[one(o) for o in tail],
        out_shape=outs+[S((1,FF),F32)]+tail,
        scratch_shapes=[pltpu.VMEM((T,D),F32),pltpu.VMEM((T,D),BF),pltpu.VMEM((D,T),BF),pltpu.VMEM((T,D),F32),pltpu.VMEM((T,D),F32),
            pltpu.VMEM((T,FT),BF),pltpu.VMEM((T,FT),BF),
            pltpu.VMEM((C,SIDE,WIDE),BF),pltpu.VMEM((C,sum(sizes[1:]),WIDE),BF),sem((C,bits)),sem((C,bits))],
        compiler_params=pltpu.CompilerParams(collective_id=collective_id,has_side_effects=True,vmem_limit_bytes=64<<20),name="feed_forward")(x,cot,att,wo,vec,wu,wd,ub)


def from_partner(block, axis, stride):
    count = lax.axis_size(axis)
    route = []
    for low in range(count):
        high = low | 1 << stride
        if high != low and high < count:
            route += [(low, high), (high, low)]
    return lax.ppermute(block, axis, route)


def layer_norm(values, norm_gain, norm_shift):
    center = values - jnp.mean(values, axis=-1, keepdims=True)
    spread = jnp.mean(center * center, axis=-1, keepdims=True)
    return center * lax.rsqrt(spread + EPSILON) * norm_gain + norm_shift


def norm_back(values, norm_gain, norm_shift, upstream):
    unused, pull_back = jax.vjp(layer_norm, values, norm_gain, norm_shift)
    return pull_back(upstream)


def gelu_exact(values):
    return jax.nn.gelu(values, approximate=False)


def gelu_back(values, upstream):
    unused, pull_back = jax.vjp(gelu_exact, values)
    return pull_back(upstream)[0]


def prepare(segment_ids, box_cells, table, is_vision):
    cell = (box_cells[:, 0] * 16 + box_cells[:, 1]).reshape(-1)
    cells = jnp.arange(256)
    e = (cell[:, None] == cells[None]).astype(BF)
    et = (cells[:, None] == cell[None]).astype(BF)
    lane = jnp.arange(128)
    same = segment_ids.reshape(-1)[:, None] == lane[None] - 64
    inside = (lane >= 64) & (lane < 68)
    qseg = same.astype(BF)
    kseg = jnp.where(inside[None] & ~same & jnp.logical_not(is_vision), MASKED, 0.0).astype(BF)
    return e, et, qseg, kseg


def code_onehot():
    c = jnp.arange(65536)
    step_x = jnp.minimum(jnp.abs(c // 4096 - (c // 16) % 16), GRID - 1)
    step_y = jnp.minimum(jnp.abs((c // 256) % 16 - c % 16), GRID - 1)
    return ((step_x * GRID + step_y)[None] == jnp.arange(GRID * GRID)[:, None]).astype(BF)


def on_device(features, cotangent, segment_ids, box_cells, ln_gain, ln_shift, w_qkv, attn_bias,
              distance_table, w_out, w_up, up_bias, w_down, down_bias):
    rows, length, width = features.shape[1:]
    tokens = rows * length
    heads = distance_table.shape[2]
    is_vision = lax.axis_index("stream") != 0
    norm_gains, norm_shifts = ln_gain[0], ln_shift[0]
    bias_rows = attn_bias[0]
    qkv_weight, out_weight, up_weight, down_weight = w_qkv[0], w_out[0], w_up[0], w_down[0]
    plain_in = features[0].reshape(tokens, width).astype(jnp.float32)
    normed = layer_norm(plain_in, norm_gains[0], norm_shifts[0]).astype(BF)
    combined = jnp.dot(normed, qkv_weight, preferred_element_type=jnp.float32)
    queries = (combined[:, :width] + bias_rows[0]).astype(BF) * BF(0.125)
    key_part = combined[:, width:2 * width].astype(BF)
    value_part = (combined[:, 2 * width:] + bias_rows[1]).astype(BF)
    partner_k = from_partner(key_part, "stream", 0)
    partner_v = from_partner(value_part, "stream", 0)
    e, et, qseg, kseg = prepare(segment_ids, box_cells[0], distance_table[0], is_vision)
    onehot = code_onehot()
    bt = jnp.dot(distance_table[0].T.astype(BF), onehot, preferred_element_type=jnp.float32).astype(BF).reshape(heads, 256, 256)
    attended, qmisc = fwd(queries, key_part, partner_k, value_part, partner_v, e, bt, qseg, kseg, length)
    vec = jnp.concatenate([bias_rows[2:3], norm_gains[1:2], norm_shifts[1:2], down_bias, jnp.zeros((4, width), F32)])
    q_send, m_send = lax.optimization_barrier((queries, qmisc))
    partner_q = from_partner(q_send, "stream", 0)
    partner_m = from_partner(m_send, "stream", 0)
    group = lax.axis_size("batch")
    (output, grad_middle, grad_attended, dmisc, grad_out, grad_up, grad_down, grad_up_bias, small_mid, segs) = mid(
        features[0].reshape(tokens, width), cotangent[0].reshape(tokens, width), attended, out_weight, vec,
        up_weight, down_weight, up_bias, group, 5)
    output = output.reshape(1, rows, length, width)
    small_up = grad_up_bias.reshape(-1, 128)
    early = jnp.concatenate([small_mid.reshape(-1, 128), small_up])
    vec_one = jnp.concatenate([norm_gains[0:1], norm_shifts[0:1], jnp.zeros((6, width), F32)])
    input_grad, small_a, small_b, sum_up, sum_down, sum_out, sum_qkv = back(
        queries, key_part, partner_k, value_part, partner_v, grad_attended, dmisc, qmisc, e, et, bt, kseg,
        partner_q, partner_m, features[0].reshape(tokens, width), qkv_weight, grad_middle, vec_one, early,
        segs, [grad_up, grad_down, grad_out], up_weight.shape[1], length, group, 4)
    input_grad = input_grad.reshape(1, rows, length, width)
    tab_rows = 16 * heads
    by_gap = small_a[:tab_rows, :16].reshape(heads, 2, GRID, 16)
    turn = jnp.arange(16)
    reach = jnp.minimum(jnp.stack([turn, 16 - turn]), GRID - 1)
    near = (reach[:, :, None] == jnp.arange(GRID)).astype(F32)
    dist = jnp.einsum("hpyd,pdx->xyh", by_gap, near, precision=lax.Precision.HIGHEST).reshape(1, GRID * GRID, heads)
    mid_sums = small_a[tab_rows:tab_rows + 8 * width // 128].reshape(8, width)
    upb = small_a[tab_rows + 8 * width // 128:].reshape(1, -1)
    last = small_b.reshape(4, width)
    gain = jnp.stack([last[0], mid_sums[0]])[None]
    shift = jnp.stack([last[1], mid_sums[1]])[None]
    bias = jnp.stack([last[2], last[3], mid_sums[2]])[None]
    downb = mid_sums[3][None]
    f32 = lambda a: a.astype(jnp.float32)[None]
    return (output, input_grad, gain, shift, f32(sum_qkv), bias, dist, f32(sum_out), f32(sum_up), upb, f32(sum_down), downb)


def solution(mesh):
    in_specs = (
        P("stream", "batch", None, None),
        P("stream", "batch", None, None),
        P("batch", None),
        P("stream", "batch", None, None),
        P("stream", None, None),
        P("stream", None, None),
        P("stream", None, None),
        P("stream", None, None),
        P("stream", None, None),
        P("stream", None, None),
        P("stream", None, None),
        P("stream", None),
        P("stream", None, None),
        P("stream", None),
    )
    out_specs = (
        P("stream", "batch", None, None),
        P("stream", "batch", None, None),
        P("stream", None, None),
        P("stream", None, None),
        P("stream", None, None),
        P("stream", None, None),
        P("stream", None, None),
        P("stream", None, None),
        P("stream", None, None),
        P("stream", None),
        P("stream", None, None),
        P("stream", None),
    )
    return jax.shard_map(
        on_device, mesh=mesh, in_specs=in_specs, out_specs=out_specs, check_vma=False
    )
```

```python
import functools
import jax
import jax.numpy as jnp
from jax import lax
from jax.experimental import pallas as pl
from jax.experimental.pallas import tpu as pltpu
from jax.sharding import PartitionSpec as P

GRID = 8
EPSILON = 1e-05
MASKED = -1000000000.0

NT=(((1,),(1,)),((),())); NN=(((1,),(0,)),((),())); TN=(((0,),(0,)),((),()))
def mm(a,b,dn=NN): return lax.dot_general(a,b,dn,preferred_element_type=jnp.float32)
BF=jnp.bfloat16

def three(x):
    hi=x.astype(BF); r=x-hi.astype(jnp.float32); mid=r.astype(BF); lo=(r-mid.astype(jnp.float32)).astype(BF)
    return hi,mid,lo

def fwd_kernel(CQ, q_ref,kn_ref,kf_ref,vn_ref,vf_ref,e_ref,b_ref,qseg_ref,kseg_ref,o_ref,qm_ref):
    pair=pl.program_id(1)
    L=q_ref.shape[0]
    lane=lax.broadcasted_iota(jnp.int32,(1,128),1)
    @pl.when(pair==0)
    def _():
        qm_ref[...]=qseg_ref[...]
    outs=[None]*(L//CQ)
    for hh in range(2):
        mh=(lane<64) if hh==0 else (lane>=64)
        h=2*pair+hh
        C=mm(e_ref[...],b_ref[hh]).astype(BF)
        kx=jnp.concatenate([kn_ref[...],C,kseg_ref[...]],axis=1)
        kf=kf_ref[...]
        one=jnp.ones((),BF); zero=jnp.zeros((),BF)
        vnx=jnp.where(mh,vn_ref[...],one); vfx=jnp.where(mh,vf_ref[...],one)
        for c in range(L//CQ):
            sl=slice(c*CQ,(c+1)*CQ)
            qm=jnp.where(mh,q_ref[sl,:],zero)
            qx=jnp.concatenate([qm,e_ref[sl,:],qseg_ref[sl,:]],axis=1)
            sn=mm(qx,kx,NT); sf=mm(qm,kf,NT)
            m=jnp.maximum(jnp.max(sn,axis=1,keepdims=True),jnp.max(sf,axis=1,keepdims=True))
            pn=jnp.exp(sn-m).astype(BF); pf=jnp.exp(sf-m).astype(BF)
            o=mm(pn,vnx)+mm(pf,vfx)
            l=pltpu.roll(o,64,1)
            on=o/l
            outs[c]=on if hh==0 else jnp.where(mh,on,outs[c])
            lse=-(m+jnp.log(jnp.where(mh,l,o)))
            hi,mid,lo=three(lse)
            cur=qm_ref[sl,:]
            cur=jnp.where(lane==3*h,hi,cur); cur=jnp.where(lane==3*h+1,mid,cur); cur=jnp.where(lane==3*h+2,lo,cur)
            qm_ref[sl,:]=cur
    for c in range(L//CQ):
        o_ref[c*CQ:(c+1)*CQ,:]=outs[c].astype(BF)

def fwd(q,kn,kf,vn,vf,e,bt,qseg,kseg,L,CQ=512):
    T=q.shape[0]; R=T//L; NP=q.shape[1]//128
    blk=pl.BlockSpec((L,128),lambda r,p:(r,p))
    row=lambda w: pl.BlockSpec((L,w),lambda r,p:(r,0))
    return pl.pallas_call(functools.partial(fwd_kernel,CQ),grid=(R,NP),
        in_specs=[blk]*5+[row(256),pl.BlockSpec((2,256,256),lambda r,p:(p,0,0)),row(128),row(128)],
        out_specs=[blk,row(128)],
        out_shape=[jax.ShapeDtypeStruct(q.shape,BF),jax.ShapeDtypeStruct((T,128),BF)],
        compiler_params=pltpu.CompilerParams(vmem_limit_bytes=48<<20),name="att_fwd")(q,kn,kf,vn,vf,e,bt,qseg,kseg)


F32=jnp.float32


MESH=pl.DeviceIdType.MESH
SIDE=768
WIDE=384
LAG=3
STEP=48

def bit_order(n, c):
    plain=list(range(n.bit_length()-1))
    other=[0]+plain[2:]+[1] if len(plain)>2 else plain
    return other if c%6==3 else plain

def plan_of(bits, rows):
    sizes=[rows]
    for _ in range(bits):
        m=sizes[-1]
        sizes.append(m//2 if m%32==0 else m)
    return sizes

def place(me, b):
    bit=(me//(1<<b))%2
    return bit, me+(1-2*bit)*(1<<b)

def rows_at(off, size):
    return pl.ds(off if isinstance(off,int) else pl.multiple_of(off,16),size)

class Engine:
    def __init__(self, n, me, chunks, x, recv, segs, sums, ss, rs, os):
        self.me,self.chunks=me,chunks
        self.x,self.recv,self.segs,self.sums=x,recv,segs,sums
        self.ss,self.rs,self.os=ss,rs,os
        self.bits=n.bit_length()-1
        self.sizes=plan_of(self.bits,SIDE)
        self.offs=[sum(self.sizes[1:s+1]) for s in range(self.bits+1)]
        self.n=n

    def seg(self,c,upto):
        order=bit_order(self.n,self.chunks[c]["kind"]); off=0
        for s in range(upto):
            if self.sizes[s+1]!=self.sizes[s]:
                off=off+place(self.me,order[s])[0]*self.sizes[s+1]
        return off,self.sizes[upto]

    def out(self,c,off,m):
        a,i,k=self.chunks[c]["to"]
        return self.sums[a].at[rows_at(i*SIDE+off,m),pl.ds(k*WIDE,WIDE)]

    def final(self,c):
        off,m=self.seg(c,self.bits)
        ch=self.chunks[c]
        if ch["first"]: return self.segs.at[ch["seg"]]
        return self.x.at[ch["slot"],rows_at(off,m)]

    def copy(self,c,stage):
        B,sizes,ch=self.bits,self.sizes,self.chunks[c]
        order=bit_order(self.n,ch["kind"])
        if stage<B:
            bit,partner=place(self.me,order[stage])
            off,m=self.seg(c,stage)
            if sizes[stage+1]!=m:
                src=self.x.at[ch["slot"],rows_at(off+(1-bit)*(m//2),m//2)]
            else:
                src=self.x.at[ch["slot"],rows_at(off,m)]
            dst=self.recv.at[ch["land"],pl.ds(self.offs[stage],sizes[stage+1])]
        else:
            s=2*B-1-stage
            if sizes[s+1]==sizes[s]:
                return None
            partner=place(self.me,order[s])[1]
            off,m=self.seg(c,s+1)
            dst=self.out(c,off,m)
            src=self.final(c) if stage==B else dst
        return pltpu.make_async_remote_copy(src,dst,self.ss.at[c,stage],self.rs.at[c,stage],
            device_id={"batch":partner},device_id_type=MESH)

    def keep(self,c):
        off,m=self.seg(c,self.bits)
        return pltpu.make_async_copy(self.final(c),self.out(c,off,m),self.os.at[c])

    def start(self,c,stage):
        if stage==self.bits:
            self.keep(c).start()
        d=self.copy(c,stage)
        if d is not None: d.start()

    def finish(self,c,stage):
        d=self.copy(c,stage)
        if d is not None: d.wait()
        if stage==self.bits:
            self.keep(c).wait()
        if stage<self.bits:
            off,m=self.seg(c,stage+1)
            ro=self.offs[stage]; x,recv=self.x,self.recv
            h,land=self.chunks[c]["slot"],self.chunks[c]["land"]
            def body(i,_):
                at=rows_at(off+i*STEP,STEP)
                more=recv[land,pl.ds(pl.multiple_of(ro+i*STEP,16),STEP)]
                x[h,at]=(x[h,at].astype(F32)+more.astype(F32)).astype(BF)
                return 0
            lax.fori_loop(0,m//STEP,body,0)
            if stage==self.bits-1 and self.chunks[c]["last"]==self.bits:
                self.segs[self.chunks[c]["seg"]]=x[h,rows_at(off,m)]

    def times(self,c):
        ch=self.chunks[c]
        order=bit_order(self.n,ch["kind"]); order=order+order[::-1]
        at=[ch["entry"]]
        for s in range(ch["first"],ch["last"]): at.append(at[-1]+(1 if order[s]==0 else LAG))
        return at

    def slot(self,t,load):
        todo=[]
        for c in range(len(self.chunks)):
            at=self.times(c)
            if t in at:
                todo.append((self.chunks[c]["entry"],c,self.chunks[c]["first"]+at.index(t)))
        for _,c,s in sorted(todo):
            ch=self.chunks[c]
            if s==ch["first"]: load(c)
            else: self.finish(c,s-1)
            if s<ch["last"]: self.start(c,s)

    def end(self):
        return 1+max(self.times(c)[-1] for c in range(len(self.chunks)))

def small_copy(me,x,recv,ss,rs,s):
    return pltpu.make_async_remote_copy(x.at[s],recv.at[s],ss.at[s],rs.at[s],device_id={"batch":place(me,s)[1]},device_id_type=MESH)

def back_kernel(n, NP, R, chunks, loads, cuts,
               q_ref,kn_ref,kf_ref,vn_ref,vf_ref,do_ref,dm_ref,qm_ref,e_ref,et_ref,b_ref,kseg_ref,qf_ref,qmf_ref,
               feat_ref,wqkv_ref,gm_ref,vec_ref,early_ref,
               do_any,dm_any,gu_any,gd_any,go_any,
               ig_ref,small_ref,su_any,sd_any,so_any,sq_any,
               dof,dmf,gmix,nt_s,g_s,tab,x,recv,ax,arecv,in_sem,out_sem,ss,rs,xs_sem,xr_sem,a_ss,a_rs):
    step=pl.program_id(0)
    per=NP*R
    second=(step>=per)&(step<2*per)
    inner=step%per; pair=inner//R; r=inner%R
    L=q_ref.shape[0]; T=feat_ref.shape[0]; D=feat_ref.shape[1]
    me=lax.axis_index("batch"); other={"stream":1-lax.axis_index("stream")}
    lane=lax.broadcasted_iota(jnp.int32,(1,128),1)
    zero=jnp.zeros((),BF)
    RC=256
    grads=(gu_any,gd_any,go_any)
    eng=Engine(n,me,chunks,x,recv,None,(su_any,sd_any,so_any,sq_any),ss,rs,out_sem)
    B=eng.bits
    q_set,mid_set,end_set=[[c for c in range(len(chunks)) if chunks[c].get("set")==i] for i in range(3)]
    def load(c):
        a,i,k=loads[c]
        return pltpu.make_async_copy(grads[a].at[pl.ds(i*SIDE,SIDE),pl.ds(k*WIDE,WIDE)],x.at[chunks[c]["slot"]],in_sem.at[c])
    def ready(c):
        if c in loads: load(c).wait()
    def across():
        res=[pltpu.make_async_remote_copy(dm_any,dmf,xs_sem.at[NP],xr_sem.at[NP],device_id=other,device_id_type=MESH)]
        for p in range(NP):
            res.append(pltpu.make_async_remote_copy(do_any.at[:,pl.ds(p*128,128)],dof.at[p],xs_sem.at[p],xr_sem.at[p],device_id=other,device_id_type=MESH))
        return res

    @pl.when(step==0)
    def _():
        sem=pltpu.get_barrier_semaphore()
        for b in range(B):
            pl.semaphore_signal(sem,inc=1,device_id={"batch":place(me,b)[1]},device_id_type=MESH)
        pl.semaphore_signal(sem,inc=1,device_id=other,device_id_type=MESH)
        for c in loads: load(c).start()
        pl.semaphore_wait(sem,B+1)
        for d in across(): d.start()
    def spread(lo,hi,parts): return [lo+(hi-lo)*i//parts for i in range(parts)]
    edges=spread(0,cuts[0],2*per)+spread(cuts[0],cuts[1],per)+spread(cuts[1],cuts[2],per)+[cuts[2]]
    def form(c):
        a,i,k=chunks[c]["to"]
        x[chunks[c]["slot"]]=mm(nt_s[i*SIDE:(i+1)*SIDE,:],gmix[:,k*WIDE:(k+1)*WIDE]).astype(BF)
    def tick(half):
        for k in range(2*per):
            i=k*2+half
            group=q_set if i==2*per else mid_set if i==3*per else []
            if edges[i]==edges[i+1] and not group: continue
            @pl.when(step==k)
            def _():
                if i==2*per:
                    for j in range(T//RC):
                        sl=slice(j*RC,(j+1)*RC)
                        nrm,_=norm_parts(feat_ref[sl,:].astype(F32))
                        nt_s[:,sl]=(nrm*vec_ref[0:1,:]+vec_ref[1:2,:]).astype(BF).T
                for c in group: form(c)
                for t in range(edges[i],edges[i+1]): eng.slot(t,ready)
    def half_of(hh):
        return (lane<64) if hh==0 else (lane>=64)
    def ones_of(h):
        return jnp.where((lane>=3*h)&(lane<3*h+3),1.0,0.0)
    add=lambda a,b: b if a is None else a+b
    def cols(part): return pl.ds(pl.multiple_of(part*D+pair*128,128),128)
    at=pl.ds(pl.multiple_of(r*L,L),L)

    tick(0)
    @pl.when(step<per)
    def _():
        dkn=None; dvn=None; dq=None
        for hh in range(2):
            mh=half_of(hh); h=2*pair+hh
            ones_h=ones_of(h); ones_b=jnp.broadcast_to(ones_h.astype(BF),(L,128))
            qm=jnp.where(mh,q_ref[...],zero); dom=jnp.where(mh,do_ref[...],zero)
            C_h=mm(e_ref[...],b_ref[hh]).astype(BF)
            qx=jnp.concatenate([qm,e_ref[...],qm_ref[...]],axis=1)
            dox=jnp.concatenate([dom,dm_ref[...]],axis=1)
            kseg=(kseg_ref[...].astype(F32)+ones_h).astype(BF)
            p=jnp.exp(mm(jnp.concatenate([kn_ref[...],C_h,kseg],axis=1),qx,NT))
            ds=(p*mm(jnp.concatenate([vn_ref[...],ones_b],axis=1),dox,NT)).astype(BF)
            dvn=add(dvn,mm(p.astype(BF),dom))
            t=mm(ds,jnp.concatenate([qm,e_ref[...]],axis=1))
            dkn=add(dkn,t[:,:128])
            g=mm(et_ref[...],t[:,128:].astype(BF))
            dq=add(dq,mm(ds,jnp.where(mh,kn_ref[...],zero),TN))
            p=jnp.exp(mm(jnp.concatenate([kf_ref[...],ones_b],axis=1),jnp.concatenate([qm,qm_ref[...]],axis=1),NT))
            ds=(p*mm(jnp.concatenate([vf_ref[...],ones_b],axis=1),dox,NT)).astype(BF)
            dq=add(dq,mm(ds,jnp.where(mh,kf_ref[...],zero),TN))
            @pl.when(r==0)
            def _(): g_s[hh]=g
            @pl.when(r!=0)
            def _(): g_s[hh]+=g
        gmix[at,cols(0)]=(dq*0.125).astype(BF)
        gmix[at,cols(1)]=dkn.astype(BF); gmix[at,cols(2)]=dvn.astype(BF)
    @pl.when((step<per)&(r==R-1))
    def _():
        turn=lax.broadcasted_iota(jnp.int32,(1,256),1)
        gap=jnp.minimum(jnp.abs(lax.broadcasted_iota(jnp.int32,(16,256),0)-turn%16),7)
        for hh in range(2):
            ahead=None; behind=None
            for i in range(16):
                blk=g_s[hh,16*i:16*i+16,:]
                if i: blk=pltpu.roll(blk,256-16*i,1)
                ahead=add(ahead,jnp.where(turn<256-16*i,blk,0.0))
                behind=add(behind,jnp.where(turn<256-16*i,0.0,blk))
            sums=[colsum(jnp.where(gap==k,v,0.0)) for v in (ahead,behind) for k in range(8)]
            tab[pl.ds(pl.multiple_of((2*pair+hh)*16,16),16),:]=jnp.concatenate(sums,axis=0)
    tick(1)
    @pl.when(step==per)
    def _():
        for d in across(): d.wait_recv()
    @pl.when(second)
    def _():
        dk=gmix[at,cols(1)].astype(F32); dv=gmix[at,cols(2)].astype(F32)
        for hh in range(2):
            mh=half_of(hh); h=2*pair+hh
            ones_b=jnp.broadcast_to(ones_of(h).astype(BF),(L,128))
            qm=jnp.where(mh,qf_ref[...],zero); dom=jnp.where(mh,dof[pair,at],zero)
            p=jnp.exp(mm(jnp.concatenate([kn_ref[...],ones_b],axis=1),jnp.concatenate([qm,qmf_ref[...]],axis=1),NT))
            ds=(p*mm(jnp.concatenate([vn_ref[...],ones_b],axis=1),jnp.concatenate([dom,dmf[at]],axis=1),NT)).astype(BF)
            dv=dv+mm(p.astype(BF),dom)
            dk=dk+mm(ds,qm)
        gmix[at,cols(1)]=dk.astype(BF); gmix[at,cols(2)]=dv.astype(BF)
    @pl.when(step==2*per)
    def _():
        now=cuts[2]
        for c in end_set:
            form(c); eng.slot(now,ready); now+=1
        gain=0.0; shift=0.0; qb=0.0; vb=0.0
        for i in range(T//RC):
            sl=slice(i*RC,(i+1)*RC)
            g=mm(gmix[sl,:],wqkv_ref[...],NT)
            nrm,inv=norm_parts(feat_ref[sl,:].astype(F32))
            gain=gain+colsum(g*nrm); shift=shift+colsum(g)
            qb=qb+colsum(gmix[sl,:D].astype(F32)); vb=vb+colsum(gmix[sl,2*D:].astype(F32))
            qg=g*vec_ref[0:1,:]
            ig_ref[sl,:]=(gm_ref[sl,:]+(qg-jnp.mean(qg,axis=1,keepdims=True)-nrm*jnp.mean(qg*nrm,axis=1,keepdims=True))*inv).astype(BF)
            eng.slot(now,ready); now+=1
        w=D//128; base=2*NP*16+early_ref.shape[0]
        for i,v in enumerate((gain,shift,qb,vb)):
            for k in range(w): ax[0,base+i*w+k:base+i*w+k+1,:]=v[:,k*128:(k+1)*128]
        put=(lax.broadcasted_iota(jnp.int32,(256,128),1)==lax.broadcasted_iota(jnp.int32,(256,128),0)//16).astype(BF)
        ax[0,:2*NP*16]=sum(mm(v,put) for v in three(tab[...]))
        ax[0,2*NP*16:base]=early_ref[...]
        small_copy(me,ax,arecv,a_ss,a_rs,0).start()
        done=1
        for t in range(now,max(eng.end(),now+LAG*B)):
            eng.slot(t,ready)
            if (t-now)%LAG==LAG-1 and done<=B:
                small_copy(me,ax,arecv,a_ss,a_rs,done-1).wait()
                ax[done]=ax[done-1]+arecv[done-1]
                if done<B: small_copy(me,ax,arecv,a_ss,a_rs,done).start()
                done+=1
        assert done==B+1
        small_ref[...]=ax[B]
        for d in across(): d.wait_send()

def back(q,kn,kf,vn,vf,do,dm,qmisc,e,et,bt,kseg,qf,qmf,feat,wqkv,gm,vec,early,grads,L,n,collective_id):
    T,D=q.shape; R=T//L; NP=D//128; per=R*NP
    def one(step): i=jnp.minimum(step,per-1); return i%R,i//R
    def cyc(step): i=jnp.minimum(step,2*per-1)%per; return i%R,i//R
    def two(step): i=jnp.clip(step-per,0,per-1); return i%R,i//R
    blk=lambda f: pl.BlockSpec((L,128),f)
    row=lambda w,f: pl.BlockSpec((L,w),lambda s:(f(s)[0],0))
    full=lambda a: pl.BlockSpec(a.shape,lambda s:(0,)*len(a.shape),pipeline_mode=pl.Buffered(1))
    any_=pl.BlockSpec(memory_space=pl.ANY)
    S=jax.ShapeDtypeStruct; sem=pltpu.SemaphoreType.DMA
    bits=n.bit_length()-1; per_side=D//WIDE; full_ff=grads[0].shape[1]; tiles=full_ff//SIDE; early_tiles=0
    count=per_side*(2*tiles+1)
    cuts=(count,count+per_side,count+2*per_side)
    chunks=[]; loads={}
    def chunk(to,entry,**more):
        ch=dict(to=to,entry=entry,kind=len(chunks),first=0,last=2*bits); ch.update(more); chunks.append(ch)
    late=[]
    for t in range(early_tiles,tiles):
        late+=[(0,0,t*per_side+k) for k in range(per_side)]+[(1,t,k) for k in range(per_side)]
    late+=[(2,0,k) for k in range(per_side)]
    for i,(a,r,k) in enumerate(late):
        loads[len(chunks)]=(a,r-early_tiles if a==1 else 0,k-early_tiles*per_side if a==0 else k)
        chunk((a,r,k),i,slot=i,land=i)
    place_of=[p for t in range(early_tiles) for p in [(0,0,t*per_side+k) for k in range(per_side)]+[(1,t,k) for k in range(per_side)]]
    for i,p in enumerate(place_of):
        chunk(p,2*i+1,first=bits,seg=i,kind=i)
    at=len(loads)
    half=per_side//2
    for g,group in enumerate(([k for k in range(per_side)],[per_side+k for k in range(half)]+[2*per_side+k for k in range(half)],
                  [per_side+k for k in range(half,per_side)]+[2*per_side+k for k in range(half,per_side)])):
        for i,k in enumerate(group):
            chunk((3,0,k),cuts[g]+i,slot=at,land=at,set=g); at+=1
    C=len(chunks)
    rows=sum(plan_of(bits,SIDE)[1:])
    asmall=(2*NP*16+early.shape[0]+4*D//128,128)
    outs=[S((T,D),BF),S(asmall,F32)]
    sums=[S((D,full_ff),BF),S((full_ff,D),BF),S((D,D),BF),S(wqkv.shape,BF)]
    return pl.pallas_call(functools.partial(back_kernel,n,NP,R,chunks,loads,cuts),grid=(2*per+1,),
        in_specs=[blk(one),blk(cyc),blk(one),blk(cyc),blk(one),blk(one),row(128,one),row(128,one),row(256,one),
                  pl.BlockSpec((256,L),lambda s:(0,one(s)[0])),pl.BlockSpec((2,256,256),lambda s:(one(s)[1],0,0)),row(128,one),blk(two),row(128,two),
                  full(feat),full(wqkv),full(gm),full(vec),full(early)]+[any_]*5,
        out_specs=[full(o) for o in outs]+[any_]*4,
        out_shape=outs+sums,
        scratch_shapes=[pltpu.VMEM((NP,T,128),BF),pltpu.VMEM((T,128),BF),pltpu.VMEM((T,3*D),BF),pltpu.VMEM((D,T),BF),pltpu.VMEM((2,256,256),F32),pltpu.VMEM((2*NP*16,256),F32),
            pltpu.VMEM((at,SIDE,WIDE),BF),pltpu.VMEM((at,rows,WIDE),BF),
            pltpu.VMEM((bits+1,)+asmall,F32),pltpu.VMEM((bits,)+asmall,F32),
            sem((C,)),sem((C,)),sem((C,2*bits)),sem((C,2*bits)),sem((NP+1,)),sem((NP+1,)),sem((bits,)),sem((bits,))],
        compiler_params=pltpu.CompilerParams(collective_id=collective_id,has_side_effects=True,vmem_limit_bytes=64<<20),
        name="att_bwd")(q,kn,kf,vn,vf,do,dm,qmisc,e,et,bt,kseg,qf,qmf,feat,wqkv,gm,vec,early,do,dm,*grads)


def gelu_both(u):
    a=jnp.abs(u)
    t=1.0/(1.0+a*(0.3275911*0.7071067811865476))
    ex=jnp.exp(u*u*-0.5)
    poly=((((1.061405429*t-1.453152027)*t+1.421413741)*t-0.284496736)*t+0.254829592)*t
    half=0.5*poly*ex
    cdf=jnp.where(u<0,half,1.0-half)
    return u*cdf, cdf+u*ex*0.3989422804014327

def norm_parts(v):
    center=v-jnp.mean(v,axis=1,keepdims=True)
    inv=lax.rsqrt(jnp.mean(center*center,axis=1,keepdims=True)+EPSILON)
    return center*inv,inv

def colsum(v): return jnp.sum(v,axis=0,keepdims=True)

def mid_kernel(RC, x_ref,cot_ref,att_ref,wo_ref,vec_ref,wu_ref,wd_ref,ub_ref,
               out_ref,gm_ref,do_ref,dm_ref,gwo_ref,gwu_ref,gwd_ref,gub_ref,small_ref,
               mid_s,nt_s,ntt_s,acc_s,gn_s):
    j=pl.program_id(0); T=x_ref.shape[0]; NTL=pl.num_programs(0)
    chunks=[slice(i*RC,(i+1)*RC) for i in range(T//RC)]
    @pl.when(j==0)
    def _():
        for sl in chunks:
            v=x_ref[sl,:].astype(F32)+mm(att_ref[sl,:],wo_ref[...])+vec_ref[0:1,:]
            mid_s[sl,:]=v
            n,_=norm_parts(v)
            nt=(n*vec_ref[1:2,:]+vec_ref[2:3,:]).astype(BF)
            nt_s[sl,:]=nt
            ntt_s[:,sl]=nt.T
            acc_s[sl,:]=v+vec_ref[3:4,:]
            gn_s[sl,:]=jnp.zeros_like(v)
    gub=0.0; gwd=0.0; gwu=0.0
    for sl in chunks:
        pre=mm(nt_s[sl,:],wu_ref[...])+ub_ref[...]
        act,slope=gelu_both(pre)
        act=act.astype(BF)
        gp=(mm(cot_ref[sl,:],wd_ref[...],NT)*slope).astype(BF)
        acc_s[sl,:]+=mm(act,wd_ref[...])
        gn_s[sl,:]+=mm(gp,wu_ref[...],NT)
        gub=gub+colsum(gp.astype(F32))
        gwd=gwd+mm(act,cot_ref[sl,:],TN)
        gwu=gwu+mm(ntt_s[:,sl],gp)
    gub_ref[...]=gub
    gwd_ref[...]=gwd.astype(BF); gwu_ref[...]=gwu.astype(BF)
    @pl.when(j==NTL-1)
    def _():
        g2=0.0; s2=0.0; ob=0.0; db=0.0; gwo=0.0
        row=lax.broadcasted_iota(jnp.int32,(x_ref.shape[1],128),0)//64
        col=lax.broadcasted_iota(jnp.int32,(x_ref.shape[1],128),1)
        pick=(row==col//3).astype(BF)
        lane=lax.broadcasted_iota(jnp.int32,(1,128),1)
        for sl in chunks:
            out_ref[sl,:]=acc_s[sl,:].astype(BF)
            n,inv=norm_parts(mid_s[sl,:])
            q=gn_s[sl,:]
            g2=g2+colsum(q*n); s2=s2+colsum(q)
            qg=q*vec_ref[1:2,:]
            cot=cot_ref[sl,:].astype(F32)
            db=db+colsum(cot)
            gm=cot+(qg-jnp.mean(qg,axis=1,keepdims=True)-n*jnp.mean(qg*n,axis=1,keepdims=True))*inv
            gm_ref[sl,:]=gm
            gb=gm.astype(BF)
            ob=ob+colsum(gb.astype(F32))
            do=mm(gb,wo_ref[...],NT).astype(BF)
            do_ref[sl,:]=do
            gwo=gwo+mm(att_ref[sl,:],gb,TN)
            prod=do.astype(F32)*att_ref[sl,:].astype(F32)
            hi=prod.astype(BF); lo=(prod-hi.astype(F32)).astype(BF)
            delta=-(mm(hi,pick)+mm(lo,pick))
            hi,md,lo=three(delta)
            dm_ref[sl,:]=jnp.where(lane>=36,jnp.zeros((),BF),jnp.where(lane%3==0,hi,jnp.where(lane%3==1,md,lo)))
        gwo_ref[...]=gwo.astype(BF)
        small_ref[0:1,:]=g2; small_ref[1:2,:]=s2; small_ref[2:3,:]=ob; small_ref[3:4,:]=db
        small_ref[4:8,:]=jnp.zeros((4,x_ref.shape[1]),F32)

def mid(x,cot,att,wo,vec,wu,wd,ub,FT=512,RC=256):
    T,D=x.shape; FF=wu.shape[1]
    full=lambda a: pl.BlockSpec(a.shape,lambda j:(0,0))
    S=jax.ShapeDtypeStruct
    fs=lambda *s: pl.BlockSpec(s,lambda j:(0,0))
    return pl.pallas_call(functools.partial(mid_kernel,RC),grid=(FF//FT,),
        in_specs=[full(x),full(cot),full(att),full(wo),full(vec),pl.BlockSpec((D,FT),lambda j:(0,j)),pl.BlockSpec((FT,D),lambda j:(j,0)),pl.BlockSpec((1,FT),lambda j:(0,j))],
        out_specs=[fs(T,D),fs(T,D),fs(T,D),fs(T,128),fs(D,D),pl.BlockSpec((D,FT),lambda j:(0,j)),pl.BlockSpec((FT,D),lambda j:(j,0)),pl.BlockSpec((1,FT),lambda j:(0,j)),fs(8,D)],
        out_shape=[S((T,D),BF),S((T,D),F32),S((T,D),BF),S((T,128),BF),S((D,D),BF),S((D,FF),BF),S((FF,D),BF),S((1,FF),F32),S((8,D),F32)],
        scratch_shapes=[pltpu.VMEM((T,D),F32),pltpu.VMEM((T,D),BF),pltpu.VMEM((D,T),BF),pltpu.VMEM((T,D),F32),pltpu.VMEM((T,D),F32)],
        compiler_params=pltpu.CompilerParams(vmem_limit_bytes=60<<20),name="feed_forward")(x,cot,att,wo,vec,wu,wd,ub)


def from_partner(block, axis, stride):
    count = lax.axis_size(axis)
    route = []
    for low in range(count):
        high = low | 1 << stride
        if high != low and high < count:
            route += [(low, high), (high, low)]
    return lax.ppermute(block, axis, route)


def layer_norm(values, norm_gain, norm_shift):
    center = values - jnp.mean(values, axis=-1, keepdims=True)
    spread = jnp.mean(center * center, axis=-1, keepdims=True)
    return center * lax.rsqrt(spread + EPSILON) * norm_gain + norm_shift


def norm_back(values, norm_gain, norm_shift, upstream):
    unused, pull_back = jax.vjp(layer_norm, values, norm_gain, norm_shift)
    return pull_back(upstream)


def gelu_exact(values):
    return jax.nn.gelu(values, approximate=False)


def gelu_back(values, upstream):
    unused, pull_back = jax.vjp(gelu_exact, values)
    return pull_back(upstream)[0]


def prepare(segment_ids, box_cells, table, is_vision):
    cell = (box_cells[:, 0] * 16 + box_cells[:, 1]).reshape(-1)
    cells = jnp.arange(256)
    e = (cell[:, None] == cells[None]).astype(BF)
    et = (cells[:, None] == cell[None]).astype(BF)
    lane = jnp.arange(128)
    same = segment_ids.reshape(-1)[:, None] == lane[None] - 64
    inside = (lane >= 64) & (lane < 68)
    qseg = same.astype(BF)
    kseg = jnp.where(inside[None] & ~same & jnp.logical_not(is_vision), MASKED, 0.0).astype(BF)
    return e, et, qseg, kseg


def code_onehot():
    c = jnp.arange(65536)
    step_x = jnp.minimum(jnp.abs(c // 4096 - (c // 16) % 16), GRID - 1)
    step_y = jnp.minimum(jnp.abs((c // 256) % 16 - c % 16), GRID - 1)
    return ((step_x * GRID + step_y)[None] == jnp.arange(GRID * GRID)[:, None]).astype(BF)


def on_device(features, cotangent, segment_ids, box_cells, ln_gain, ln_shift, w_qkv, attn_bias,
              distance_table, w_out, w_up, up_bias, w_down, down_bias):
    rows, length, width = features.shape[1:]
    tokens = rows * length
    heads = distance_table.shape[2]
    is_vision = lax.axis_index("stream") != 0
    norm_gains, norm_shifts = ln_gain[0], ln_shift[0]
    bias_rows = attn_bias[0]
    qkv_weight, out_weight, up_weight, down_weight = w_qkv[0], w_out[0], w_up[0], w_down[0]
    plain_in = features[0].reshape(tokens, width).astype(jnp.float32)
    normed = layer_norm(plain_in, norm_gains[0], norm_shifts[0]).astype(BF)
    combined = jnp.dot(normed, qkv_weight, preferred_element_type=jnp.float32)
    queries = (combined[:, :width] + bias_rows[0]).astype(BF) * BF(0.125)
    key_part = combined[:, width:2 * width].astype(BF)
    value_part = (combined[:, 2 * width:] + bias_rows[1]).astype(BF)
    partner_k = from_partner(key_part, "stream", 0)
    partner_v = from_partner(value_part, "stream", 0)
    e, et, qseg, kseg = prepare(segment_ids, box_cells[0], distance_table[0], is_vision)
    onehot = code_onehot()
    bt = jnp.dot(distance_table[0].T.astype(BF), onehot, preferred_element_type=jnp.float32).astype(BF).reshape(heads, 256, 256)
    attended, qmisc = fwd(queries, key_part, partner_k, value_part, partner_v, e, bt, qseg, kseg, length)
    vec = jnp.concatenate([bias_rows[2:3], norm_gains[1:2], norm_shifts[1:2], down_bias, jnp.zeros((4, width), F32)])
    q_send, m_send = lax.optimization_barrier((queries, qmisc))
    partner_q = from_partner(q_send, "stream", 0)
    partner_m = from_partner(m_send, "stream", 0)
    group = lax.axis_size("batch")
    (output, grad_middle, grad_attended, dmisc, grad_out, grad_up, grad_down, grad_up_bias, small_mid) = mid(
        features[0].reshape(tokens, width), cotangent[0].reshape(tokens, width), attended, out_weight, vec,
        up_weight, down_weight, up_bias)
    output = output.reshape(1, rows, length, width)
    small_up = grad_up_bias.reshape(-1, 128)
    early = jnp.concatenate([small_mid.reshape(-1, 128), small_up])
    vec_one = jnp.concatenate([norm_gains[0:1], norm_shifts[0:1], jnp.zeros((6, width), F32)])
    input_grad, small_a, sum_up, sum_down, sum_out, sum_qkv = back(
        queries, key_part, partner_k, value_part, partner_v, grad_attended, dmisc, qmisc, e, et, bt, kseg,
        partner_q, partner_m, features[0].reshape(tokens, width), qkv_weight, grad_middle, vec_one, early,
        [grad_up, grad_down, grad_out], length, group, 4)
    input_grad = input_grad.reshape(1, rows, length, width)
    tab_rows = 16 * heads
    by_gap = small_a[:tab_rows, :16].reshape(heads, 2, GRID, 16)
    turn = jnp.arange(16)
    reach = jnp.minimum(jnp.stack([turn, 16 - turn]), GRID - 1)
    near = (reach[:, :, None] == jnp.arange(GRID)).astype(F32)
    dist = jnp.einsum("hpyd,pdx->xyh", by_gap, near, precision=lax.Precision.HIGHEST).reshape(1, GRID * GRID, heads)
    mid_sums = small_a[tab_rows:tab_rows + 8 * width // 128].reshape(8, width)
    tail = small_a.shape[0] - 4 * width // 128
    upb = small_a[tab_rows + 8 * width // 128:tail].reshape(1, -1)
    last = small_a[tail:].reshape(4, width)
    gain = jnp.stack([last[0], mid_sums[0]])[None]
    shift = jnp.stack([last[1], mid_sums[1]])[None]
    bias = jnp.stack([last[2], last[3], mid_sums[2]])[None]
    downb = mid_sums[3][None]
    f32 = lambda a: a.astype(jnp.float32)[None]
    return (output, input_grad, gain, shift, f32(sum_qkv), bias, dist, f32(sum_out), f32(sum_up), upb, f32(sum_down), downb)


def solution(mesh):
    in_specs = (
        P("stream", "batch", None, None),
        P("stream", "batch", None, None),
        P("batch", None),
        P("stream", "batch", None, None),
        P("stream", None, None),
        P("stream", None, None),
        P("stream", None, None),
        P("stream", None, None),
        P("stream", None, None),
        P("stream", None, None),
        P("stream", None, None),
        P("stream", None),
        P("stream", None, None),
        P("stream", None),
    )
    out_specs = (
        P("stream", "batch", None, None),
        P("stream", "batch", None, None),
        P("stream", None, None),
        P("stream", None, None),
        P("stream", None, None),
        P("stream", None, None),
        P("stream", None, None),
        P("stream", None, None),
        P("stream", None, None),
        P("stream", None),
        P("stream", None, None),
        P("stream", None),
    )
    return jax.shard_map(
        on_device, mesh=mesh, in_specs=in_specs, out_specs=out_specs, check_vma=False
    )
```

```python
import functools
import jax
import jax.numpy as jnp
from jax import lax
from jax.experimental import pallas as pl
from jax.experimental.pallas import tpu as pltpu
from jax.sharding import PartitionSpec as P

GRID = 8
EPSILON = 1e-05
MASKED = -1000000000.0

NT=(((1,),(1,)),((),())); NN=(((1,),(0,)),((),())); TN=(((0,),(0,)),((),()))
def mm(a,b,dn=NN): return lax.dot_general(a,b,dn,preferred_element_type=jnp.float32)
BF=jnp.bfloat16

def three(x):
    hi=x.astype(BF); r=x-hi.astype(jnp.float32); mid=r.astype(BF); lo=(r-mid.astype(jnp.float32)).astype(BF)
    return hi,mid,lo


F32=jnp.float32


MESH=pl.DeviceIdType.MESH
SIDE=768
WIDE=384
LAG=3
STEP=48

def bit_order(n, c):
    plain=list(range(n.bit_length()-1))
    other=[0]+plain[2:]+[1] if len(plain)>2 else plain
    return other if c%6==3 else plain

def plan_of(bits, rows):
    sizes=[rows]
    for _ in range(bits):
        m=sizes[-1]
        sizes.append(m//2 if m%32==0 else m)
    return sizes

def place(me, b):
    bit=(me//(1<<b))%2
    return bit, me+(1-2*bit)*(1<<b)

def rows_at(off, size):
    return pl.ds(off if isinstance(off,int) else pl.multiple_of(off,16),size)

class Engine:
    def __init__(self, n, me, chunks, x, recv, segs, sums, ss, rs, os):
        self.me,self.chunks=me,chunks
        self.x,self.recv,self.segs,self.sums=x,recv,segs,sums
        self.ss,self.rs,self.os=ss,rs,os
        self.bits=n.bit_length()-1
        self.sizes=plan_of(self.bits,SIDE)
        self.offs=[sum(self.sizes[1:s+1]) for s in range(self.bits+1)]
        self.n=n

    def seg(self,c,upto):
        order=bit_order(self.n,self.chunks[c]["kind"]); off=0
        for s in range(upto):
            if self.sizes[s+1]!=self.sizes[s]:
                off=off+place(self.me,order[s])[0]*self.sizes[s+1]
        return off,self.sizes[upto]

    def out(self,c,off,m):
        a,i,k=self.chunks[c]["to"]
        return self.sums[a].at[rows_at(i*SIDE+off,m),pl.ds(k*WIDE,WIDE)]

    def final(self,c):
        off,m=self.seg(c,self.bits)
        ch=self.chunks[c]
        if ch["first"]: return self.segs.at[ch["seg"]]
        return self.x.at[ch["slot"],rows_at(off,m)]

    def copy(self,c,stage):
        B,sizes,ch=self.bits,self.sizes,self.chunks[c]
        order=bit_order(self.n,ch["kind"])
        if stage<B:
            bit,partner=place(self.me,order[stage])
            off,m=self.seg(c,stage)
            if sizes[stage+1]!=m:
                src=self.x.at[ch["slot"],rows_at(off+(1-bit)*(m//2),m//2)]
            else:
                src=self.x.at[ch["slot"],rows_at(off,m)]
            dst=self.recv.at[ch["land"],pl.ds(self.offs[stage],sizes[stage+1])]
        else:
            s=2*B-1-stage
            if sizes[s+1]==sizes[s]:
                return None
            partner=place(self.me,order[s])[1]
            off,m=self.seg(c,s+1)
            dst=self.out(c,off,m)
            src=self.final(c) if stage==B else dst
        return pltpu.make_async_remote_copy(src,dst,self.ss.at[c,stage],self.rs.at[c,stage],
            device_id={"batch":partner},device_id_type=MESH)

    def keep(self,c):
        off,m=self.seg(c,self.bits)
        return pltpu.make_async_copy(self.final(c),self.out(c,off,m),self.os.at[c])

    def start(self,c,stage):
        if stage==self.bits:
            self.keep(c).start()
        d=self.copy(c,stage)
        if d is not None: d.start()

    def finish(self,c,stage):
        d=self.copy(c,stage)
        if d is not None: d.wait()
        if stage==self.bits:
            self.keep(c).wait()
        if stage<self.bits:
            off,m=self.seg(c,stage+1)
            ro=self.offs[stage]; x,recv=self.x,self.recv
            h,land=self.chunks[c]["slot"],self.chunks[c]["land"]
            def body(i,_):
                at=rows_at(off+i*STEP,STEP)
                more=recv[land,pl.ds(pl.multiple_of(ro+i*STEP,16),STEP)]
                x[h,at]=(x[h,at].astype(F32)+more.astype(F32)).astype(BF)
                return 0
            lax.fori_loop(0,m//STEP,body,0)
            if stage==self.bits-1 and self.chunks[c]["last"]==self.bits:
                self.segs[self.chunks[c]["seg"]]=x[h,rows_at(off,m)]

    def times(self,c):
        ch=self.chunks[c]
        order=bit_order(self.n,ch["kind"]); order=order+order[::-1]
        at=[ch["entry"]]
        for s in range(ch["first"],ch["last"]): at.append(at[-1]+(1 if order[s]==0 else LAG))
        return at

    def slot(self,t,load):
        todo=[]
        for c in range(len(self.chunks)):
            at=self.times(c)
            if t in at:
                todo.append((self.chunks[c]["entry"],c,self.chunks[c]["first"]+at.index(t)))
        for _,c,s in sorted(todo):
            ch=self.chunks[c]
            if s==ch["first"]: load(c)
            else: self.finish(c,s-1)
            if s<ch["last"]: self.start(c,s)

    def end(self):
        return 1+max(self.times(c)[-1] for c in range(len(self.chunks)))

def small_copy(me,x,recv,ss,rs,s):
    return pltpu.make_async_remote_copy(x.at[s],recv.at[s],ss.at[s],rs.at[s],device_id={"batch":place(me,s)[1]},device_id_type=MESH)

def back_kernel(n, NP, R, chunks, loads, cuts,
               q_ref,kn_ref,kf_ref,vn_ref,vf_ref,do_ref,dm_ref,qm_ref,e_ref,et_ref,b_ref,kseg_ref,qf_ref,qmf_ref,
               feat_ref,wqkv_ref,gm_ref,vec_ref,early_ref,
               do_any,dm_any,gu_any,gd_any,go_any,
               ig_ref,small_ref,su_any,sd_any,so_any,sq_any,
               dof,dmf,gmix,nt_s,g_s,tab,x,recv,ax,arecv,in_sem,out_sem,ss,rs,xs_sem,xr_sem,a_ss,a_rs):
    step=pl.program_id(0)
    per=NP*R
    second=(step>=per)&(step<2*per)
    inner=step%per; pair=inner//R; r=inner%R
    L=q_ref.shape[0]; T=feat_ref.shape[0]; D=feat_ref.shape[1]
    me=lax.axis_index("batch"); other={"stream":1-lax.axis_index("stream")}
    lane=lax.broadcasted_iota(jnp.int32,(1,128),1)
    zero=jnp.zeros((),BF)
    RC=256
    grads=(gu_any,gd_any,go_any)
    eng=Engine(n,me,chunks,x,recv,None,(su_any,sd_any,so_any,sq_any),ss,rs,out_sem)
    B=eng.bits
    q_set,mid_set,end_set=[[c for c in range(len(chunks)) if chunks[c].get("set")==i] for i in range(3)]
    def load(c):
        a,i,k=loads[c]
        return pltpu.make_async_copy(grads[a].at[pl.ds(i*SIDE,SIDE),pl.ds(k*WIDE,WIDE)],x.at[chunks[c]["slot"]],in_sem.at[c])
    def ready(c):
        if c in loads: load(c).wait()
    def across():
        res=[pltpu.make_async_remote_copy(dm_any,dmf,xs_sem.at[NP],xr_sem.at[NP],device_id=other,device_id_type=MESH)]
        for p in range(NP):
            res.append(pltpu.make_async_remote_copy(do_any.at[:,pl.ds(p*128,128)],dof.at[p],xs_sem.at[p],xr_sem.at[p],device_id=other,device_id_type=MESH))
        return res

    @pl.when(step==0)
    def _():
        sem=pltpu.get_barrier_semaphore()
        for b in range(B):
            pl.semaphore_signal(sem,inc=1,device_id={"batch":place(me,b)[1]},device_id_type=MESH)
        pl.semaphore_signal(sem,inc=1,device_id=other,device_id_type=MESH)
        for c in loads: load(c).start()
        pl.semaphore_wait(sem,B+1)
        for d in across(): d.start()
    def spread(lo,hi,parts): return [lo+(hi-lo)*i//parts for i in range(parts)]
    edges=spread(0,cuts[0],2*per)+spread(cuts[0],cuts[1],per)+spread(cuts[1],cuts[2],per)+[cuts[2]]
    def form(c):
        a,i,k=chunks[c]["to"]
        x[chunks[c]["slot"]]=mm(nt_s[i*SIDE:(i+1)*SIDE,:],gmix[:,k*WIDE:(k+1)*WIDE]).astype(BF)
    def tick(half):
        for k in range(2*per):
            i=k*2+half
            group=q_set if i==2*per else mid_set if i==3*per else []
            if edges[i]==edges[i+1] and not group: continue
            @pl.when(step==k)
            def _():
                if i==2*per:
                    for j in range(T//RC):
                        sl=slice(j*RC,(j+1)*RC)
                        nrm,_=norm_parts(feat_ref[sl,:].astype(F32))
                        nt_s[:,sl]=(nrm*vec_ref[0:1,:]+vec_ref[1:2,:]).astype(BF).T
                for c in group: form(c)
                for t in range(edges[i],edges[i+1]): eng.slot(t,ready)
    def half_of(hh):
        return (lane<64) if hh==0 else (lane>=64)
    def ones_of(h):
        return jnp.where((lane>=3*h)&(lane<3*h+3),1.0,0.0)
    add=lambda a,b: b if a is None else a+b
    def cols(part): return pl.ds(pl.multiple_of(part*D+pair*128,128),128)
    at=pl.ds(pl.multiple_of(r*L,L),L)

    tick(0)
    @pl.when(step<per)
    def _():
        dkn=None; dvn=None; dq=None
        for hh in range(2):
            mh=half_of(hh); h=2*pair+hh
            ones_h=ones_of(h); ones_b=jnp.broadcast_to(ones_h.astype(BF),(L,128))
            qm=jnp.where(mh,q_ref[...],zero); dom=jnp.where(mh,do_ref[...],zero)
            C_h=mm(e_ref[...],b_ref[hh]).astype(BF)
            qx=jnp.concatenate([qm,e_ref[...],qm_ref[...]],axis=1)
            dox=jnp.concatenate([dom,dm_ref[...]],axis=1)
            kseg=(kseg_ref[...].astype(F32)+ones_h).astype(BF)
            p=jnp.exp(mm(jnp.concatenate([kn_ref[...],C_h,kseg],axis=1),qx,NT))
            ds=(p*mm(jnp.concatenate([vn_ref[...],ones_b],axis=1),dox,NT)).astype(BF)
            dvn=add(dvn,mm(p.astype(BF),dom))
            t=mm(ds,jnp.concatenate([qm,e_ref[...]],axis=1))
            dkn=add(dkn,t[:,:128])
            g=mm(et_ref[...],t[:,128:].astype(BF))
            dq=add(dq,mm(ds,jnp.where(mh,kn_ref[...],zero),TN))
            p=jnp.exp(mm(jnp.concatenate([kf_ref[...],ones_b],axis=1),jnp.concatenate([qm,qm_ref[...]],axis=1),NT))
            ds=(p*mm(jnp.concatenate([vf_ref[...],ones_b],axis=1),dox,NT)).astype(BF)
            dq=add(dq,mm(ds,jnp.where(mh,kf_ref[...],zero),TN))
            @pl.when(r==0)
            def _(): g_s[hh]=g
            @pl.when(r!=0)
            def _(): g_s[hh]+=g
        gmix[at,cols(0)]=(dq*0.125).astype(BF)
        gmix[at,cols(1)]=dkn.astype(BF); gmix[at,cols(2)]=dvn.astype(BF)
    @pl.when((step<per)&(r==R-1))
    def _():
        turn=lax.broadcasted_iota(jnp.int32,(1,256),1)
        gap=jnp.minimum(jnp.abs(lax.broadcasted_iota(jnp.int32,(16,256),0)-turn%16),7)
        for hh in range(2):
            ahead=None; behind=None
            for i in range(16):
                blk=g_s[hh,16*i:16*i+16,:]
                if i: blk=pltpu.roll(blk,256-16*i,1)
                ahead=add(ahead,jnp.where(turn<256-16*i,blk,0.0))
                behind=add(behind,jnp.where(turn<256-16*i,0.0,blk))
            sums=[colsum(jnp.where(gap==k,v,0.0)) for v in (ahead,behind) for k in range(8)]
            tab[pl.ds(pl.multiple_of((2*pair+hh)*16,16),16),:]=jnp.concatenate(sums,axis=0)
    tick(1)
    @pl.when(step==per)
    def _():
        for d in across(): d.wait_recv()
    @pl.when(second)
    def _():
        dk=gmix[at,cols(1)].astype(F32); dv=gmix[at,cols(2)].astype(F32)
        for hh in range(2):
            mh=half_of(hh); h=2*pair+hh
            ones_b=jnp.broadcast_to(ones_of(h).astype(BF),(L,128))
            qm=jnp.where(mh,qf_ref[...],zero); dom=jnp.where(mh,dof[pair,at],zero)
            p=jnp.exp(mm(jnp.concatenate([kn_ref[...],ones_b],axis=1),jnp.concatenate([qm,qmf_ref[...]],axis=1),NT))
            ds=(p*mm(jnp.concatenate([vn_ref[...],ones_b],axis=1),jnp.concatenate([dom,dmf[at]],axis=1),NT)).astype(BF)
            dv=dv+mm(p.astype(BF),dom)
            dk=dk+mm(ds,qm)
        gmix[at,cols(1)]=dk.astype(BF); gmix[at,cols(2)]=dv.astype(BF)
    @pl.when(step==2*per)
    def _():
        now=cuts[2]
        for c in end_set:
            form(c); eng.slot(now,ready); now+=1
        gain=0.0; shift=0.0; qb=0.0; vb=0.0
        for i in range(T//RC):
            sl=slice(i*RC,(i+1)*RC)
            g=mm(gmix[sl,:],wqkv_ref[...],NT)
            nrm,inv=norm_parts(feat_ref[sl,:].astype(F32))
            gain=gain+colsum(g*nrm); shift=shift+colsum(g)
            qb=qb+colsum(gmix[sl,:D].astype(F32)); vb=vb+colsum(gmix[sl,2*D:].astype(F32))
            qg=g*vec_ref[0:1,:]
            ig_ref[sl,:]=(gm_ref[sl,:]+(qg-jnp.mean(qg,axis=1,keepdims=True)-nrm*jnp.mean(qg*nrm,axis=1,keepdims=True))*inv).astype(BF)
            eng.slot(now,ready); now+=1
        w=D//128; base=2*NP*16+early_ref.shape[0]
        for i,v in enumerate((gain,shift,qb,vb)):
            for k in range(w): ax[0,base+i*w+k:base+i*w+k+1,:]=v[:,k*128:(k+1)*128]
        put=(lax.broadcasted_iota(jnp.int32,(256,128),1)==lax.broadcasted_iota(jnp.int32,(256,128),0)//16).astype(BF)
        ax[0,:2*NP*16]=sum(mm(v,put) for v in three(tab[...]))
        ax[0,2*NP*16:base]=early_ref[...]
        small_copy(me,ax,arecv,a_ss,a_rs,0).start()
        done=1
        for t in range(now,max(eng.end(),now+LAG*B)):
            eng.slot(t,ready)
            if (t-now)%LAG==LAG-1 and done<=B:
                small_copy(me,ax,arecv,a_ss,a_rs,done-1).wait()
                ax[done]=ax[done-1]+arecv[done-1]
                if done<B: small_copy(me,ax,arecv,a_ss,a_rs,done).start()
                done+=1
        assert done==B+1
        small_ref[...]=ax[B]
        for d in across(): d.wait_send()

def back(q,kn,kf,vn,vf,do,dm,qmisc,e,et,bt,kseg,qf,qmf,feat,wqkv,gm,vec,early,grads,L,n,collective_id):
    T,D=q.shape; R=T//L; NP=D//128; per=R*NP
    def one(step): i=jnp.minimum(step,per-1); return i%R,i//R
    def cyc(step): i=jnp.minimum(step,2*per-1)%per; return i%R,i//R
    def two(step): i=jnp.clip(step-per,0,per-1); return i%R,i//R
    blk=lambda f: pl.BlockSpec((L,128),f)
    row=lambda w,f: pl.BlockSpec((L,w),lambda s:(f(s)[0],0))
    full=lambda a: pl.BlockSpec(a.shape,lambda s:(0,)*len(a.shape),pipeline_mode=pl.Buffered(1))
    any_=pl.BlockSpec(memory_space=pl.ANY)
    S=jax.ShapeDtypeStruct; sem=pltpu.SemaphoreType.DMA
    bits=n.bit_length()-1; per_side=D//WIDE; full_ff=grads[0].shape[1]; tiles=full_ff//SIDE; early_tiles=0
    count=per_side*(2*tiles+1)
    cuts=(count,count+per_side,count+2*per_side)
    chunks=[]; loads={}
    def chunk(to,entry,**more):
        ch=dict(to=to,entry=entry,kind=len(chunks),first=0,last=2*bits); ch.update(more); chunks.append(ch)
    late=[]
    for t in range(early_tiles,tiles):
        late+=[(0,0,t*per_side+k) for k in range(per_side)]+[(1,t,k) for k in range(per_side)]
    late+=[(2,0,k) for k in range(per_side)]
    for i,(a,r,k) in enumerate(late):
        loads[len(chunks)]=(a,r-early_tiles if a==1 else 0,k-early_tiles*per_side if a==0 else k)
        chunk((a,r,k),i,slot=i,land=i)
    place_of=[p for t in range(early_tiles) for p in [(0,0,t*per_side+k) for k in range(per_side)]+[(1,t,k) for k in range(per_side)]]
    for i,p in enumerate(place_of):
        chunk(p,2*i+1,first=bits,seg=i,kind=i)
    at=len(loads)
    half=per_side//2
    for g,group in enumerate(([k for k in range(per_side)],[per_side+k for k in range(half)]+[2*per_side+k for k in range(half)],
                  [per_side+k for k in range(half,per_side)]+[2*per_side+k for k in range(half,per_side)])):
        for i,k in enumerate(group):
            chunk((3,0,k),cuts[g]+i,slot=at,land=at,set=g); at+=1
    C=len(chunks)
    rows=sum(plan_of(bits,SIDE)[1:])
    asmall=(2*NP*16+early.shape[0]+4*D//128,128)
    outs=[S((T,D),BF),S(asmall,F32)]
    sums=[S((D,full_ff),BF),S((full_ff,D),BF),S((D,D),BF),S(wqkv.shape,BF)]
    return pl.pallas_call(functools.partial(back_kernel,n,NP,R,chunks,loads,cuts),grid=(2*per+1,),
        in_specs=[blk(one),blk(cyc),blk(one),blk(cyc),blk(one),blk(one),row(128,one),row(128,one),row(256,one),
                  pl.BlockSpec((256,L),lambda s:(0,one(s)[0])),pl.BlockSpec((2,256,256),lambda s:(one(s)[1],0,0)),row(128,one),blk(two),row(128,two),
                  full(feat),full(wqkv),full(gm),full(vec),full(early)]+[any_]*5,
        out_specs=[full(o) for o in outs]+[any_]*4,
        out_shape=outs+sums,
        scratch_shapes=[pltpu.VMEM((NP,T,128),BF),pltpu.VMEM((T,128),BF),pltpu.VMEM((T,3*D),BF),pltpu.VMEM((D,T),BF),pltpu.VMEM((2,256,256),F32),pltpu.VMEM((2*NP*16,256),F32),
            pltpu.VMEM((at,SIDE,WIDE),BF),pltpu.VMEM((at,rows,WIDE),BF),
            pltpu.VMEM((bits+1,)+asmall,F32),pltpu.VMEM((bits,)+asmall,F32),
            sem((C,)),sem((C,)),sem((C,2*bits)),sem((C,2*bits)),sem((NP+1,)),sem((NP+1,)),sem((bits,)),sem((bits,))],
        compiler_params=pltpu.CompilerParams(collective_id=collective_id,has_side_effects=True,vmem_limit_bytes=64<<20),
        name="att_bwd")(q,kn,kf,vn,vf,do,dm,qmisc,e,et,bt,kseg,qf,qmf,feat,wqkv,gm,vec,early,do,dm,*grads)


def front_kernel(NP, R, q_ref, kn_ref, vn_ref, e_ref, b_ref, qseg_ref, kseg_ref, k_any, v_any,
                 o_ref, kf_ref, vf_ref, qm_ref, kfs, vfs, onear, mnear, ks, kr, vs, vr):
    step = pl.program_id(0)
    per = NP * R
    inner = step % per
    pair = inner // R
    r = inner % R
    L = q_ref.shape[0]
    other = {"stream": 1 - lax.axis_index("stream")}
    lane = lax.broadcasted_iota(jnp.int32, (1, 128), 1)
    zero = jnp.zeros((), BF)
    one = jnp.ones((), BF)
    at = pl.ds(pl.multiple_of(r * L, L), L)

    def copies(p):
        cols = pl.ds(p * 128, 128)
        return (pltpu.make_async_remote_copy(k_any.at[:, cols], kfs.at[p], ks.at[p], kr.at[p], device_id=other, device_id_type=MESH),
                pltpu.make_async_remote_copy(v_any.at[:, cols], vfs.at[p], vs.at[p], vr.at[p], device_id=other, device_id_type=MESH))

    @pl.when(step == 0)
    def _():
        sem = pltpu.get_barrier_semaphore()
        pl.semaphore_signal(sem, inc=1, device_id=other, device_id_type=MESH)
        pl.semaphore_wait(sem, 1)
        for p in range(2):
            for d in copies(p):
                d.start()
        qm_ref[...] = qseg_ref[...]

    @pl.when(step == 2 * per // 3)
    def _():
        for d in copies(0):
            d.wait_send()
        for d in copies(2):
            d.start()

    for p in range(NP):
        @pl.when(step == per + p * R)
        def _():
            for d in copies(p):
                d.wait_recv()
            if p > 0:
                for d in copies(p):
                    d.wait_send()
                if p + 2 < NP:
                    for d in copies(p + 2):
                        d.start()

    def half_of(hh):
        return (lane < 64) if hh == 0 else (lane >= 64)

    @pl.when(step < per)
    def _():
        for hh in range(2):
            mh = half_of(hh)
            table = mm(e_ref[...], b_ref[hh]).astype(BF)
            kx = jnp.concatenate([kn_ref[...], table, kseg_ref[at, :]], axis=1)
            qx = jnp.concatenate([jnp.where(mh, q_ref[...], zero), e_ref[...], qseg_ref[at, :]], axis=1)
            s = mm(qx, kx, NT)
            m = jnp.max(s, axis=1, keepdims=True)
            p = jnp.exp(s - m).astype(BF)
            onear[inner, hh] = mm(p, jnp.where(mh, vn_ref[...], one))
            mnear[inner, hh] = jnp.broadcast_to(m, (L, 128))

    @pl.when(step >= per)
    def _():
        out = None
        kf = kfs[pair, at]
        vf = vfs[pair, at]
        kf_ref[...] = kf
        vf_ref[...] = vf
        for hh in range(2):
            mh = half_of(hh)
            h = 2 * pair + hh
            s = mm(jnp.where(mh, q_ref[...], zero), kf, NT)
            before = mnear[inner, hh]
            m = jnp.maximum(before, jnp.max(s, axis=1, keepdims=True))
            p = jnp.exp(s - m[:, :1]).astype(BF)
            o = mm(p, jnp.where(mh, vf, one)) + jnp.exp(before - m) * onear[inner, hh]
            l = pltpu.roll(o, 64, 1)
            on = o / l
            out = on if hh == 0 else jnp.where(mh, on, out)
            hi, mid_part, lo = three(-(m + jnp.log(jnp.where(mh, l, o))))
            cur = qm_ref[at, :]
            cur = jnp.where(lane == 3 * h, hi, cur)
            cur = jnp.where(lane == 3 * h + 1, mid_part, cur)
            qm_ref[at, :] = jnp.where(lane == 3 * h + 2, lo, cur)
        o_ref[...] = out.astype(BF)


def front(q, k, v, e, bt, qseg, kseg, L, collective_id):
    T, D = q.shape
    R, NP = T // L, D // 128
    per = R * NP

    def cyc(s):
        return (s % per) % R, (s % per) // R

    def one(s):
        i = jnp.minimum(s, per - 1)
        return i % R, i // R

    def two(s):
        i = jnp.maximum(s - per, 0)
        return i % R, i // R

    blk = lambda f: pl.BlockSpec((L, 128), f)
    full = lambda a: pl.BlockSpec(a.shape, lambda s: (0,) * len(a.shape), pipeline_mode=pl.Buffered(1))
    any_ = pl.BlockSpec(memory_space=pl.ANY)
    S = jax.ShapeDtypeStruct
    sem = pltpu.SemaphoreType.DMA((NP,))
    return pl.pallas_call(
        functools.partial(front_kernel, NP, R), grid=(2 * per,),
        in_specs=[blk(cyc), blk(one), blk(one), pl.BlockSpec((L, 256), lambda s: (one(s)[0], 0)),
                  pl.BlockSpec((2, 256, 256), lambda s: (one(s)[1], 0, 0)), full(qseg), full(kseg), any_, any_],
        out_specs=[blk(two)] * 3 + [full(qseg)],
        out_shape=[S((T, D), BF)] * 3 + [S((T, 128), BF)],
        scratch_shapes=[pltpu.VMEM((NP, T, 128), BF), pltpu.VMEM((NP, T, 128), BF),
                        pltpu.VMEM((per, 2, L, 128), F32), pltpu.VMEM((per, 2, L, 128), F32), sem, sem, sem, sem],
        compiler_params=pltpu.CompilerParams(collective_id=collective_id, has_side_effects=True, vmem_limit_bytes=60 << 20),
        name="att_fwd")(q, k, v, e, bt, qseg, kseg, k, v)


def widen_kernel(*refs):
    half = len(refs) // 2
    for i in range(half):
        refs[half + i][...] = refs[i][...].astype(F32)


def widen(arrays, parts=16):
    spec = lambda a: pl.BlockSpec((a.shape[0] // parts, a.shape[1]), lambda i: (i, 0))
    return pl.pallas_call(
        widen_kernel, grid=(parts,), in_specs=[spec(a) for a in arrays], out_specs=[spec(a) for a in arrays],
        out_shape=[jax.ShapeDtypeStruct(a.shape, F32) for a in arrays],
        compiler_params=pltpu.CompilerParams(vmem_limit_bytes=32 << 20), name="widen")(*arrays)


def gelu_both(u):
    a=jnp.abs(u)
    t=1.0/(1.0+a*(0.3275911*0.7071067811865476))
    ex=jnp.exp(u*u*-0.5)
    poly=((((1.061405429*t-1.453152027)*t+1.421413741)*t-0.284496736)*t+0.254829592)*t
    half=0.5*poly*ex
    cdf=jnp.where(u<0,half,1.0-half)
    return u*cdf, cdf+u*ex*0.3989422804014327

def norm_parts(v):
    center=v-jnp.mean(v,axis=1,keepdims=True)
    inv=lax.rsqrt(jnp.mean(center*center,axis=1,keepdims=True)+EPSILON)
    return center*inv,inv

def colsum(v): return jnp.sum(v,axis=0,keepdims=True)

def mid_kernel(RC, x_ref,cot_ref,att_ref,wo_ref,vec_ref,wu_ref,wd_ref,ub_ref,
               out_ref,gm_ref,do_ref,dm_ref,gwo_ref,gwu_ref,gwd_ref,gub_ref,small_ref,
               mid_s,nt_s,ntt_s,acc_s,gn_s):
    j=pl.program_id(0); T=x_ref.shape[0]; NTL=pl.num_programs(0)
    chunks=[slice(i*RC,(i+1)*RC) for i in range(T//RC)]
    @pl.when(j==0)
    def _():
        for sl in chunks:
            v=x_ref[sl,:].astype(F32)+mm(att_ref[sl,:],wo_ref[...])+vec_ref[0:1,:]
            mid_s[sl,:]=v
            n,_=norm_parts(v)
            nt=(n*vec_ref[1:2,:]+vec_ref[2:3,:]).astype(BF)
            nt_s[sl,:]=nt
            ntt_s[:,sl]=nt.T
            acc_s[sl,:]=v+vec_ref[3:4,:]
            gn_s[sl,:]=jnp.zeros_like(v)
    gub=0.0; gwd=0.0; gwu=0.0
    for sl in chunks:
        pre=mm(nt_s[sl,:],wu_ref[...])+ub_ref[...]
        act,slope=gelu_both(pre)
        act=act.astype(BF)
        gp=(mm(cot_ref[sl,:],wd_ref[...],NT)*slope).astype(BF)
        acc_s[sl,:]+=mm(act,wd_ref[...])
        gn_s[sl,:]+=mm(gp,wu_ref[...],NT)
        gub=gub+colsum(gp.astype(F32))
        gwd=gwd+mm(act,cot_ref[sl,:],TN)
        gwu=gwu+mm(ntt_s[:,sl],gp)
    gub_ref[...]=gub
    gwd_ref[...]=gwd.astype(BF); gwu_ref[...]=gwu.astype(BF)
    @pl.when(j==NTL-1)
    def _():
        g2=0.0; s2=0.0; ob=0.0; db=0.0; gwo=0.0
        row=lax.broadcasted_iota(jnp.int32,(x_ref.shape[1],128),0)//64
        col=lax.broadcasted_iota(jnp.int32,(x_ref.shape[1],128),1)
        pick=(row==col//3).astype(BF)
        lane=lax.broadcasted_iota(jnp.int32,(1,128),1)
        for sl in chunks:
            out_ref[sl,:]=acc_s[sl,:].astype(BF)
            n,inv=norm_parts(mid_s[sl,:])
            q=gn_s[sl,:]
            g2=g2+colsum(q*n); s2=s2+colsum(q)
            qg=q*vec_ref[1:2,:]
            cot=cot_ref[sl,:].astype(F32)
            db=db+colsum(cot)
            gm=cot+(qg-jnp.mean(qg,axis=1,keepdims=True)-n*jnp.mean(qg*n,axis=1,keepdims=True))*inv
            gm_ref[sl,:]=gm
            gb=gm.astype(BF)
            ob=ob+colsum(gb.astype(F32))
            do=mm(gb,wo_ref[...],NT).astype(BF)
            do_ref[sl,:]=do
            gwo=gwo+mm(att_ref[sl,:],gb,TN)
            prod=do.astype(F32)*att_ref[sl,:].astype(F32)
            hi=prod.astype(BF); lo=(prod-hi.astype(F32)).astype(BF)
            delta=-(mm(hi,pick)+mm(lo,pick))
            hi,md,lo=three(delta)
            dm_ref[sl,:]=jnp.where(lane>=36,jnp.zeros((),BF),jnp.where(lane%3==0,hi,jnp.where(lane%3==1,md,lo)))
        gwo_ref[...]=gwo.astype(BF)
        small_ref[0:1,:]=g2; small_ref[1:2,:]=s2; small_ref[2:3,:]=ob; small_ref[3:4,:]=db
        small_ref[4:8,:]=jnp.zeros((4,x_ref.shape[1]),F32)

def mid(x,cot,att,wo,vec,wu,wd,ub,FT=512,RC=256):
    T,D=x.shape; FF=wu.shape[1]
    full=lambda a: pl.BlockSpec(a.shape,lambda j:(0,0))
    S=jax.ShapeDtypeStruct
    fs=lambda *s: pl.BlockSpec(s,lambda j:(0,0))
    return pl.pallas_call(functools.partial(mid_kernel,RC),grid=(FF//FT,),
        in_specs=[full(x),full(cot),full(att),full(wo),full(vec),pl.BlockSpec((D,FT),lambda j:(0,j)),pl.BlockSpec((FT,D),lambda j:(j,0)),pl.BlockSpec((1,FT),lambda j:(0,j))],
        out_specs=[fs(T,D),fs(T,D),fs(T,D),fs(T,128),fs(D,D),pl.BlockSpec((D,FT),lambda j:(0,j)),pl.BlockSpec((FT,D),lambda j:(j,0)),pl.BlockSpec((1,FT),lambda j:(0,j)),fs(8,D)],
        out_shape=[S((T,D),BF),S((T,D),F32),S((T,D),BF),S((T,128),BF),S((D,D),BF),S((D,FF),BF),S((FF,D),BF),S((1,FF),F32),S((8,D),F32)],
        scratch_shapes=[pltpu.VMEM((T,D),F32),pltpu.VMEM((T,D),BF),pltpu.VMEM((D,T),BF),pltpu.VMEM((T,D),F32),pltpu.VMEM((T,D),F32)],
        compiler_params=pltpu.CompilerParams(vmem_limit_bytes=60<<20),name="feed_forward")(x,cot,att,wo,vec,wu,wd,ub)


def from_partner(block, axis, stride):
    count = lax.axis_size(axis)
    route = []
    for low in range(count):
        high = low | 1 << stride
        if high != low and high < count:
            route += [(low, high), (high, low)]
    return lax.ppermute(block, axis, route)


def layer_norm(values, norm_gain, norm_shift):
    center = values - jnp.mean(values, axis=-1, keepdims=True)
    spread = jnp.mean(center * center, axis=-1, keepdims=True)
    return center * lax.rsqrt(spread + EPSILON) * norm_gain + norm_shift


def norm_back(values, norm_gain, norm_shift, upstream):
    unused, pull_back = jax.vjp(layer_norm, values, norm_gain, norm_shift)
    return pull_back(upstream)


def gelu_exact(values):
    return jax.nn.gelu(values, approximate=False)


def gelu_back(values, upstream):
    unused, pull_back = jax.vjp(gelu_exact, values)
    return pull_back(upstream)[0]


def prepare(segment_ids, box_cells, table, is_vision):
    cell = (box_cells[:, 0] * 16 + box_cells[:, 1]).reshape(-1)
    cells = jnp.arange(256)
    e = (cell[:, None] == cells[None]).astype(BF)
    et = (cells[:, None] == cell[None]).astype(BF)
    lane = jnp.arange(128)
    same = segment_ids.reshape(-1)[:, None] == lane[None] - 64
    inside = (lane >= 64) & (lane < 68)
    qseg = same.astype(BF)
    kseg = jnp.where(inside[None] & ~same & jnp.logical_not(is_vision), MASKED, 0.0).astype(BF)
    return e, et, qseg, kseg


def code_onehot():
    c = jnp.arange(65536)
    step_x = jnp.minimum(jnp.abs(c // 4096 - (c // 16) % 16), GRID - 1)
    step_y = jnp.minimum(jnp.abs((c // 256) % 16 - c % 16), GRID - 1)
    return ((step_x * GRID + step_y)[None] == jnp.arange(GRID * GRID)[:, None]).astype(BF)


def on_device(features, cotangent, segment_ids, box_cells, ln_gain, ln_shift, w_qkv, attn_bias,
              distance_table, w_out, w_up, up_bias, w_down, down_bias):
    rows, length, width = features.shape[1:]
    tokens = rows * length
    heads = distance_table.shape[2]
    is_vision = lax.axis_index("stream") != 0
    norm_gains, norm_shifts = ln_gain[0], ln_shift[0]
    bias_rows = attn_bias[0]
    qkv_weight, out_weight, up_weight, down_weight = w_qkv[0], w_out[0], w_up[0], w_down[0]
    plain_in = features[0].reshape(tokens, width).astype(jnp.float32)
    normed = layer_norm(plain_in, norm_gains[0], norm_shifts[0]).astype(BF)
    combined = jnp.dot(normed, qkv_weight, preferred_element_type=jnp.float32)
    queries = (combined[:, :width] + bias_rows[0]).astype(BF) * BF(0.125)
    key_part = combined[:, width:2 * width].astype(BF)
    value_part = (combined[:, 2 * width:] + bias_rows[1]).astype(BF)
    e, et, qseg, kseg = prepare(segment_ids, box_cells[0], distance_table[0], is_vision)
    onehot = code_onehot()
    bt = jnp.dot(distance_table[0].T.astype(BF), onehot, preferred_element_type=jnp.float32).astype(BF).reshape(heads, 256, 256)
    attended, partner_k, partner_v, qmisc = front(queries, key_part, value_part, e, bt, qseg, kseg, length, 6)
    vec = jnp.concatenate([bias_rows[2:3], norm_gains[1:2], norm_shifts[1:2], down_bias, jnp.zeros((4, width), F32)])
    q_send, m_send = lax.optimization_barrier((queries, qmisc))
    partner_q = from_partner(q_send, "stream", 0)
    partner_m = from_partner(m_send, "stream", 0)
    group = lax.axis_size("batch")
    (output, grad_middle, grad_attended, dmisc, grad_out, grad_up, grad_down, grad_up_bias, small_mid) = mid(
        features[0].reshape(tokens, width), cotangent[0].reshape(tokens, width), attended, out_weight, vec,
        up_weight, down_weight, up_bias)
    output = output.reshape(1, rows, length, width)
    small_up = grad_up_bias.reshape(-1, 128)
    early = jnp.concatenate([small_mid.reshape(-1, 128), small_up])
    vec_one = jnp.concatenate([norm_gains[0:1], norm_shifts[0:1], jnp.zeros((6, width), F32)])
    input_grad, small_a, sum_up, sum_down, sum_out, sum_qkv = back(
        queries, key_part, partner_k, value_part, partner_v, grad_attended, dmisc, qmisc, e, et, bt, kseg,
        partner_q, partner_m, features[0].reshape(tokens, width), qkv_weight, grad_middle, vec_one, early,
        [grad_up, grad_down, grad_out], length, group, 4)
    input_grad = input_grad.reshape(1, rows, length, width)
    tab_rows = 16 * heads
    by_gap = small_a[:tab_rows, :16].reshape(heads, 2, GRID, 16)
    turn = jnp.arange(16)
    reach = jnp.minimum(jnp.stack([turn, 16 - turn]), GRID - 1)
    near = (reach[:, :, None] == jnp.arange(GRID)).astype(F32)
    dist = jnp.einsum("hpyd,pdx->xyh", by_gap, near, precision=lax.Precision.HIGHEST).reshape(1, GRID * GRID, heads)
    mid_sums = small_a[tab_rows:tab_rows + 8 * width // 128].reshape(8, width)
    tail = small_a.shape[0] - 4 * width // 128
    upb = small_a[tab_rows + 8 * width // 128:tail].reshape(1, -1)
    last = small_a[tail:].reshape(4, width)
    gain = jnp.stack([last[0], mid_sums[0]])[None]
    shift = jnp.stack([last[1], mid_sums[1]])[None]
    bias = jnp.stack([last[2], last[3], mid_sums[2]])[None]
    downb = mid_sums[3][None]
    sum_qkv, sum_out, sum_up, sum_down = widen([sum_qkv, sum_out, sum_up, sum_down])
    f32 = lambda a: a[None]
    return (output, input_grad, gain, shift, f32(sum_qkv), bias, dist, f32(sum_out), f32(sum_up), upb, f32(sum_down), downb)


def solution(mesh):
    in_specs = (
        P("stream", "batch", None, None),
        P("stream", "batch", None, None),
        P("batch", None),
        P("stream", "batch", None, None),
        P("stream", None, None),
        P("stream", None, None),
        P("stream", None, None),
        P("stream", None, None),
        P("stream", None, None),
        P("stream", None, None),
        P("stream", None, None),
        P("stream", None),
        P("stream", None, None),
        P("stream", None),
    )
    out_specs = (
        P("stream", "batch", None, None),
        P("stream", "batch", None, None),
        P("stream", None, None),
        P("stream", None, None),
        P("stream", None, None),
        P("stream", None, None),
        P("stream", None, None),
        P("stream", None, None),
        P("stream", None, None),
        P("stream", None),
        P("stream", None, None),
        P("stream", None),
    )
    return jax.shard_map(
        on_device, mesh=mesh, in_specs=in_specs, out_specs=out_specs, check_vma=False
    )
```

```python
import functools
import jax
import jax.numpy as jnp
from jax import lax
from jax.experimental import pallas as pl
from jax.experimental.pallas import tpu as pltpu
from jax.sharding import PartitionSpec as P

GRID = 8
EPSILON = 1e-05
MASKED = -1000000000.0

NT=(((1,),(1,)),((),())); NN=(((1,),(0,)),((),())); TN=(((0,),(0,)),((),()))
def mm(a,b,dn=NN): return lax.dot_general(a,b,dn,preferred_element_type=jnp.float32)
BF=jnp.bfloat16

def three(x):
    hi=x.astype(BF); r=x-hi.astype(jnp.float32); mid=r.astype(BF); lo=(r-mid.astype(jnp.float32)).astype(BF)
    return hi,mid,lo


F32=jnp.float32


MESH=pl.DeviceIdType.MESH
SIDE=768
WIDE=384
LAG=3
STEP=48

def bit_order(n, c):
    plain=list(range(n.bit_length()-1))
    other=[0]+plain[2:]+[1] if len(plain)>2 else plain
    return other if c%6==3 else plain

def plan_of(bits, rows):
    sizes=[rows]
    for _ in range(bits):
        m=sizes[-1]
        sizes.append(m//2 if m%32==0 else m)
    return sizes

def place(me, b):
    bit=(me//(1<<b))%2
    return bit, me+(1-2*bit)*(1<<b)

def rows_at(off, size):
    return pl.ds(off if isinstance(off,int) else pl.multiple_of(off,16),size)

class Engine:
    def __init__(self, n, me, chunks, x, recv, segs, sums, ss, rs, os):
        self.me,self.chunks=me,chunks
        self.x,self.recv,self.segs,self.sums=x,recv,segs,sums
        self.ss,self.rs,self.os=ss,rs,os
        self.bits=n.bit_length()-1
        self.sizes=plan_of(self.bits,SIDE)
        self.offs=[sum(self.sizes[1:s+1]) for s in range(self.bits+1)]
        self.n=n

    def seg(self,c,upto):
        order=bit_order(self.n,self.chunks[c]["kind"]); off=0
        for s in range(upto):
            if self.sizes[s+1]!=self.sizes[s]:
                off=off+place(self.me,order[s])[0]*self.sizes[s+1]
        return off,self.sizes[upto]

    def out(self,c,off,m):
        a,i,k=self.chunks[c]["to"]
        return self.sums[a].at[rows_at(i*SIDE+off,m),pl.ds(k*WIDE,WIDE)]

    def final(self,c):
        off,m=self.seg(c,self.bits)
        ch=self.chunks[c]
        if ch["first"]: return self.segs.at[ch["seg"]]
        return self.x.at[ch["slot"],rows_at(off,m)]

    def copy(self,c,stage):
        B,sizes,ch=self.bits,self.sizes,self.chunks[c]
        order=bit_order(self.n,ch["kind"])
        if stage<B:
            bit,partner=place(self.me,order[stage])
            off,m=self.seg(c,stage)
            if sizes[stage+1]!=m:
                src=self.x.at[ch["slot"],rows_at(off+(1-bit)*(m//2),m//2)]
            else:
                src=self.x.at[ch["slot"],rows_at(off,m)]
            dst=self.recv.at[ch["land"],pl.ds(self.offs[stage],sizes[stage+1])]
        else:
            s=2*B-1-stage
            if sizes[s+1]==sizes[s]:
                return None
            partner=place(self.me,order[s])[1]
            off,m=self.seg(c,s+1)
            dst=self.out(c,off,m)
            src=self.final(c) if stage==B else dst
        return pltpu.make_async_remote_copy(src,dst,self.ss.at[c,stage],self.rs.at[c,stage],
            device_id={"batch":partner},device_id_type=MESH)

    def keep(self,c):
        off,m=self.seg(c,self.bits)
        return pltpu.make_async_copy(self.final(c),self.out(c,off,m),self.os.at[c])

    def start(self,c,stage):
        if stage==self.bits:
            self.keep(c).start()
        d=self.copy(c,stage)
        if d is not None: d.start()

    def finish(self,c,stage):
        d=self.copy(c,stage)
        if d is not None: d.wait()
        if stage==self.bits:
            self.keep(c).wait()
        if stage<self.bits:
            off,m=self.seg(c,stage+1)
            ro=self.offs[stage]; x,recv=self.x,self.recv
            h,land=self.chunks[c]["slot"],self.chunks[c]["land"]
            def body(i,_):
                at=rows_at(off+i*STEP,STEP)
                more=recv[land,pl.ds(pl.multiple_of(ro+i*STEP,16),STEP)]
                x[h,at]=(x[h,at].astype(F32)+more.astype(F32)).astype(BF)
                return 0
            lax.fori_loop(0,m//STEP,body,0)
            if stage==self.bits-1 and self.chunks[c]["last"]==self.bits:
                self.segs[self.chunks[c]["seg"]]=x[h,rows_at(off,m)]

    def times(self,c):
        ch=self.chunks[c]
        order=bit_order(self.n,ch["kind"]); order=order+order[::-1]
        at=[ch["entry"]]
        for s in range(ch["first"],ch["last"]): at.append(at[-1]+(1 if order[s]==0 else LAG))
        return at

    def slot(self,t,load):
        todo=[]
        for c in range(len(self.chunks)):
            at=self.times(c)
            if t in at:
                todo.append((self.chunks[c]["entry"],c,self.chunks[c]["first"]+at.index(t)))
        for _,c,s in sorted(todo):
            ch=self.chunks[c]
            if s==ch["first"]: load(c)
            else: self.finish(c,s-1)
            if s<ch["last"]: self.start(c,s)

    def end(self):
        return 1+max(self.times(c)[-1] for c in range(len(self.chunks)))

def small_copy(me,x,recv,ss,rs,s):
    return pltpu.make_async_remote_copy(x.at[s],recv.at[s],ss.at[s],rs.at[s],device_id={"batch":place(me,s)[1]},device_id_type=MESH)

def back_kernel(n, NP, R, chunks, loads, cuts,
               q_ref,kn_ref,kf_ref,vn_ref,vf_ref,do_ref,dm_ref,qm_ref,e_ref,et_ref,b_ref,kseg_ref,qf_ref,qmf_ref,
               feat_ref,wqkv_ref,gm_ref,vec_ref,early_ref,
               do_any,dm_any,gu_any,gd_any,go_any,
               ig_ref,small_ref,su_any,sd_any,so_any,sq_any,
               dof,dmf,gmix,nt_s,g_s,tab,x,recv,ax,arecv,in_sem,out_sem,ss,rs,xs_sem,xr_sem,a_ss,a_rs):
    step=pl.program_id(0)
    per=NP*R
    second=(step>=per)&(step<2*per)
    inner=step%per; pair=inner//R; r=inner%R
    L=q_ref.shape[0]; T=feat_ref.shape[0]; D=feat_ref.shape[1]
    me=lax.axis_index("batch"); other={"stream":1-lax.axis_index("stream")}
    lane=lax.broadcasted_iota(jnp.int32,(1,128),1)
    zero=jnp.zeros((),BF)
    RC=256
    grads=(gu_any,gd_any,go_any)
    eng=Engine(n,me,chunks,x,recv,None,(su_any,sd_any,so_any,sq_any),ss,rs,out_sem)
    B=eng.bits
    q_set,mid_set,end_set=[[c for c in range(len(chunks)) if chunks[c].get("set")==i] for i in range(3)]
    def load(c):
        a,i,k=loads[c]
        return pltpu.make_async_copy(grads[a].at[pl.ds(i*SIDE,SIDE),pl.ds(k*WIDE,WIDE)],x.at[chunks[c]["slot"]],in_sem.at[c])
    def ready(c):
        if c in loads: load(c).wait()
    def across():
        res=[pltpu.make_async_remote_copy(dm_any,dmf,xs_sem.at[NP],xr_sem.at[NP],device_id=other,device_id_type=MESH)]
        for p in range(NP):
            res.append(pltpu.make_async_remote_copy(do_any.at[:,pl.ds(p*128,128)],dof.at[p],xs_sem.at[p],xr_sem.at[p],device_id=other,device_id_type=MESH))
        return res

    @pl.when(step==0)
    def _():
        sem=pltpu.get_barrier_semaphore()
        for b in range(B):
            pl.semaphore_signal(sem,inc=1,device_id={"batch":place(me,b)[1]},device_id_type=MESH)
        pl.semaphore_signal(sem,inc=1,device_id=other,device_id_type=MESH)
        for c in loads: load(c).start()
        pl.semaphore_wait(sem,B+1)
        for d in across(): d.start()
    def spread(lo,hi,parts): return [lo+(hi-lo)*i//parts for i in range(parts)]
    edges=spread(0,cuts[0],2*per)+spread(cuts[0],cuts[1],per)+spread(cuts[1],cuts[2],per)+[cuts[2]]
    def form(c):
        a,i,k=chunks[c]["to"]
        x[chunks[c]["slot"]]=mm(nt_s[i*SIDE:(i+1)*SIDE,:],gmix[:,k*WIDE:(k+1)*WIDE]).astype(BF)
    def tick(half):
        for k in range(2*per):
            i=k*2+half
            group=q_set if i==2*per else mid_set if i==3*per else []
            if edges[i]==edges[i+1] and not group: continue
            @pl.when(step==k)
            def _():
                if i==2*per:
                    for j in range(T//RC):
                        sl=slice(j*RC,(j+1)*RC)
                        nrm,_=norm_parts(feat_ref[sl,:].astype(F32))
                        nt_s[:,sl]=(nrm*vec_ref[0:1,:]+vec_ref[1:2,:]).astype(BF).T
                for c in group: form(c)
                for t in range(edges[i],edges[i+1]): eng.slot(t,ready)
    def half_of(hh):
        return (lane<64) if hh==0 else (lane>=64)
    def ones_of(h):
        return jnp.where((lane>=3*h)&(lane<3*h+3),1.0,0.0)
    add=lambda a,b: b if a is None else a+b
    def cols(part): return pl.ds(pl.multiple_of(part*D+pair*128,128),128)
    at=pl.ds(pl.multiple_of(r*L,L),L)

    tick(0)
    @pl.when(step<per)
    def _():
        dkn=None; dvn=None; dq=None
        for hh in range(2):
            mh=half_of(hh); h=2*pair+hh
            ones_h=ones_of(h); ones_b=jnp.broadcast_to(ones_h.astype(BF),(L,128))
            qm=jnp.where(mh,q_ref[...],zero); dom=jnp.where(mh,do_ref[...],zero)
            C_h=mm(e_ref[...],b_ref[hh]).astype(BF)
            qx=jnp.concatenate([qm,e_ref[...],qm_ref[...]],axis=1)
            dox=jnp.concatenate([dom,dm_ref[...]],axis=1)
            kseg=(kseg_ref[...].astype(F32)+ones_h).astype(BF)
            p=jnp.exp(mm(jnp.concatenate([kn_ref[...],C_h,kseg],axis=1),qx,NT))
            ds=(p*mm(jnp.concatenate([vn_ref[...],ones_b],axis=1),dox,NT)).astype(BF)
            dvn=add(dvn,mm(p.astype(BF),dom))
            t=mm(ds,jnp.concatenate([qm,e_ref[...]],axis=1))
            dkn=add(dkn,t[:,:128])
            g=mm(et_ref[...],t[:,128:].astype(BF))
            dq=add(dq,mm(ds,jnp.where(mh,kn_ref[...],zero),TN))
            p=jnp.exp(mm(jnp.concatenate([kf_ref[...],ones_b],axis=1),jnp.concatenate([qm,qm_ref[...]],axis=1),NT))
            ds=(p*mm(jnp.concatenate([vf_ref[...],ones_b],axis=1),dox,NT)).astype(BF)
            dq=add(dq,mm(ds,jnp.where(mh,kf_ref[...],zero),TN))
            @pl.when(r==0)
            def _(): g_s[hh]=g
            @pl.when(r!=0)
            def _(): g_s[hh]+=g
        gmix[at,cols(0)]=(dq*0.125).astype(BF)
        gmix[at,cols(1)]=dkn.astype(BF); gmix[at,cols(2)]=dvn.astype(BF)
    @pl.when((step<per)&(r==R-1))
    def _():
        turn=lax.broadcasted_iota(jnp.int32,(1,256),1)
        gap=jnp.minimum(jnp.abs(lax.broadcasted_iota(jnp.int32,(16,256),0)-turn%16),7)
        for hh in range(2):
            ahead=None; behind=None
            for i in range(16):
                blk=g_s[hh,16*i:16*i+16,:]
                if i: blk=pltpu.roll(blk,256-16*i,1)
                ahead=add(ahead,jnp.where(turn<256-16*i,blk,0.0))
                behind=add(behind,jnp.where(turn<256-16*i,0.0,blk))
            sums=[colsum(jnp.where(gap==k,v,0.0)) for v in (ahead,behind) for k in range(8)]
            tab[pl.ds(pl.multiple_of((2*pair+hh)*16,16),16),:]=jnp.concatenate(sums,axis=0)
    tick(1)
    @pl.when(step==per)
    def _():
        for d in across(): d.wait_recv()
    @pl.when(second)
    def _():
        dk=gmix[at,cols(1)].astype(F32); dv=gmix[at,cols(2)].astype(F32)
        for hh in range(2):
            mh=half_of(hh); h=2*pair+hh
            ones_b=jnp.broadcast_to(ones_of(h).astype(BF),(L,128))
            qm=jnp.where(mh,qf_ref[...],zero); dom=jnp.where(mh,dof[pair,at],zero)
            p=jnp.exp(mm(jnp.concatenate([kn_ref[...],ones_b],axis=1),jnp.concatenate([qm,qmf_ref[...]],axis=1),NT))
            ds=(p*mm(jnp.concatenate([vn_ref[...],ones_b],axis=1),jnp.concatenate([dom,dmf[at]],axis=1),NT)).astype(BF)
            dv=dv+mm(p.astype(BF),dom)
            dk=dk+mm(ds,qm)
        gmix[at,cols(1)]=dk.astype(BF); gmix[at,cols(2)]=dv.astype(BF)
    @pl.when(step==2*per)
    def _():
        now=cuts[2]
        for c in end_set:
            form(c); eng.slot(now,ready); now+=1
        gain=0.0; shift=0.0; qb=0.0; vb=0.0
        for i in range(T//RC):
            sl=slice(i*RC,(i+1)*RC)
            g=mm(gmix[sl,:],wqkv_ref[...],NT)
            nrm,inv=norm_parts(feat_ref[sl,:].astype(F32))
            gain=gain+colsum(g*nrm); shift=shift+colsum(g)
            qb=qb+colsum(gmix[sl,:D].astype(F32)); vb=vb+colsum(gmix[sl,2*D:].astype(F32))
            qg=g*vec_ref[0:1,:]
            ig_ref[sl,:]=(gm_ref[sl,:]+(qg-jnp.mean(qg,axis=1,keepdims=True)-nrm*jnp.mean(qg*nrm,axis=1,keepdims=True))*inv).astype(BF)
            eng.slot(now,ready); now+=1
        w=D//128; base=2*NP*16+early_ref.shape[0]
        for i,v in enumerate((gain,shift,qb,vb)):
            for k in range(w): ax[0,base+i*w+k:base+i*w+k+1,:]=v[:,k*128:(k+1)*128]
        put=(lax.broadcasted_iota(jnp.int32,(256,128),1)==lax.broadcasted_iota(jnp.int32,(256,128),0)//16).astype(BF)
        ax[0,:2*NP*16]=sum(mm(v,put) for v in three(tab[...]))
        ax[0,2*NP*16:base]=early_ref[...]
        small_copy(me,ax,arecv,a_ss,a_rs,0).start()
        done=1
        for t in range(now,max(eng.end(),now+LAG*B)):
            eng.slot(t,ready)
            if (t-now)%LAG==LAG-1 and done<=B:
                small_copy(me,ax,arecv,a_ss,a_rs,done-1).wait()
                ax[done]=ax[done-1]+arecv[done-1]
                if done<B: small_copy(me,ax,arecv,a_ss,a_rs,done).start()
                done+=1
        assert done==B+1
        small_ref[...]=ax[B]
        for d in across(): d.wait_send()

def back(q,kn,kf,vn,vf,do,dm,qmisc,e,et,bt,kseg,qf,qmf,feat,wqkv,gm,vec,early,grads,L,n,collective_id):
    T,D=q.shape; R=T//L; NP=D//128; per=R*NP
    def one(step): i=jnp.minimum(step,per-1); return i%R,i//R
    def cyc(step): i=jnp.minimum(step,2*per-1)%per; return i%R,i//R
    def two(step): i=jnp.clip(step-per,0,per-1); return i%R,i//R
    blk=lambda f: pl.BlockSpec((L,128),f)
    row=lambda w,f: pl.BlockSpec((L,w),lambda s:(f(s)[0],0))
    full=lambda a: pl.BlockSpec(a.shape,lambda s:(0,)*len(a.shape),pipeline_mode=pl.Buffered(1))
    any_=pl.BlockSpec(memory_space=pl.ANY)
    S=jax.ShapeDtypeStruct; sem=pltpu.SemaphoreType.DMA
    bits=n.bit_length()-1; per_side=D//WIDE; full_ff=grads[0].shape[1]; tiles=full_ff//SIDE; early_tiles=0
    count=per_side*(2*tiles+1)
    cuts=(count,count+per_side,count+2*per_side)
    chunks=[]; loads={}
    def chunk(to,entry,**more):
        ch=dict(to=to,entry=entry,kind=len(chunks),first=0,last=2*bits); ch.update(more); chunks.append(ch)
    late=[]
    for t in range(early_tiles,tiles):
        late+=[(0,0,t*per_side+k) for k in range(per_side)]+[(1,t,k) for k in range(per_side)]
    late+=[(2,0,k) for k in range(per_side)]
    for i,(a,r,k) in enumerate(late):
        loads[len(chunks)]=(a,r-early_tiles if a==1 else 0,k-early_tiles*per_side if a==0 else k)
        chunk((a,r,k),i,slot=i,land=i)
    place_of=[p for t in range(early_tiles) for p in [(0,0,t*per_side+k) for k in range(per_side)]+[(1,t,k) for k in range(per_side)]]
    for i,p in enumerate(place_of):
        chunk(p,2*i+1,first=bits,seg=i,kind=i)
    at=len(loads)
    half=per_side//2
    for g,group in enumerate(([k for k in range(per_side)],[per_side+k for k in range(half)]+[2*per_side+k for k in range(half)],
                  [per_side+k for k in range(half,per_side)]+[2*per_side+k for k in range(half,per_side)])):
        for i,k in enumerate(group):
            chunk((3,0,k),cuts[g]+i,slot=at,land=at,set=g); at+=1
    C=len(chunks)
    rows=sum(plan_of(bits,SIDE)[1:])
    asmall=(2*NP*16+early.shape[0]+4*D//128,128)
    outs=[S((T,D),BF),S(asmall,F32)]
    sums=[S((D,full_ff),BF),S((full_ff,D),BF),S((D,D),BF),S(wqkv.shape,BF)]
    return pl.pallas_call(functools.partial(back_kernel,n,NP,R,chunks,loads,cuts),grid=(2*per+1,),
        in_specs=[blk(one),blk(cyc),blk(one),blk(cyc),blk(one),blk(one),row(128,one),row(128,one),row(256,one),
                  pl.BlockSpec((256,L),lambda s:(0,one(s)[0])),pl.BlockSpec((2,256,256),lambda s:(one(s)[1],0,0)),row(128,one),blk(two),row(128,two),
                  full(feat),full(wqkv),full(gm),full(vec),full(early)]+[any_]*5,
        out_specs=[full(o) for o in outs]+[any_]*4,
        out_shape=outs+sums,
        scratch_shapes=[pltpu.VMEM((NP,T,128),BF),pltpu.VMEM((T,128),BF),pltpu.VMEM((T,3*D),BF),pltpu.VMEM((D,T),BF),pltpu.VMEM((2,256,256),F32),pltpu.VMEM((2*NP*16,256),F32),
            pltpu.VMEM((at,SIDE,WIDE),BF),pltpu.VMEM((at,rows,WIDE),BF),
            pltpu.VMEM((bits+1,)+asmall,F32),pltpu.VMEM((bits,)+asmall,F32),
            sem((C,)),sem((C,)),sem((C,2*bits)),sem((C,2*bits)),sem((NP+1,)),sem((NP+1,)),sem((bits,)),sem((bits,))],
        compiler_params=pltpu.CompilerParams(collective_id=collective_id,has_side_effects=True,vmem_limit_bytes=64<<20),
        name="att_bwd")(q,kn,kf,vn,vf,do,dm,qmisc,e,et,bt,kseg,qf,qmf,feat,wqkv,gm,vec,early,do,dm,*grads)


def front_kernel(NP, R, feat_ref, w_ref, vec_ref, e_ref, b_ref, qseg_ref, kseg_ref,
                 o_ref, kf_ref, vf_ref, qm_ref, q_s, k_s, v_s, nrm_s, kfs, vfs, onear, mnear, ks, kr, vs, vr):
    step = pl.program_id(0)
    per = NP * R
    inner = step % per
    pair = inner // R
    r = inner % R
    L = e_ref.shape[0]
    T, D = feat_ref.shape
    GROUP = 256
    mine = pl.ds(pl.multiple_of(pair * 128, 128), 128)
    other = {"stream": 1 - lax.axis_index("stream")}
    lane = lax.broadcasted_iota(jnp.int32, (1, 128), 1)
    zero = jnp.zeros((), BF)
    one = jnp.ones((), BF)
    at = pl.ds(pl.multiple_of(r * L, L), L)

    def copies(p):
        cols = pl.ds(p * 128, 128)
        return (pltpu.make_async_remote_copy(k_s.at[:, cols], kfs.at[p], ks.at[p], kr.at[p], device_id=other, device_id_type=MESH),
                pltpu.make_async_remote_copy(v_s.at[:, cols], vfs.at[p], vs.at[p], vr.at[p], device_id=other, device_id_type=MESH))

    @pl.when(step == 0)
    def _():
        sem = pltpu.get_barrier_semaphore()
        pl.semaphore_signal(sem, inc=1, device_id=other, device_id_type=MESH)
        for i in range(T // GROUP):
            sl = slice(i * GROUP, (i + 1) * GROUP)
            nrm, _ = norm_parts(feat_ref[sl, :].astype(F32))
            nrm_s[sl, :] = (nrm * vec_ref[0:1, :] + vec_ref[1:2, :]).astype(BF)
        for g in range(D // GROUP):
            sl = slice(g * GROUP, (g + 1) * GROUP)
            k_s[:, sl] = mm(nrm_s[...], w_ref[:, D + g * GROUP:D + (g + 1) * GROUP]).astype(BF)
            v_s[:, sl] = (mm(nrm_s[...], w_ref[:, 2 * D + g * GROUP:2 * D + (g + 1) * GROUP]) + vec_ref[3:4, sl]).astype(BF)
            if g == 0:
                pl.semaphore_wait(sem, 1)
                for p in range(2):
                    for d in copies(p):
                        d.start()
        for g in range(D // GROUP):
            sl = slice(g * GROUP, (g + 1) * GROUP)
            q_s[:, sl] = (mm(nrm_s[...], w_ref[:, sl]) + vec_ref[2:3, sl]).astype(BF) * BF(0.125)
        qm_ref[...] = qseg_ref[...]

    @pl.when(step == 2 * per // 3)
    def _():
        for d in copies(0):
            d.wait_send()
        for d in copies(2):
            d.start()

    for p in range(NP):
        @pl.when(step == per + p * R)
        def _():
            for d in copies(p):
                d.wait_recv()
            if p > 0:
                for d in copies(p):
                    d.wait_send()
                if p + 2 < NP:
                    for d in copies(p + 2):
                        d.start()

    def half_of(hh):
        return (lane < 64) if hh == 0 else (lane >= 64)

    @pl.when(step < per)
    def _():
        for hh in range(2):
            mh = half_of(hh)
            table = mm(e_ref[...], b_ref[hh]).astype(BF)
            kx = jnp.concatenate([k_s[at, mine], table, kseg_ref[at, :]], axis=1)
            qx = jnp.concatenate([jnp.where(mh, q_s[at, mine], zero), e_ref[...], qseg_ref[at, :]], axis=1)
            s = mm(qx, kx, NT)
            m = jnp.max(s, axis=1, keepdims=True)
            p = jnp.exp(s - m).astype(BF)
            onear[inner, hh] = mm(p, jnp.where(mh, v_s[at, mine], one))
            mnear[inner, hh] = jnp.broadcast_to(m, (L, 128))

    @pl.when(step >= per)
    def _():
        out = None
        kf = kfs[pair, at]
        vf = vfs[pair, at]
        kf_ref[...] = kf
        vf_ref[...] = vf
        for hh in range(2):
            mh = half_of(hh)
            h = 2 * pair + hh
            s = mm(jnp.where(mh, q_s[at, mine], zero), kf, NT)
            before = mnear[inner, hh]
            m = jnp.maximum(before, jnp.max(s, axis=1, keepdims=True))
            p = jnp.exp(s - m[:, :1]).astype(BF)
            o = mm(p, jnp.where(mh, vf, one)) + jnp.exp(before - m) * onear[inner, hh]
            l = pltpu.roll(o, 64, 1)
            on = o / l
            out = on if hh == 0 else jnp.where(mh, on, out)
            hi, mid_part, lo = three(-(m + jnp.log(jnp.where(mh, l, o))))
            cur = qm_ref[at, :]
            cur = jnp.where(lane == 3 * h, hi, cur)
            cur = jnp.where(lane == 3 * h + 1, mid_part, cur)
            qm_ref[at, :] = jnp.where(lane == 3 * h + 2, lo, cur)
        o_ref[...] = out.astype(BF)


def front(feat, w, vec, e, bt, qseg, kseg, L, collective_id):
    T, D = feat.shape
    R, NP = T // L, D // 128
    per = R * NP

    def one(s):
        i = jnp.minimum(s, per - 1)
        return i % R, i // R

    def two(s):
        i = jnp.maximum(s - per, 0)
        return i % R, i // R

    blk = lambda f: pl.BlockSpec((L, 128), f)
    full = lambda a: pl.BlockSpec(a.shape, lambda s: (0,) * len(a.shape), pipeline_mode=pl.Buffered(1))
    any_ = pl.BlockSpec(memory_space=pl.ANY)
    S = jax.ShapeDtypeStruct
    sem = pltpu.SemaphoreType.DMA((NP,))
    return pl.pallas_call(
        functools.partial(front_kernel, NP, R), grid=(2 * per,),
        in_specs=[full(feat), full(w), full(vec), pl.BlockSpec((L, 256), lambda s: (one(s)[0], 0)),
                  pl.BlockSpec((2, 256, 256), lambda s: (one(s)[1], 0, 0)), full(qseg), full(kseg)],
        out_specs=[blk(two)] * 3 + [full(qseg)] + [full(feat)] * 3,
        out_shape=[S((T, D), BF)] * 3 + [S((T, 128), BF)] + [S((T, D), BF)] * 3,
        scratch_shapes=[pltpu.VMEM((T, D), BF), pltpu.VMEM((NP, T, 128), BF), pltpu.VMEM((NP, T, 128), BF),
                        pltpu.VMEM((per, 2, L, 128), F32), pltpu.VMEM((per, 2, L, 128), F32), sem, sem, sem, sem],
        compiler_params=pltpu.CompilerParams(collective_id=collective_id, has_side_effects=True, vmem_limit_bytes=60 << 20),
        name="att_fwd")(feat, w, vec, e, bt, qseg, kseg)


def widen_kernel(*refs):
    half = len(refs) // 2
    for i in range(half):
        refs[half + i][...] = refs[i][...].astype(F32)


def widen(arrays, parts=16):
    spec = lambda a: pl.BlockSpec((a.shape[0] // parts, a.shape[1]), lambda i: (i, 0))
    return pl.pallas_call(
        widen_kernel, grid=(parts,), in_specs=[spec(a) for a in arrays], out_specs=[spec(a) for a in arrays],
        out_shape=[jax.ShapeDtypeStruct(a.shape, F32) for a in arrays],
        compiler_params=pltpu.CompilerParams(vmem_limit_bytes=62 << 20), name="widen")(*arrays)


def gelu_both(u):
    a=jnp.abs(u)
    t=1.0/(1.0+a*(0.3275911*0.7071067811865476))
    ex=jnp.exp(u*u*-0.5)
    poly=((((1.061405429*t-1.453152027)*t+1.421413741)*t-0.284496736)*t+0.254829592)*t
    half=0.5*poly*ex
    cdf=jnp.where(u<0,half,1.0-half)
    return u*cdf, cdf+u*ex*0.3989422804014327

def norm_parts(v):
    center=v-jnp.mean(v,axis=1,keepdims=True)
    inv=lax.rsqrt(jnp.mean(center*center,axis=1,keepdims=True)+EPSILON)
    return center*inv,inv

def colsum(v): return jnp.sum(v,axis=0,keepdims=True)

def mid_kernel(RC, x_ref,cot_ref,att_ref,wo_ref,vec_ref,wu_ref,wd_ref,ub_ref,
               out_ref,gm_ref,do_ref,dm_ref,gwo_ref,gwu_ref,gwd_ref,gub_ref,small_ref,
               mid_s,nt_s,ntt_s,acc_s,gn_s):
    j=pl.program_id(0); T=x_ref.shape[0]; NTL=pl.num_programs(0)
    chunks=[slice(i*RC,(i+1)*RC) for i in range(T//RC)]
    @pl.when(j==0)
    def _():
        for sl in chunks:
            v=x_ref[sl,:].astype(F32)+mm(att_ref[sl,:],wo_ref[...])+vec_ref[0:1,:]
            mid_s[sl,:]=v
            n,_=norm_parts(v)
            nt=(n*vec_ref[1:2,:]+vec_ref[2:3,:]).astype(BF)
            nt_s[sl,:]=nt
            ntt_s[:,sl]=nt.T
            acc_s[sl,:]=v+vec_ref[3:4,:]
            gn_s[sl,:]=jnp.zeros_like(v)
    gub=0.0; gwd=0.0; gwu=0.0
    for sl in chunks:
        pre=mm(nt_s[sl,:],wu_ref[...])+ub_ref[...]
        act,slope=gelu_both(pre)
        act=act.astype(BF)
        gp=(mm(cot_ref[sl,:],wd_ref[...],NT)*slope).astype(BF)
        acc_s[sl,:]+=mm(act,wd_ref[...])
        gn_s[sl,:]+=mm(gp,wu_ref[...],NT)
        gub=gub+colsum(gp.astype(F32))
        gwd=gwd+mm(act,cot_ref[sl,:],TN)
        gwu=gwu+mm(ntt_s[:,sl],gp)
    gub_ref[...]=gub
    gwd_ref[...]=gwd.astype(BF); gwu_ref[...]=gwu.astype(BF)
    @pl.when(j==NTL-1)
    def _():
        g2=0.0; s2=0.0; ob=0.0; db=0.0; gwo=0.0
        row=lax.broadcasted_iota(jnp.int32,(x_ref.shape[1],128),0)//64
        col=lax.broadcasted_iota(jnp.int32,(x_ref.shape[1],128),1)
        pick=(row==col//3).astype(BF)
        lane=lax.broadcasted_iota(jnp.int32,(1,128),1)
        for sl in chunks:
            out_ref[sl,:]=acc_s[sl,:].astype(BF)
            n,inv=norm_parts(mid_s[sl,:])
            q=gn_s[sl,:]
            g2=g2+colsum(q*n); s2=s2+colsum(q)
            qg=q*vec_ref[1:2,:]
            cot=cot_ref[sl,:].astype(F32)
            db=db+colsum(cot)
            gm=cot+(qg-jnp.mean(qg,axis=1,keepdims=True)-n*jnp.mean(qg*n,axis=1,keepdims=True))*inv
            gm_ref[sl,:]=gm
            gb=gm.astype(BF)
            ob=ob+colsum(gb.astype(F32))
            do=mm(gb,wo_ref[...],NT).astype(BF)
            do_ref[sl,:]=do
            gwo=gwo+mm(att_ref[sl,:],gb,TN)
            prod=do.astype(F32)*att_ref[sl,:].astype(F32)
            hi=prod.astype(BF); lo=(prod-hi.astype(F32)).astype(BF)
            delta=-(mm(hi,pick)+mm(lo,pick))
            hi,md,lo=three(delta)
            dm_ref[sl,:]=jnp.where(lane>=36,jnp.zeros((),BF),jnp.where(lane%3==0,hi,jnp.where(lane%3==1,md,lo)))
        gwo_ref[...]=gwo.astype(BF)
        small_ref[0:1,:]=g2; small_ref[1:2,:]=s2; small_ref[2:3,:]=ob; small_ref[3:4,:]=db
        small_ref[4:8,:]=jnp.zeros((4,x_ref.shape[1]),F32)

def mid(x,cot,att,wo,vec,wu,wd,ub,FT=512,RC=256):
    T,D=x.shape; FF=wu.shape[1]
    full=lambda a: pl.BlockSpec(a.shape,lambda j:(0,0))
    S=jax.ShapeDtypeStruct
    fs=lambda *s: pl.BlockSpec(s,lambda j:(0,0))
    return pl.pallas_call(functools.partial(mid_kernel,RC),grid=(FF//FT,),
        in_specs=[full(x),full(cot),full(att),full(wo),full(vec),pl.BlockSpec((D,FT),lambda j:(0,j)),pl.BlockSpec((FT,D),lambda j:(j,0)),pl.BlockSpec((1,FT),lambda j:(0,j))],
        out_specs=[fs(T,D),fs(T,D),fs(T,D),fs(T,128),fs(D,D),pl.BlockSpec((D,FT),lambda j:(0,j)),pl.BlockSpec((FT,D),lambda j:(j,0)),pl.BlockSpec((1,FT),lambda j:(0,j)),fs(8,D)],
        out_shape=[S((T,D),BF),S((T,D),F32),S((T,D),BF),S((T,128),BF),S((D,D),BF),S((D,FF),BF),S((FF,D),BF),S((1,FF),F32),S((8,D),F32)],
        scratch_shapes=[pltpu.VMEM((T,D),F32),pltpu.VMEM((T,D),BF),pltpu.VMEM((D,T),BF),pltpu.VMEM((T,D),F32),pltpu.VMEM((T,D),F32)],
        compiler_params=pltpu.CompilerParams(vmem_limit_bytes=60<<20),name="feed_forward")(x,cot,att,wo,vec,wu,wd,ub)


def from_partner(block, axis, stride):
    count = lax.axis_size(axis)
    route = []
    for low in range(count):
        high = low | 1 << stride
        if high != low and high < count:
            route += [(low, high), (high, low)]
    return lax.ppermute(block, axis, route)


def layer_norm(values, norm_gain, norm_shift):
    center = values - jnp.mean(values, axis=-1, keepdims=True)
    spread = jnp.mean(center * center, axis=-1, keepdims=True)
    return center * lax.rsqrt(spread + EPSILON) * norm_gain + norm_shift


def norm_back(values, norm_gain, norm_shift, upstream):
    unused, pull_back = jax.vjp(layer_norm, values, norm_gain, norm_shift)
    return pull_back(upstream)


def gelu_exact(values):
    return jax.nn.gelu(values, approximate=False)


def gelu_back(values, upstream):
    unused, pull_back = jax.vjp(gelu_exact, values)
    return pull_back(upstream)[0]


def prepare(segment_ids, box_cells, table, is_vision):
    cell = (box_cells[:, 0] * 16 + box_cells[:, 1]).reshape(-1)
    cells = jnp.arange(256)
    e = (cell[:, None] == cells[None]).astype(BF)
    et = (cells[:, None] == cell[None]).astype(BF)
    lane = jnp.arange(128)
    same = segment_ids.reshape(-1)[:, None] == lane[None] - 64
    inside = (lane >= 64) & (lane < 68)
    qseg = same.astype(BF)
    kseg = jnp.where(inside[None] & ~same & jnp.logical_not(is_vision), MASKED, 0.0).astype(BF)
    return e, et, qseg, kseg


def code_onehot():
    c = jnp.arange(65536)
    step_x = jnp.minimum(jnp.abs(c // 4096 - (c // 16) % 16), GRID - 1)
    step_y = jnp.minimum(jnp.abs((c // 256) % 16 - c % 16), GRID - 1)
    return ((step_x * GRID + step_y)[None] == jnp.arange(GRID * GRID)[:, None]).astype(BF)


def on_device(features, cotangent, segment_ids, box_cells, ln_gain, ln_shift, w_qkv, attn_bias,
              distance_table, w_out, w_up, up_bias, w_down, down_bias):
    rows, length, width = features.shape[1:]
    tokens = rows * length
    heads = distance_table.shape[2]
    is_vision = lax.axis_index("stream") != 0
    norm_gains, norm_shifts = ln_gain[0], ln_shift[0]
    bias_rows = attn_bias[0]
    qkv_weight, out_weight, up_weight, down_weight = w_qkv[0], w_out[0], w_up[0], w_down[0]
    e, et, qseg, kseg = prepare(segment_ids, box_cells[0], distance_table[0], is_vision)
    onehot = code_onehot()
    bt = jnp.dot(distance_table[0].T.astype(BF), onehot, preferred_element_type=jnp.float32).astype(BF).reshape(heads, 256, 256)
    feat = features[0].reshape(tokens, width)
    vec_one = jnp.concatenate([norm_gains[0:1], norm_shifts[0:1], bias_rows[0:2], jnp.zeros((4, width), F32)])
    attended, partner_k, partner_v, qmisc, queries, key_part, value_part = front(
        feat, qkv_weight, vec_one, e, bt, qseg, kseg, length, 6)
    vec = jnp.concatenate([bias_rows[2:3], norm_gains[1:2], norm_shifts[1:2], down_bias, jnp.zeros((4, width), F32)])
    q_send, m_send = lax.optimization_barrier((queries, qmisc))
    partner_q = from_partner(q_send, "stream", 0)
    partner_m = from_partner(m_send, "stream", 0)
    group = lax.axis_size("batch")
    (output, grad_middle, grad_attended, dmisc, grad_out, grad_up, grad_down, grad_up_bias, small_mid) = mid(
        features[0].reshape(tokens, width), cotangent[0].reshape(tokens, width), attended, out_weight, vec,
        up_weight, down_weight, up_bias)
    output = output.reshape(1, rows, length, width)
    small_up = grad_up_bias.reshape(-1, 128)
    early = jnp.concatenate([small_mid.reshape(-1, 128), small_up])
    input_grad, small_a, sum_up, sum_down, sum_out, sum_qkv = back(
        queries, key_part, partner_k, value_part, partner_v, grad_attended, dmisc, qmisc, e, et, bt, kseg,
        partner_q, partner_m, features[0].reshape(tokens, width), qkv_weight, grad_middle, vec_one, early,
        [grad_up, grad_down, grad_out], length, group, 4)
    input_grad = input_grad.reshape(1, rows, length, width)
    tab_rows = 16 * heads
    by_gap = small_a[:tab_rows, :16].reshape(heads, 2, GRID, 16)
    turn = jnp.arange(16)
    reach = jnp.minimum(jnp.stack([turn, 16 - turn]), GRID - 1)
    near = (reach[:, :, None] == jnp.arange(GRID)).astype(F32)
    dist = jnp.einsum("hpyd,pdx->xyh", by_gap, near, precision=lax.Precision.HIGHEST).reshape(1, GRID * GRID, heads)
    mid_sums = small_a[tab_rows:tab_rows + 8 * width // 128].reshape(8, width)
    tail = small_a.shape[0] - 4 * width // 128
    upb = small_a[tab_rows + 8 * width // 128:tail].reshape(1, -1)
    last = small_a[tail:].reshape(4, width)
    gain = jnp.stack([last[0], mid_sums[0]])[None]
    shift = jnp.stack([last[1], mid_sums[1]])[None]
    bias = jnp.stack([last[2], last[3], mid_sums[2]])[None]
    downb = mid_sums[3][None]
    sum_qkv, sum_out, sum_up, sum_down = widen([sum_qkv, sum_out, sum_up, sum_down])
    f32 = lambda a: a[None]
    return (output, input_grad, gain, shift, f32(sum_qkv), bias, dist, f32(sum_out), f32(sum_up), upb, f32(sum_down), downb)


def solution(mesh):
    in_specs = (
        P("stream", "batch", None, None),
        P("stream", "batch", None, None),
        P("batch", None),
        P("stream", "batch", None, None),
        P("stream", None, None),
        P("stream", None, None),
        P("stream", None, None),
        P("stream", None, None),
        P("stream", None, None),
        P("stream", None, None),
        P("stream", None, None),
        P("stream", None),
        P("stream", None, None),
        P("stream", None),
    )
    out_specs = (
        P("stream", "batch", None, None),
        P("stream", "batch", None, None),
        P("stream", None, None),
        P("stream", None, None),
        P("stream", None, None),
        P("stream", None, None),
        P("stream", None, None),
        P("stream", None, None),
        P("stream", None, None),
        P("stream", None),
        P("stream", None, None),
        P("stream", None),
    )
    return jax.shard_map(
        on_device, mesh=mesh, in_specs=in_specs, out_specs=out_specs, check_vma=False
    )
```
